32 devices in a mesh: section: 2 (over x), dp: 16 (over z, y, core).
Axes of the slice: x: 2, y: 2, z: 4, core: 2. Of those that a mesh axis runs over, the one named last changes fastest.
Arguments:
- block_input: bfloat16 [2, 1024, 1024], P(None, 'dp'), may hold values from -6 to 6
- crop_ids: int32 [2, 1024], P(None, 'dp'), may hold values from -1 to 1, as said below
- out_grad: bfloat16 [2, 1024, 1024], P(None, 'dp'), may hold values from -6 to 6
- norm1_gain: bfloat16 [2, 1024], P('section', 'dp'), may hold values from 0.099609375 to 1.8984375
- norm1_shift: bfloat16 [2, 1024], P('section', 'dp'), may hold values from -3 to 3
- w_qkv: bfloat16 [2, 1024, 3072], P('section', 'dp'), may hold values from -0.1875 to 0.1875
- w_out: bfloat16 [2, 1024, 1024], P('section', 'dp'), may hold values from -0.75 to 0.75
- b_out: bfloat16 [2, 1024], P('section', 'dp'), may hold values from -3 to 3
- norm2_gain: bfloat16 [2, 1024], P('section', 'dp'), may hold values from 0.099609375 to 1.8984375
- norm2_shift: bfloat16 [2, 1024], P('section', 'dp'), may hold values from -3 to 3
- w_up: bfloat16 [2, 1024, 4096], P('section', 'dp'), may hold values from -0.1875 to 0.1875
- b_up: bfloat16 [2, 4096], P('section', 'dp'), may hold values from -3 to 3
- w_down: bfloat16 [2, 4096, 1024], P('section', 'dp'), may hold values from -0.09375 to 0.09375
- b_down: bfloat16 [2, 1024], P('section', 'dp'), may hold values from -3 to 3
Outputs:
- layer_outputs: bfloat16 [2, 2, 1024, 1024], P('section', None, 'dp')
- input_grads: bfloat16 [2, 2, 1024, 1024], P('section', None, 'dp')
- grad_norm1_gain: float32 [2, 1024], P('section', 'dp')
- grad_norm1_shift: float32 [2, 1024], P('section', 'dp')
- grad_w_qkv: float32 [2, 1024, 3072], P('section', 'dp')
- grad_w_out: float32 [2, 1024, 1024], P('section', 'dp')
- grad_b_out: float32 [2, 1024], P('section', 'dp')
- grad_norm2_gain: float32 [2, 1024], P('section', 'dp')
- grad_norm2_shift: float32 [2, 1024], P('section', 'dp')
- grad_w_up: float32 [2, 1024, 4096], P('section', 'dp')
- grad_b_up: float32 [2, 4096], P('section', 'dp')
- grad_w_down: float32 [2, 4096, 1024], P('section', 'dp')
- grad_b_down: float32 [2, 1024], P('section', 'dp')
The draws below stay inside these ranges and needn't reach their ends.
Inputs may be any that keep to these rules, and one draw needn't show every extreme that they name: `crop_ids`: within each block of 64 rows of one micro-batch and one device, crops are numbered from 0 in row order: first one or more global crops of 50 rows (never more than fit in 64 rows), then local crops of 10 rows that fill the remaining room but for at most two crops' worth, then padding rows marked -1; blocks are independent.
All inputs are finite; a program needn't handle non-finite values.
Results may differ from the reference program's by a relative error of at most 0.015.
Values may be sent and summed in bfloat16 or wider, within the bound.
A program may use at most 256 MiB of HBM per device.

```python
import jax
import jax.numpy as jnp
from jax import lax

D = 1024
HEAD = 64
FF = 4096
R = 64
M = 2
TOKENS = 1024


def draw_crop_ids(key, part):
    key = jax.random.fold_in(key, 7)
    key_wide, key_slack = jax.random.split(key)
    block_count = M * (TOKENS // R)
    most_wide = max(R // 50, 1)
    wide_count = jax.random.randint(key_wide, (block_count,), 1, most_wide + 1)
    wide_count = wide_count.at[0].set(1)
    room_left = (R - 50 * wide_count) // 10
    slack_count = jax.random.randint(key_slack, (block_count,), 0, 3)
    slack_count = jnp.minimum(slack_count, room_left).at[0].set(0)
    local_count = room_left - slack_count
    row_index = jnp.arange(R)[None, :]
    wide_rows = 50 * wide_count[:, None]
    local_rows = wide_rows + 10 * local_count[:, None]
    crop_number = jnp.where(row_index < wide_rows, row_index // 50, jnp.where(row_index < local_rows, wide_count[:, None] + (row_index - wide_rows) // 10, -1))
    return crop_number.reshape(M, TOKENS).astype(jnp.int32)


def with_spikes(entries, rng, source, target, blocks, factor):
    def block_of(position):
        return (jnp.arange(entries.shape[position]) // (entries.shape[position] // blocks)).reshape((-1,) + (1,) * (entries.ndim - 1 - position))

    near = jax.random.permutation(rng, blocks)[block_of(target)]
    other_side = (block_of(target) + blocks // 2) % blocks
    return jnp.where((block_of(source) == near) | (block_of(source) == other_side), factor * entries, entries)


def shard_levels(stream_key, shape, pieces, smallest, high):
    def one(axis_at, blocks):
        draws = jax.random.uniform(jax.random.fold_in(jax.random.fold_in(stream_key, 6), axis_at), (blocks,), jnp.float32, smallest / len(pieces), high / len(pieces))
        return jnp.repeat(jnp.exp(draws), shape[axis_at] // blocks).reshape((-1,) + (1,) * (len(shape) - axis_at - 1))

    level = one(*pieces[0])
    for cut in pieces[1:]:
        level = level * one(*cut)
    return level


def bell_draw(own_key, extent, scale, reach, pieces=(), held_as=jnp.bfloat16):
    array = scale * jax.random.normal(own_key, extent, jnp.float32)
    if pieces:
        array = array * shard_levels(own_key, extent, pieces, -0.22, 0.18)
    return jnp.clip(array, -reach, reach).astype(held_as)


def heavy_noise(own_key, dims, deviation, bound, cuts, heavy, dtype=jnp.bfloat16):
    drawn = deviation * jax.random.normal(own_key, dims, jnp.float32)
    if cuts:
        drawn = drawn * shard_levels(own_key, dims, cuts, -0.22, 0.18)
    return jnp.clip(with_spikes(drawn, jax.random.fold_in(own_key, 3), *heavy), -bound, bound).astype(dtype)


def setup_inputs(seed: int = 0) -> dict:
    streams_of = jax.random.split(jax.random.key(seed), 15)
    block_input = heavy_noise(streams_of[0], (M, TOKENS, D), 1.0, 6.0, ((1, 16),), (1, 2, 16, 2.0))
    crop_ids = draw_crop_ids(jax.random.fold_in(streams_of[14], 71), 0)
    out_grad = bell_draw(streams_of[2], (M, TOKENS, D), 1.0, 6.0, ((1, 16),))
    norm1_gain = jnp.clip(1.0 + 0.18 * jax.random.normal(streams_of[3], (2, D), jnp.float32), 0.099609375, 1.8984375).astype(jnp.bfloat16)
    norm1_shift = bell_draw(streams_of[4], (2, D), 0.5, 3.0, ((0, 2), (1, 16)))
    w_qkv = bell_draw(streams_of[5], (2, D, 3 * D), D ** -0.5, 0.1875, ((0, 2), (1, 16)))
    w_out = bell_draw(streams_of[6], (2, D, D), (D // 16) ** -0.5, 0.75, ((0, 2), (1, 16)))
    b_out = bell_draw(streams_of[7], (2, D), 0.5, 3.0, ((0, 2), (1, 16)))
    norm2_gain = jnp.clip(1.0 + 0.18 * jax.random.normal(streams_of[8], (2, D), jnp.float32), 0.099609375, 1.8984375).astype(jnp.bfloat16)
    norm2_shift = bell_draw(streams_of[9], (2, D), 0.5, 3.0, ((0, 2), (1, 16)))
    w_up = bell_draw(streams_of[10], (2, D, FF), D ** -0.5, 0.1875, ((0, 2), (1, 16)))
    b_up = bell_draw(streams_of[11], (2, FF), 0.5, 3.0, ((0, 2), (1, 16)))
    w_down = bell_draw(streams_of[12], (2, FF, D), FF ** -0.5, 0.09375, ((0, 2), (1, 16)))
    b_down = bell_draw(streams_of[13], (2, D), 0.5, 3.0, ((0, 2), (1, 16)))
    return {"block_input": block_input, "crop_ids": crop_ids, "out_grad": out_grad, "norm1_gain": norm1_gain, "norm1_shift": norm1_shift, "w_qkv": w_qkv, "w_out": w_out, "b_out": b_out, "norm2_gain": norm2_gain, "norm2_shift": norm2_shift, "w_up": w_up, "b_up": b_up, "w_down": w_down, "b_down": b_down}


@jax.custom_vjp
def low(v):
    return lax.optimization_barrier(v.astype(jnp.bfloat16)).astype(jnp.float32)

@jax.custom_vjp
def low_back(v):
    return v

def low_keep(v):
    return (low(v), None)

def low_pass(kept, grad):
    return (grad,)

def back_keep(v):
    return (v, None)

def back_low(kept, grad):
    return (low(grad),)
low.defvjp(low_keep, low_pass)
low_back.defvjp(back_keep, back_low)

def norm_rows(values, gain, shift):
    centred = values - lax.optimization_barrier(jnp.mean(values, axis=-1, keepdims=True))
    spread = lax.optimization_barrier(jnp.mean(centred * centred, axis=-1, keepdims=True))
    return centred * lax.rsqrt(spread + 1e-06) * gain + shift

def matmul(left, right):
    return jnp.dot(left, right, precision=lax.Precision.HIGHEST)

def attend_block(qkv_rows, crop_rows):
    model_width = qkv_rows.shape[1] // 3
    head_count = model_width // HEAD
    queries = qkv_rows[:, :model_width].reshape(-1, head_count, HEAD)
    key_rows = qkv_rows[:, model_width:2 * model_width].reshape(-1, head_count, HEAD)
    value_rows = qkv_rows[:, 2 * model_width:].reshape(-1, head_count, HEAD)
    scores = jnp.einsum('qhd,khd->hqk', queries, key_rows, precision=lax.Precision.HIGHEST)
    scores = low_back(scores * HEAD ** (-0.5))
    same_crop = crop_rows[:, None] == crop_rows[None, :]
    scores = jnp.where(same_crop[None], scores, -1e+30)
    row_peak = lax.optimization_barrier(jnp.max(scores, axis=-1, keepdims=True))
    raised = jnp.exp(scores - row_peak)
    softmax_out = low(raised / lax.optimization_barrier(jnp.sum(raised, axis=-1, keepdims=True)))
    mixed_heads = jnp.einsum('hqk,khd->qhd', softmax_out, value_rows, precision=lax.Precision.HIGHEST)
    return mixed_heads.reshape(-1, model_width)

def layer(stream, crop_blocks, params):
    gain_one, shift_one, w_qkv, w_out, b_out, gain_two, shift_two, w_up, b_up, w_down, b_down = params
    block_count = crop_blocks.shape[0]
    block_rows = crop_blocks.shape[1]
    normed = low(norm_rows(stream, gain_one, shift_one))
    qkv_rows = low_back(low(matmul(normed, w_qkv)))
    attend = jax.checkpoint(attend_block)
    mixed_heads = lax.map(lambda item: attend(item[0], item[1]), (qkv_rows.reshape(block_count, block_rows, -1), crop_blocks))
    mixed_heads = low_back(low(mixed_heads.reshape(stream.shape[0], -1)))
    hidden = stream + low_back(matmul(mixed_heads, w_out) + b_out)
    squeezed = low(norm_rows(hidden, gain_two, shift_two))
    up_rows = low_back(matmul(squeezed, w_up) + b_up)
    active = low(jax.nn.gelu(up_rows, approximate=False))
    return hidden + low_back(matmul(active, w_down) + b_down)

def reference(block_input, crop_ids, out_grad, norm1_gain, norm1_shift, w_qkv, w_out, b_out, norm2_gain, norm2_shift, w_up, b_up, w_down, b_down):
    params = tuple((item.astype(jnp.float32) for item in (norm1_gain, norm1_shift, w_qkv, w_out, b_out, norm2_gain, norm2_shift, w_up, b_up, w_down, b_down)))
    group_rows = 32 * R
    group_count = M * TOKENS // group_rows
    model_width = block_input.shape[2]
    stream_groups = block_input.reshape(group_count, group_rows, model_width).astype(jnp.float32)
    crop_groups = crop_ids.reshape(group_count, 32, R).astype(jnp.int32)
    grad_groups = out_grad.reshape(group_count, group_rows, model_width).astype(jnp.float32)
    zero_grads = tuple((jnp.zeros_like(item) for item in params))

    def one_group(totals, item):
        stream, crop_blocks, cotangent = item

        def forward(entry, weights, extra):
            first_out = layer(entry, crop_blocks, tuple((part[0] for part in weights)))
            sent_rows = low_back(low(first_out))
            second_out = layer(sent_rows + extra, crop_blocks, tuple((part[1] for part in weights)))
            return (sent_rows, second_out)
        (sent_rows, second_out), pull = jax.vjp(forward, stream, params, jnp.zeros_like(stream))
        grad_entry, grad_params, grad_extra = pull((jnp.zeros_like(sent_rows), cotangent))
        totals = tuple((left + right for left, right in zip(totals, grad_params)))
        return (totals, (sent_rows.astype(jnp.bfloat16), second_out.astype(jnp.bfloat16), grad_entry.astype(jnp.bfloat16), grad_extra.astype(jnp.bfloat16)))
    totals, (first_rows, second_rows, first_grads, second_grads) = lax.scan(one_group, zero_grads, (stream_groups, crop_groups, grad_groups))
    shape_out = (M, TOKENS, model_width)
    layer_outputs = jnp.stack([first_rows.reshape(shape_out), second_rows.reshape(shape_out)])
    input_grads = jnp.stack([first_grads.reshape(shape_out), second_grads.reshape(shape_out)])
    return (layer_outputs, input_grads, totals[0], totals[1], totals[2], totals[3], totals[4], totals[5], totals[6], totals[7], totals[8], totals[9], totals[10])
```

```python
import jax
import jax.numpy as jnp
from jax import lax
from jax.experimental import pallas as pl
from jax.experimental.pallas import tpu as pltpu
from jax.sharding import PartitionSpec as P

HEAD = 64


def passed_along(x, axis, by):
    devices = lax.axis_size(axis)
    pairs = [(i, i + by) for i in range(devices) if 0 <= i + by < devices]
    return lax.ppermute(x, axis, pairs)


def norm_rows(values, gain, shift):
    centred = values - jnp.mean(values, axis=-1, keepdims=True)
    spread = jnp.mean(centred * centred, axis=-1, keepdims=True)
    return centred * lax.rsqrt(spread + 1e-06) * gain + shift


def gelu_exact(values):
    return jax.nn.gelu(values, approximate=False)


def inner_rows(left, right):
    return lax.dot_general(
        left, right, (((0,), (0,)), ((), ())), preferred_element_type=jnp.float32
    )


def times_transpose(left, right):
    return lax.dot_general(
        left, right, (((1,), (1,)), ((), ())), preferred_element_type=jnp.float32
    )


def split_heads(qkv_rows):
    model_width = qkv_rows.shape[1] // 3
    head_count = model_width // HEAD
    queries = qkv_rows[:, :model_width].reshape(-1, head_count, HEAD)
    key_rows = qkv_rows[:, model_width : 2 * model_width].reshape(-1, head_count, HEAD)
    value_rows = qkv_rows[:, 2 * model_width :].reshape(-1, head_count, HEAD)
    return (queries, key_rows, value_rows)


def head_scores(qkv_rows, crop_rows):
    queries, key_rows, value_rows = split_heads(qkv_rows)
    scores = jnp.einsum("qhd,khd->hqk", queries, key_rows, preferred_element_type=jnp.float32)
    scores = scores * HEAD ** (-0.5)
    same_crop = crop_rows[:, None] == crop_rows[None, :]
    return jnp.where(same_crop[None], scores, -1e30)


def forward_layer(layer_in, crop_rows, weights):
    gain_one, shift_one, w_qkv, w_out, b_out, gain_two, shift_two, w_up, b_up, w_down, b_down = (
        weights
    )
    row_count = layer_in.shape[0]
    normed = norm_rows(
        layer_in, gain_one.astype(jnp.float32), shift_one.astype(jnp.float32)
    ).astype(jnp.bfloat16)
    qkv_rows = jnp.dot(normed, w_qkv, preferred_element_type=jnp.float32).astype(jnp.bfloat16)
    scores = head_scores(qkv_rows, crop_rows)
    row_peak = jnp.max(scores, axis=-1, keepdims=True)
    log_total = row_peak + jnp.log(jnp.sum(jnp.exp(scores - row_peak), axis=-1, keepdims=True))
    softmax_low = jnp.exp(scores - log_total).astype(jnp.bfloat16)
    queries, key_rows, value_rows = split_heads(qkv_rows)
    mixed_heads = jnp.einsum(
        "hqk,khd->qhd", softmax_low, value_rows, preferred_element_type=jnp.float32
    )
    mixed_heads = mixed_heads.reshape(row_count, -1).astype(jnp.bfloat16)
    hidden = (
        layer_in
        + jnp.dot(mixed_heads, w_out, preferred_element_type=jnp.float32)
        + b_out.astype(jnp.float32)
    )
    squeezed = norm_rows(
        hidden, gain_two.astype(jnp.float32), shift_two.astype(jnp.float32)
    ).astype(jnp.bfloat16)
    up_rows = jnp.dot(squeezed, w_up, preferred_element_type=jnp.float32) + b_up.astype(jnp.float32)
    active = gelu_exact(up_rows).astype(jnp.bfloat16)
    result = (
        hidden
        + jnp.dot(active, w_down, preferred_element_type=jnp.float32)
        + b_down.astype(jnp.float32)
    )
    return (
        layer_in,
        normed,
        qkv_rows,
        log_total,
        mixed_heads,
        hidden,
        squeezed,
        up_rows,
        active,
        result,
    )


def backward_feed(grad_result, saved, weights):
    gain_one, shift_one, w_qkv, w_out, b_out, gain_two, shift_two, w_up, b_up, w_down, b_down = (
        weights
    )
    (
        layer_in,
        normed,
        qkv_rows,
        log_total,
        mixed_heads,
        hidden,
        squeezed,
        up_rows,
        active,
        result,
    ) = saved
    grad_branch = grad_result.astype(jnp.bfloat16)
    grad_w_down = inner_rows(active, grad_branch)
    grad_b_down = jnp.sum(grad_branch.astype(jnp.float32), axis=0)
    grad_active = times_transpose(grad_branch, w_down)
    gelu_value, gelu_pull = jax.vjp(gelu_exact, up_rows)
    grad_up = gelu_pull(grad_active)[0].astype(jnp.bfloat16)
    grad_w_up = inner_rows(squeezed, grad_up)
    grad_b_up = jnp.sum(grad_up.astype(jnp.float32), axis=0)
    grad_squeezed = times_transpose(grad_up, w_up)
    norm_value, norm_pull = jax.vjp(
        norm_rows, hidden, gain_two.astype(jnp.float32), shift_two.astype(jnp.float32)
    )
    grad_hid, grad_gain_two, grad_shift_two = norm_pull(grad_squeezed)
    grad_hidden = grad_result + grad_hid
    return (
        grad_hidden,
        (grad_gain_two, grad_shift_two, grad_w_up, grad_b_up, grad_w_down, grad_b_down),
    )


def backward_attend(grad_hidden, saved, crop_rows, weights):
    gain_one, shift_one, w_qkv, w_out, b_out, gain_two, shift_two, w_up, b_up, w_down, b_down = (
        weights
    )
    (
        layer_in,
        normed,
        qkv_rows,
        log_total,
        mixed_heads,
        hidden,
        squeezed,
        up_rows,
        active,
        result,
    ) = saved
    row_count = layer_in.shape[0]
    grad_attn = grad_hidden.astype(jnp.bfloat16)
    grad_w_out = inner_rows(mixed_heads, grad_attn)
    grad_b_out = jnp.sum(grad_attn.astype(jnp.float32), axis=0)
    grad_mixed = times_transpose(grad_attn, w_out).astype(jnp.bfloat16)
    queries, key_rows, value_rows = split_heads(qkv_rows)
    grad_mixed = grad_mixed.reshape(queries.shape)
    softmax_out = jnp.exp(head_scores(qkv_rows, crop_rows) - log_total)
    grad_soft = jnp.einsum(
        "qhd,khd->hqk", grad_mixed, value_rows, preferred_element_type=jnp.float32
    )
    grad_values = jnp.einsum(
        "hqk,qhd->khd",
        softmax_out.astype(jnp.bfloat16),
        grad_mixed,
        preferred_element_type=jnp.float32,
    )
    row_centre = jnp.sum(grad_soft * softmax_out, axis=-1, keepdims=True)
    grad_scores = (softmax_out * (grad_soft - row_centre)).astype(jnp.bfloat16)
    grad_queries = jnp.einsum(
        "hqk,khd->qhd", grad_scores, key_rows, preferred_element_type=jnp.float32
    ) * HEAD ** (-0.5)
    grad_keys = jnp.einsum(
        "hqk,qhd->khd", grad_scores, queries, preferred_element_type=jnp.float32
    ) * HEAD ** (-0.5)
    grad_qkv = jnp.concatenate(
        [
            grad_queries.reshape(row_count, -1),
            grad_keys.reshape(row_count, -1),
            grad_values.reshape(row_count, -1),
        ],
        axis=1,
    ).astype(jnp.bfloat16)
    grad_w_qkv = inner_rows(normed, grad_qkv)
    grad_normed = times_transpose(grad_qkv, w_qkv)
    first_value, first_pull = jax.vjp(
        norm_rows, layer_in, gain_one.astype(jnp.float32), shift_one.astype(jnp.float32)
    )
    grad_in, grad_gain_one, grad_shift_one = first_pull(grad_normed)
    return (
        grad_hidden + grad_in,
        (grad_gain_one, grad_shift_one, grad_w_qkv, grad_w_out, grad_b_out),
    )


def local(
    block_input,
    crop_ids,
    out_grad,
    norm1_gain,
    norm1_shift,
    w_qkv,
    w_out,
    b_out,
    norm2_gain,
    norm2_shift,
    w_up,
    b_up,
    w_down,
    b_down,
):
    is_first = lax.axis_index("section") == 0
    shards = (
        norm1_gain,
        norm1_shift,
        w_qkv,
        w_out,
        b_out,
        norm2_gain,
        norm2_shift,
        w_up,
        b_up,
        w_down,
        b_down,
    )
    gathered = (
        lax.all_gather(shards[0], "dp", axis=1, tiled=True),
        lax.all_gather(shards[1], "dp", axis=1, tiled=True),
        lax.all_gather(shards[2], "dp", axis=1, tiled=True),
        lax.all_gather(shards[3], "dp", axis=1, tiled=True),
        lax.all_gather(shards[4], "dp", axis=1, tiled=True),
        lax.all_gather(shards[5], "dp", axis=1, tiled=True),
        lax.all_gather(shards[6], "dp", axis=1, tiled=True),
        lax.all_gather(shards[7], "dp", axis=1, tiled=True),
        lax.all_gather(shards[8], "dp", axis=1, tiled=True),
        lax.all_gather(shards[9], "dp", axis=1, tiled=True),
        lax.all_gather(shards[10], "dp", axis=1, tiled=True),
    )
    weights = tuple((item[0] for item in gathered))
    micro_count = block_input.shape[0]

    def pick(upper, lower):
        return jax.tree.map(
            lambda later, earlier: jnp.where(is_first, earlier, later), upper, lower
        )

    incoming = jnp.zeros(block_input.shape[1:], jnp.bfloat16)
    records = []
    kept_saved = []
    forward_rows = []
    for step_index in range(micro_count + 1):
        own_rows = block_input[min(step_index, micro_count - 1)]
        source = jnp.where(is_first, own_rows, incoming)
        crop_rows = jnp.where(
            is_first, crop_ids[min(step_index, micro_count - 1)], crop_ids[max(step_index - 1, 0)]
        )
        saved = forward_layer(source.astype(jnp.float32), crop_rows, weights)
        sent_rows = saved[-1].astype(jnp.bfloat16)
        forward_rows.append(sent_rows)
        records.append((source, crop_rows))
        kept_saved.append(saved)
        if step_index < micro_count:
            incoming = passed_along(sent_rows, "section", 1)
    layer_outputs = jnp.where(
        is_first, jnp.stack(forward_rows[:micro_count]), jnp.stack(forward_rows[1:])
    )
    totals = jax.tree.map(lambda item: jnp.zeros(item.shape, jnp.float32), weights)
    back_in = jnp.zeros(block_input.shape[1:], jnp.bfloat16)
    backward_rows = []
    for step_index in range(micro_count + 1):
        late_tick = min(step_index + 1, micro_count)
        early_tick = max(step_index - 1, 0)
        source, crop_rows = pick(records[late_tick], records[early_tick])
        saved = pick(kept_saved[late_tick], kept_saved[early_tick])
        if step_index < micro_count:
            last_grad = out_grad[step_index]
        else:
            last_grad = jnp.zeros_like(out_grad[0])
        cotangent = jnp.where(is_first, back_in, last_grad)
        grad_hidden, feed_grads = backward_feed(cotangent.astype(jnp.float32), saved, weights)
        feed_totals = tuple((left + right for left, right in zip(totals[5:], feed_grads)))
        grad_in, attend_grads = backward_attend(grad_hidden, saved, crop_rows, weights)
        attend_totals = tuple((left + right for left, right in zip(totals[:5], attend_grads)))
        totals = attend_totals + feed_totals
        sent_grad = grad_in.astype(jnp.bfloat16)
        backward_rows.append(sent_grad)
        if step_index < micro_count:
            back_in = passed_along(sent_grad, "section", -1)
    input_grads = jnp.where(
        is_first, jnp.stack(backward_rows[1:]), jnp.stack(backward_rows[:micro_count])
    )
    summed = lax.psum_scatter(totals, "dp", scatter_dimension=0, tiled=True)
    outputs = tuple((item[None] for item in summed))
    return (layer_outputs[None], input_grads[None]) + outputs


MESH=pl.DeviceIdType.MESH

def place():
    s=lax.axis_index("section"); p=lax.axis_index("dp")
    z=p//4; y=(p//2)%2; c=p%2
    return s,z,y,c

def gather_kernel(n,chunks,ahead,sibling, *refs):
    own=refs[:n]; full=refs[n:2*n]; ssem,rsem,lsem=refs[2*n:]
    K=len(chunks)
    s,z,y,c=place()
    inner=jnp.logical_or(z==1,z==2)
    zo=jnp.where(z==1,0,3); zn=3-z; zon=3-zo
    zi=jnp.where(z==0,1,2)
    idx=lambda z,y,c:(z*2+y)*2+c
    me=idx(z,y,c)
    def rows(k,b):
        j,r0,nr,_=chunks[k]
        r=own[j].shape[0]
        return full[j].at[pl.ds(pl.multiple_of(b*r+r0,nr),nr)]
    def mine(k):
        j,r0,nr,_=chunks[k]
        return own[j].at[pl.ds(r0,nr)]
    counts=[0]*K
    def send(k,b,to,first=False):
        i=counts[k]; counts[k]+=1
        cp=pltpu.make_async_remote_copy(mine(k) if first else rows(k,b), rows(k,b), ssem.at[k,i], rsem.at[k,b], device_id=(s,to), device_id_type=MESH)
        cp.start(); return cp
    def recv(k,b):
        pltpu.make_async_remote_copy(rows(k,b), rows(k,b), ssem.at[k,0], rsem.at[k,b], device_id=(s,me), device_id_type=MESH).wait_recv()
    yo=1-y; co=1-c
    sib=idx(z,y,co); ypart=idx(z,yo,c); other=idx(zn,y,c)
    def late(k,take):
        by_z=chunks[k][3]
        take(k,idx(zon,y,c),*((sib,) if by_z else (ypart,sib)))
        take(k,idx(zn,yo,c),sib)
        take(k,idx(zon,yo,c),sib)
    @pl.when(inner)
    def _():
        out=[]
        loc=[]
        def begin(k):
            out.append(send(k,me,ypart,True))
            out.append(send(k,me,other,True))
            if sibling: out.append(send(k,me,sib,True))
            l=pltpu.make_async_copy(mine(k),rows(k,me),lsem.at[k]); l.start(); loc.append(l)
        def take(k,b,*to):
            recv(k,b)
            for t in to:
                if t is sib and not sibling: continue
                out.append(send(k,b,t))
        for k in range(min(ahead,K)): begin(k)
        for k in range(K):
            if k+ahead<K: begin(k+ahead)
            by_z=chunks[k][3]
            take(k,idx(zo,y,c),other,sib)
            take(k,idx(z,yo,c),sib)
            take(k,idx(zn,y,c),ypart,sib)
            take(k,idx(zo,yo,c),*((other,sib) if by_z else (sib,)))
            if k>0: late(k-1,take)
        late(K-1,take)
        for k in range(K):
            loc[k].wait()
            if sibling:
                for zz in range(4):
                    for yy in range(2):
                        recv(k,idx(zz,yy,co))
        for o in out: o.wait_send()
    counts[:]=[0]*K
    @pl.when(jnp.logical_not(inner))
    def _():
        out=[]
        def begin(k):
            out.append(send(k,me,idx(zi,y,c),True))
            out.append(send(k,me,idx(z,yo,c),True))
        for k in range(min(ahead,K)): begin(k)
        for k in range(K):
            if k+ahead<K: begin(k+ahead)
            recv(k,idx(z,yo,c))
            out.append(send(k,idx(z,yo,c),idx(zi,y,c)))
        for o in out: o.wait_send()

def gather(shards, chunks, ahead, sibling, dp, mem=pl.ANY):
    n=len(shards)
    K=len(chunks)
    return pl.pallas_call(
        lambda *r: gather_kernel(n,chunks,ahead,sibling,*r),
        out_shape=tuple(jax.ShapeDtypeStruct((dp*a.shape[0],)+a.shape[1:],a.dtype) for a in shards),
        in_specs=[pl.BlockSpec(memory_space=mem)]*n,
        out_specs=tuple([pl.BlockSpec(memory_space=mem)]*n),
        scratch_shapes=[pltpu.SemaphoreType.DMA((K,16)),pltpu.SemaphoreType.DMA((K,16)),pltpu.SemaphoreType.DMA((K,))],
        compiler_params=pltpu.CompilerParams(has_side_effects=True,vmem_limit_bytes=(60<<20) if mem!=pl.ANY else None),
        name="gather_weights",
    )(*shards)


CHUNKS = (
    (4, 0, 16, False),
    (0, 0, 32, False), (0, 32, 32, True),
    (1, 0, 64, False),
    (2, 0, 32, False), (2, 32, 32, True),
    (3, 0, 128, False), (3, 128, 128, True),
)


def middle(
    block_input, crop_ids, out_grad, norm1_gain, norm1_shift, w_qkv, w_out, b_out,
    norm2_gain, norm2_shift, w_up, b_up, w_down, b_down,
):
    dp = lax.axis_size("dp")
    is_first = lax.axis_index("section") == 0
    section, z, y, core = place()
    inner = jnp.logical_or(z == 1, z == 2)
    narrow = jnp.concatenate(
        [norm1_gain[0], norm1_shift[0], b_out[0], norm2_gain[0], norm2_shift[0], b_down[0], b_up[0]]
    ).reshape(5, 128)
    narrow = jnp.concatenate([narrow, jnp.zeros((11, 128), jnp.bfloat16)])
    w_qkv, w_out, w_up, w_down, narrow = gather(
        (w_qkv[0], w_out[0], w_up[0], w_down[0], narrow), CHUNKS, 3, True, dp
    )
    narrow = narrow.reshape(dp, 16, 128)[:, :5].reshape(dp, 640)
    small = [narrow[:, 64 * i : 64 * i + 64].reshape(-1) for i in range(6)]
    gain_one, shift_one, b_out, gain_two, shift_two, b_down = small
    b_up = narrow[:, 384:].reshape(-1)
    weights = (
        gain_one, shift_one, w_qkv, w_out, b_out, gain_two, shift_two, w_up, b_up, w_down, b_down,
    )
    pairs = [(i, i ^ 4) for i in range(dp)]
    micro, rows, width = block_input.shape
    joined = lambda own: jnp.concatenate([own, lax.ppermute(own, "dp", pairs)])
    inputs = joined(block_input.reshape(-1, width))
    cotangent = joined(out_grad.reshape(-1, width))
    crops = joined(crop_ids.reshape(-1))
    crops = crops + 1024 * (jnp.arange(crops.shape[0]) // rows)
    saved = forward_layer(inputs.astype(jnp.float32), crops, weights)
    passed = lax.ppermute(saved[-1].astype(jnp.bfloat16), "section", [(0, 1)])
    source = jnp.where(is_first, inputs, passed)
    later = forward_layer(source.astype(jnp.float32), crops, weights)
    grad = cotangent.astype(jnp.float32)
    grad_hidden, feed = backward_feed(grad, later, weights)
    grad_in, attend = backward_attend(grad_hidden, later, crops, weights)
    passed = lax.ppermute(grad_in.astype(jnp.bfloat16), "section", [(1, 0)])
    grad = jnp.where(is_first, passed, cotangent).astype(jnp.float32)
    grad_hidden, feed = backward_feed(grad, later, weights)
    grad_in, attend = backward_attend(grad_hidden, later, crops, weights)
    totals = attend + feed

    def returned(values):
        values = values.astype(jnp.bfloat16)
        half = values.shape[0] // 2
        back = lax.ppermute(values[half:], "dp", pairs)
        return jnp.where(inner, values[:half], back).reshape(1, micro, rows, width)

    summed = []
    for item in totals:
        item = jnp.where(inner, item, 0.0)
        if item.ndim == 2:
            item = item.astype(jnp.bfloat16)
        summed.append(lax.psum_scatter(item, "dp", scatter_dimension=0, tiled=True).astype(jnp.float32)[None])
    return (returned(later[-1]), returned(grad_in)) + tuple(summed)


def solution(mesh):
    in_specs = (
        P(None, "dp", None),
        P(None, "dp"),
        P(None, "dp", None),
        P("section", "dp"),
        P("section", "dp"),
        P("section", "dp", None),
        P("section", "dp", None),
        P("section", "dp"),
        P("section", "dp"),
        P("section", "dp"),
        P("section", "dp", None),
        P("section", "dp"),
        P("section", "dp", None),
        P("section", "dp"),
    )
    out_specs = (
        P("section", None, "dp", None),
        P("section", None, "dp", None),
        P("section", "dp"),
        P("section", "dp"),
        P("section", "dp", None),
        P("section", "dp", None),
        P("section", "dp"),
        P("section", "dp"),
        P("section", "dp"),
        P("section", "dp", None),
        P("section", "dp"),
        P("section", "dp", None),
        P("section", "dp"),
    )
    fits = mesh.shape["dp"] == 16 and mesh.shape["section"] == 2
    return jax.shard_map(middle if fits else local, mesh=mesh, in_specs=in_specs, out_specs=out_specs, check_vma=False)
```

```python
import functools

import jax
import jax.numpy as jnp
from jax import lax
from jax.experimental import pallas as pl
from jax.experimental.pallas import tpu as pltpu
from jax.sharding import PartitionSpec as P

HEAD = 64


def passed_along(x, axis, by):
    devices = lax.axis_size(axis)
    pairs = [(i, i + by) for i in range(devices) if 0 <= i + by < devices]
    return lax.ppermute(x, axis, pairs)


def norm_rows(values, gain, shift):
    centred = values - jnp.mean(values, axis=-1, keepdims=True)
    spread = jnp.mean(centred * centred, axis=-1, keepdims=True)
    return centred * lax.rsqrt(spread + 1e-06) * gain + shift


def gelu_exact(values):
    return jax.nn.gelu(values, approximate=False)


def inner_rows(left, right):
    return lax.dot_general(
        left, right, (((0,), (0,)), ((), ())), preferred_element_type=jnp.float32
    )


def times_transpose(left, right):
    return lax.dot_general(
        left, right, (((1,), (1,)), ((), ())), preferred_element_type=jnp.float32
    )


def split_heads(qkv_rows):
    model_width = qkv_rows.shape[1] // 3
    head_count = model_width // HEAD
    queries = qkv_rows[:, :model_width].reshape(-1, head_count, HEAD)
    key_rows = qkv_rows[:, model_width : 2 * model_width].reshape(-1, head_count, HEAD)
    value_rows = qkv_rows[:, 2 * model_width :].reshape(-1, head_count, HEAD)
    return (queries, key_rows, value_rows)


def head_scores(qkv_rows, crop_rows):
    queries, key_rows, value_rows = split_heads(qkv_rows)
    scores = jnp.einsum("qhd,khd->hqk", queries, key_rows, preferred_element_type=jnp.float32)
    scores = scores * HEAD ** (-0.5)
    same_crop = crop_rows[:, None] == crop_rows[None, :]
    return jnp.where(same_crop[None], scores, -1e30)


def forward_layer(layer_in, crop_rows, weights):
    gain_one, shift_one, w_qkv, w_out, b_out, gain_two, shift_two, w_up, b_up, w_down, b_down = (
        weights
    )
    row_count = layer_in.shape[0]
    normed = norm_rows(
        layer_in, gain_one.astype(jnp.float32), shift_one.astype(jnp.float32)
    ).astype(jnp.bfloat16)
    qkv_rows = jnp.dot(normed, w_qkv, preferred_element_type=jnp.float32).astype(jnp.bfloat16)
    scores = head_scores(qkv_rows, crop_rows)
    row_peak = jnp.max(scores, axis=-1, keepdims=True)
    log_total = row_peak + jnp.log(jnp.sum(jnp.exp(scores - row_peak), axis=-1, keepdims=True))
    softmax_low = jnp.exp(scores - log_total).astype(jnp.bfloat16)
    queries, key_rows, value_rows = split_heads(qkv_rows)
    mixed_heads = jnp.einsum(
        "hqk,khd->qhd", softmax_low, value_rows, preferred_element_type=jnp.float32
    )
    mixed_heads = mixed_heads.reshape(row_count, -1).astype(jnp.bfloat16)
    hidden = (
        layer_in
        + jnp.dot(mixed_heads, w_out, preferred_element_type=jnp.float32)
        + b_out.astype(jnp.float32)
    )
    squeezed = norm_rows(
        hidden, gain_two.astype(jnp.float32), shift_two.astype(jnp.float32)
    ).astype(jnp.bfloat16)
    up_rows = jnp.dot(squeezed, w_up, preferred_element_type=jnp.float32) + b_up.astype(jnp.float32)
    active = gelu_exact(up_rows).astype(jnp.bfloat16)
    result = (
        hidden
        + jnp.dot(active, w_down, preferred_element_type=jnp.float32)
        + b_down.astype(jnp.float32)
    )
    return (
        layer_in,
        normed,
        qkv_rows,
        log_total,
        mixed_heads,
        hidden,
        squeezed,
        up_rows,
        active,
        result,
    )


def backward_feed(grad_result, saved, weights):
    gain_one, shift_one, w_qkv, w_out, b_out, gain_two, shift_two, w_up, b_up, w_down, b_down = (
        weights
    )
    (
        layer_in,
        normed,
        qkv_rows,
        log_total,
        mixed_heads,
        hidden,
        squeezed,
        up_rows,
        active,
        result,
    ) = saved
    grad_branch = grad_result.astype(jnp.bfloat16)
    grad_w_down = inner_rows(active, grad_branch)
    grad_b_down = jnp.sum(grad_branch.astype(jnp.float32), axis=0)
    grad_active = times_transpose(grad_branch, w_down)
    gelu_value, gelu_pull = jax.vjp(gelu_exact, up_rows)
    grad_up = gelu_pull(grad_active)[0].astype(jnp.bfloat16)
    grad_w_up = inner_rows(squeezed, grad_up)
    grad_b_up = jnp.sum(grad_up.astype(jnp.float32), axis=0)
    grad_squeezed = times_transpose(grad_up, w_up)
    norm_value, norm_pull = jax.vjp(
        norm_rows, hidden, gain_two.astype(jnp.float32), shift_two.astype(jnp.float32)
    )
    grad_hid, grad_gain_two, grad_shift_two = norm_pull(grad_squeezed)
    grad_hidden = grad_result + grad_hid
    return (
        grad_hidden,
        (grad_gain_two, grad_shift_two, grad_w_up, grad_b_up, grad_w_down, grad_b_down),
    )


def backward_attend(grad_hidden, saved, crop_rows, weights):
    gain_one, shift_one, w_qkv, w_out, b_out, gain_two, shift_two, w_up, b_up, w_down, b_down = (
        weights
    )
    (
        layer_in,
        normed,
        qkv_rows,
        log_total,
        mixed_heads,
        hidden,
        squeezed,
        up_rows,
        active,
        result,
    ) = saved
    row_count = layer_in.shape[0]
    grad_attn = grad_hidden.astype(jnp.bfloat16)
    grad_w_out = inner_rows(mixed_heads, grad_attn)
    grad_b_out = jnp.sum(grad_attn.astype(jnp.float32), axis=0)
    grad_mixed = times_transpose(grad_attn, w_out).astype(jnp.bfloat16)
    queries, key_rows, value_rows = split_heads(qkv_rows)
    grad_mixed = grad_mixed.reshape(queries.shape)
    softmax_out = jnp.exp(head_scores(qkv_rows, crop_rows) - log_total)
    grad_soft = jnp.einsum(
        "qhd,khd->hqk", grad_mixed, value_rows, preferred_element_type=jnp.float32
    )
    grad_values = jnp.einsum(
        "hqk,qhd->khd",
        softmax_out.astype(jnp.bfloat16),
        grad_mixed,
        preferred_element_type=jnp.float32,
    )
    row_centre = jnp.sum(grad_soft * softmax_out, axis=-1, keepdims=True)
    grad_scores = (softmax_out * (grad_soft - row_centre)).astype(jnp.bfloat16)
    grad_queries = jnp.einsum(
        "hqk,khd->qhd", grad_scores, key_rows, preferred_element_type=jnp.float32
    ) * HEAD ** (-0.5)
    grad_keys = jnp.einsum(
        "hqk,qhd->khd", grad_scores, queries, preferred_element_type=jnp.float32
    ) * HEAD ** (-0.5)
    grad_qkv = jnp.concatenate(
        [
            grad_queries.reshape(row_count, -1),
            grad_keys.reshape(row_count, -1),
            grad_values.reshape(row_count, -1),
        ],
        axis=1,
    ).astype(jnp.bfloat16)
    grad_w_qkv = inner_rows(normed, grad_qkv)
    grad_normed = times_transpose(grad_qkv, w_qkv)
    first_value, first_pull = jax.vjp(
        norm_rows, layer_in, gain_one.astype(jnp.float32), shift_one.astype(jnp.float32)
    )
    grad_in, grad_gain_one, grad_shift_one = first_pull(grad_normed)
    return (
        grad_hidden + grad_in,
        (grad_gain_one, grad_shift_one, grad_w_qkv, grad_w_out, grad_b_out),
    )


def local(
    block_input,
    crop_ids,
    out_grad,
    norm1_gain,
    norm1_shift,
    w_qkv,
    w_out,
    b_out,
    norm2_gain,
    norm2_shift,
    w_up,
    b_up,
    w_down,
    b_down,
):
    is_first = lax.axis_index("section") == 0
    shards = (
        norm1_gain,
        norm1_shift,
        w_qkv,
        w_out,
        b_out,
        norm2_gain,
        norm2_shift,
        w_up,
        b_up,
        w_down,
        b_down,
    )
    gathered = (
        lax.all_gather(shards[0], "dp", axis=1, tiled=True),
        lax.all_gather(shards[1], "dp", axis=1, tiled=True),
        lax.all_gather(shards[2], "dp", axis=1, tiled=True),
        lax.all_gather(shards[3], "dp", axis=1, tiled=True),
        lax.all_gather(shards[4], "dp", axis=1, tiled=True),
        lax.all_gather(shards[5], "dp", axis=1, tiled=True),
        lax.all_gather(shards[6], "dp", axis=1, tiled=True),
        lax.all_gather(shards[7], "dp", axis=1, tiled=True),
        lax.all_gather(shards[8], "dp", axis=1, tiled=True),
        lax.all_gather(shards[9], "dp", axis=1, tiled=True),
        lax.all_gather(shards[10], "dp", axis=1, tiled=True),
    )
    weights = tuple((item[0] for item in gathered))
    micro_count = block_input.shape[0]

    def pick(upper, lower):
        return jax.tree.map(
            lambda later, earlier: jnp.where(is_first, earlier, later), upper, lower
        )

    incoming = jnp.zeros(block_input.shape[1:], jnp.bfloat16)
    records = []
    kept_saved = []
    forward_rows = []
    for step_index in range(micro_count + 1):
        own_rows = block_input[min(step_index, micro_count - 1)]
        source = jnp.where(is_first, own_rows, incoming)
        crop_rows = jnp.where(
            is_first, crop_ids[min(step_index, micro_count - 1)], crop_ids[max(step_index - 1, 0)]
        )
        saved = forward_layer(source.astype(jnp.float32), crop_rows, weights)
        sent_rows = saved[-1].astype(jnp.bfloat16)
        forward_rows.append(sent_rows)
        records.append((source, crop_rows))
        kept_saved.append(saved)
        if step_index < micro_count:
            incoming = passed_along(sent_rows, "section", 1)
    layer_outputs = jnp.where(
        is_first, jnp.stack(forward_rows[:micro_count]), jnp.stack(forward_rows[1:])
    )
    totals = jax.tree.map(lambda item: jnp.zeros(item.shape, jnp.float32), weights)
    back_in = jnp.zeros(block_input.shape[1:], jnp.bfloat16)
    backward_rows = []
    for step_index in range(micro_count + 1):
        late_tick = min(step_index + 1, micro_count)
        early_tick = max(step_index - 1, 0)
        source, crop_rows = pick(records[late_tick], records[early_tick])
        saved = pick(kept_saved[late_tick], kept_saved[early_tick])
        if step_index < micro_count:
            last_grad = out_grad[step_index]
        else:
            last_grad = jnp.zeros_like(out_grad[0])
        cotangent = jnp.where(is_first, back_in, last_grad)
        grad_hidden, feed_grads = backward_feed(cotangent.astype(jnp.float32), saved, weights)
        feed_totals = tuple((left + right for left, right in zip(totals[5:], feed_grads)))
        grad_in, attend_grads = backward_attend(grad_hidden, saved, crop_rows, weights)
        attend_totals = tuple((left + right for left, right in zip(totals[:5], attend_grads)))
        totals = attend_totals + feed_totals
        sent_grad = grad_in.astype(jnp.bfloat16)
        backward_rows.append(sent_grad)
        if step_index < micro_count:
            back_in = passed_along(sent_grad, "section", -1)
    input_grads = jnp.where(
        is_first, jnp.stack(backward_rows[1:]), jnp.stack(backward_rows[:micro_count])
    )
    summed = lax.psum_scatter(totals, "dp", scatter_dimension=0, tiled=True)
    outputs = tuple((item[None] for item in summed))
    return (layer_outputs[None], input_grads[None]) + outputs


MESH = pl.DeviceIdType.MESH
F = jnp.float32
B = jnp.bfloat16
VECTORS = ("g1", "s1", "bo", "g2", "s2", "bd", "bu")
PARTS = (
    (4, 0, 16, False),
    (0, 0, 32, False), (0, 32, 32, True),
    (1, 0, 64, False),
    (2, 0, 32, False), (2, 32, 32, True),
    (3, 0, 128, False), (3, 128, 128, True),
)
AHEAD = 3
SUMS = (
    (3, 0, 128, False), (3, 128, 128, True),
    (2, 0, 32, False), (2, 32, 32, True),
    (1, 0, 64, False),
    (0, 0, 32, False), (0, 32, 32, True),
    (4, 0, 16, False),
)
A, O, C, G, DM, DU, DB, DQKV = range(8)


def nt(left, right):
    return lax.dot_general(left, right, (((1,), (1,)), ((), ())), preferred_element_type=F)


def tn(left, right):
    return lax.dot_general(left, right, (((0,), (0,)), ((), ())), preferred_element_type=F)


def nn(left, right):
    return jnp.dot(left, right, preferred_element_type=F)


def tiles(total, step):
    def run(body):
        @pl.loop(0, total // step)
        def _(i):
            body(pl.ds(pl.multiple_of(i * step, step), step))

    return run


def normed(values):
    centred = values - jnp.mean(values, axis=-1, keepdims=True)
    scale = lax.rsqrt(jnp.mean(centred * centred, axis=-1, keepdims=True) + 1e-6)
    return centred * scale, scale


def norm_into(out, rows, gain, shift):
    @tiles(rows.shape[0], 64)
    def _(r):
        hat, _ = normed(rows[r, :].astype(F))
        out[r, :] = (hat * gain[...] + shift[...]).astype(B)


def norm_back(rows, grad, base, out, gain, gain_sum, shift_sum):
    gain_sum[...] = jnp.zeros_like(gain_sum)
    shift_sum[...] = jnp.zeros_like(shift_sum)

    @tiles(rows.shape[0], 64)
    def _(r):
        hat, scale = normed(rows[r, :].astype(F))
        d = grad[r, :]
        gain_sum[...] += jnp.sum(d * hat, axis=0, keepdims=True)
        shift_sum[...] += jnp.sum(d, axis=0, keepdims=True)
        d = d * gain[...]
        mean = jnp.mean(d, axis=-1, keepdims=True)
        along = jnp.mean(d * hat, axis=-1, keepdims=True)
        out[r, :] = (base[r, :].astype(F) + scale * (d - mean - hat * along)).astype(out.dtype)


def halves(pair):
    low = lax.broadcasted_iota(jnp.int32, pair.shape, 1) < HEAD
    zero = jnp.zeros_like(pair)
    return jnp.where(low, pair, zero), jnp.where(low, zero, pair)


def softmax(queries, keys, bias):
    scores = nt(queries, keys) * HEAD**-0.5 + bias
    raised = jnp.exp(scores - jnp.max(scores, axis=-1, keepdims=True))
    return raised / jnp.sum(raised, axis=-1, keepdims=True)


def attend(qkv, mixed, bias):
    width = qkv.shape[1] // 3

    @pl.loop(0, width // 128)
    def _(i):
        for t in range(qkv.shape[0] // 128):
            r = pl.ds(t * 128, 128)
            q, k, v = (qkv[r, pl.ds(pl.multiple_of(g * width + i * 128, 128), 128)] for g in range(3))
            parts = [nn(softmax(a, k, bias[r, :]).astype(B), b) for a, b in zip(halves(q), halves(v))]
            mixed[r, pl.ds(pl.multiple_of(i * 128, 128), 128)] = (parts[0] + parts[1]).astype(B)


def attend_back(qkv, grad, bias):
    width = qkv.shape[1] // 3

    @pl.loop(0, width // 128)
    def _(i):
        for t in range(qkv.shape[0] // 128):
            r = pl.ds(t * 128, 128)
            cols = [pl.ds(pl.multiple_of(g * width + i * 128, 128), 128) for g in range(3)]
            q, k, v = (qkv[r, c] for c in cols)
            d = grad[r, cols[0]]
            sums = None
            for qh, kh, dh in zip(halves(q), halves(k), halves(d)):
                p = softmax(qh, k, bias[r, :])
                dp = nt(dh, v)
                ds = (p * (dp - jnp.sum(dp * p, axis=-1, keepdims=True))).astype(B)
                terms = (nn(ds, kh), tn(ds, qh), tn(p.astype(B), dh))
                sums = terms if sums is None else [a + b for a, b in zip(sums, terms)]
            qkv[r, cols[0]] = (sums[0] * HEAD**-0.5).astype(B)
            qkv[r, cols[1]] = (sums[1] * HEAD**-0.5).astype(B)
            qkv[r, cols[2]] = sums[2].astype(B)


def relay(names, *refs):
    ref = dict(zip(names, refs))
    width = ref["x_own"].shape[1]
    rows = ref["x_own"].shape[0]
    ff = ref["w2"].shape[1]
    shard = [ref[f"own{j}"] for j in range(5)]
    full = [ref[f"w{j}"] for j in range(5)]
    both = [ref[n] for n in ("a", "o", "c", "g", "dm", "du", "db", "dqkv")]
    mine = [b.at[pl.ds(0, 2 * rows)] for b in both]
    theirs = [b.at[pl.ds(2 * rows, 2 * rows)] for b in both]
    vec = {n: ref["v_" + n] for n in VECTORS}
    vsum = {n: ref["d_" + n] for n in VECTORS}
    x, hidden, wide, dmixed, result = (ref[n] for n in ("x", "h", "wide", "do", "y"))
    p = lax.axis_index("dp")
    z, y, core = p // 4, (p // 2) % 2, p % 2
    inner = jnp.logical_or(z == 1, z == 2)
    section = lax.axis_index("section")
    zo, zn = jnp.where(z == 1, 0, 3), 3 - z
    zon = 3 - zo
    zi = jnp.where(z == 0, 1, 2)

    def idx(z, y, core):
        return (z * 2 + y) * 2 + core

    sibling, across, other = idx(z, y, 1 - core), idx(z, 1 - y, core), idx(zn, y, core)
    outer_one, inner_one = idx(zo, y, core), idx(zi, y, core)

    def remote(sec, src, dst, send_sem, recv_sem, to):
        return pltpu.make_async_remote_copy(
            src_ref=src, dst_ref=dst, send_sem=send_sem, recv_sem=recv_sem,
            device_id=(sec, to), device_id_type=MESH,
        )

    class Flow:
        def __init__(self, sec):
            self.sec = sec
            self.sent = []

        def send(self, *args, sec=None):
            copy = remote(self.sec if sec is None else sec, *args)
            copy.start()
            self.sent.append(copy)

        def arrived(self, dst, recv_sem):
            remote(self.sec, dst, dst, ref["idle_sem"].at[0], recv_sem, sibling).wait_recv()

        def finish(self):
            for copy in self.sent:
                copy.wait_send()
            self.sent = []

    def piece(k, b):
        j, first, count, _ = PARTS[k]
        size = shard[j].shape[0]
        return full[j].at[pl.ds(pl.multiple_of(b * size + first, count), count)]

    def gather_steps(flow, is_inner):
        used = [0] * len(PARTS)

        def send(k, b, to, own=False):
            j, first, count, _ = PARTS[k]
            src = shard[j].at[pl.ds(first, count)] if own else piece(k, b)
            flow.send(src, piece(k, b), ref["ag_send"].at[k, used[k]], ref["ag_recv"].at[k, b], to)
            used[k] += 1

        def take(k, b, *to):
            flow.arrived(piece(k, b), ref["ag_recv"].at[k, b])
            for target in to:
                send(k, b, target)

        def begin(k):
            if is_inner:
                for to in (across, other, sibling):
                    send(k, p, to, own=True)
                j, first, count, _ = PARTS[k]
                pltpu.make_async_copy(shard[j].at[pl.ds(first, count)], piece(k, p), ref["ag_local"].at[k]).start()
            else:
                send(k, p, inner_one, own=True)
                send(k, p, across, own=True)

        def early(k):
            if not is_inner:
                take(k, across, inner_one)
                return
            by_z = PARTS[k][3]
            take(k, idx(zo, y, core), other, sibling)
            take(k, idx(z, 1 - y, core), sibling)
            take(k, idx(zn, y, core), across, sibling)
            take(k, idx(zo, 1 - y, core), *((other, sibling) if by_z else (sibling,)))

        def late(k):
            by_z = PARTS[k][3]
            take(k, idx(zon, y, core), *((sibling,) if by_z else (across, sibling)))
            take(k, idx(zn, 1 - y, core), sibling)
            take(k, idx(zon, 1 - y, core), sibling)

        def step(k):
            if k == 0:
                for first in range(AHEAD):
                    begin(first)
            if k + AHEAD < len(PARTS):
                begin(k + AHEAD)
            if k < len(PARTS):
                early(k)
            if is_inner and k > 0:
                late(k - 1)

        return step

    def gathered(flow, j):
        for k, part in enumerate(PARTS):
            if part[0] == j:
                j_, first, count, _ = part
                pltpu.make_async_copy(shard[j].at[pl.ds(first, count)], piece(k, p), ref["ag_local"].at[k]).wait()
                for b in range(8):
                    block = 2 * b + 1 - core
                    flow.arrived(piece(k, block), ref["ag_recv"].at[k, block])

    def spread_vectors():
        for i in range(8):
            low = full[4][pl.ds(32 * i, 16), :].astype(F)
            high = full[4][pl.ds(32 * i + 16, 16), :].astype(F)
            joined = low + high
            for n, name in enumerate(VECTORS[:6]):
                vec[name][:, pl.ds(128 * i, 128)] = joined[n : n + 1]
            for n, part in enumerate((low[6:7], low[7:8], high[6:7], high[7:8])):
                vec["bu"][:, pl.ds(512 * i + 128 * n, 128)] = part

    def exchange(flow, which):
        flow.send(mine[which], theirs[which], ref["act_send"].at[which], ref["act_recv"].at[which], sibling)

    def exchanged(flow, *which):
        for w in which:
            flow.arrived(theirs[w], ref["act_recv"].at[w])

    def forward_attend(bias):
        @tiles(3 * width, 1024)
        def _(c):
            mine[DQKV][:, c] = nn(mine[A][...], full[0][:, c]).astype(B)

        attend(mine[DQKV], mine[O], bias)

    def forward_out():
        @tiles(width, 512)
        def _(c):
            hidden[:, c] = x[:, c].astype(F) + nn(mine[O][...], full[1][:, c]) + vec["bo"][:, c]

        norm_into(mine[C], hidden, vec["g2"], vec["s2"])

    def forward_up():
        @tiles(ff, 1024)
        def _(c):
            u = nn(mine[C][...], full[2][:, c]) + vec["bu"][:, c]
            phi = 0.5 + 0.5 * lax.erf(u * 0.5**0.5)
            mine[G][:, c] = (u * phi).astype(B)
            mine[DU][:, c] = (phi + u * (jnp.exp(-0.5 * u * u) * (0.5 / jnp.pi) ** 0.5)).astype(B)

    def forward_down():
        @tiles(width, 512)
        def _(c):
            result[:, c] = (hidden[:, c] + nn(mine[G][...], full[3][:, c]) + vec["bd"][:, c]).astype(B)

    def backward_du():
        vsum["bd"][...] = jnp.sum(mine[DM][...].astype(F), axis=0, keepdims=True)

        @tiles(ff, 1024)
        def _(c):
            du = (nt(mine[DM][...], full[3][c, :]) * mine[DU][:, c].astype(F)).astype(B)
            mine[DU][:, c] = du
            vsum["bu"][:, c] = jnp.sum(du.astype(F), axis=0, keepdims=True)

    def backward_dh():
        @tiles(width, 512)
        def _(c):
            wide[:, c] = nt(mine[DU][...], full[2][c, :])

        norm_back(hidden, wide, mine[DM], hidden, vec["g2"], vsum["g2"], vsum["s2"])
        mine[DB][...] = hidden[...].astype(B)
        vsum["bo"][...] = jnp.sum(mine[DB][...].astype(F), axis=0, keepdims=True)

    def backward_attend(bias):
        @tiles(width, 512)
        def _(c):
            dmixed[:, c] = nt(mine[DB][...], full[1][c, :]).astype(B)

        attend_back(mine[DQKV], dmixed, bias)

    def backward_da():
        @tiles(width, 512)
        def _(c):
            wide[:, c] = nt(mine[DQKV][...], full[0][c, :])

    def backward_dx():
        norm_back(x, wide, hidden, x, vec["g1"], vsum["g1"], vsum["s1"])

    def packed(which):
        src, out = both[which], ref["packed"]
        for i in range(width // 256):
            first = src[:, pl.ds(256 * i, 128)].astype(F)
            second = src[:, pl.ds(256 * i + 128, 128)].astype(F)
            low = lax.broadcasted_iota(jnp.int32, first.shape, 1) < HEAD
            even = jnp.where(low, first, pltpu.roll(second, HEAD, 1))
            odd = jnp.where(low, pltpu.roll(first, HEAD, 1), second)
            out[pl.ds(128 * i, 128), :] = jnp.where(core == 0, even, odd).T.astype(B)

    def grad_down():
        size = shard[3].shape[0]
        for o in range(8):
            c = pl.ds(pl.multiple_of(size * (2 * o + core), size), size)
            full[3][pl.ds(size * o, size), :] = tn(both[G][:, c], both[DM][...]).astype(B)

    def grad_of(j, left, right):
        packed(left)

        @tiles(both[right].shape[1], 512)
        def _(c):
            full[j][pl.ds(0, 8 * shard[j].shape[0]), c] = nn(ref["packed"][...], both[right][:, c]).astype(B)

    def grad_vectors():
        for o in range(8):
            for n, name in enumerate(VECTORS[:6]):
                ref["vp"][pl.ds(16 * o + n, 1), :] = vsum[name][:, pl.ds(128 * o, 128)]
            for n in range(4):
                ref["vp"][pl.ds(16 * o + 6 + n, 1), :] = vsum["bu"][:, pl.ds(512 * o + 128 * n, 128)]
            ref["vp"][pl.ds(16 * o + 10, 6), :] = jnp.zeros((6, 128), F)

    partial = [full[0], full[1], full[2], full[3], ref["vp"]]
    sums = [ref[f"out{j}"] for j in range(4)] + [ref["vs"]]
    NEAR, OWN, ALT, INNER, OUTER = range(5)
    slots = [[ref[f"r{s}_{j}"] for j in range(5)] for s in range(5)]

    def reducer(flow):
        def slot(s, k):
            j, first, count, _ = SUMS[k]
            return slots[s][j].at[pl.ds(first, count)]

        def part(k, zz, yy):
            j, first, count, _ = SUMS[k]
            size = partial[j].shape[0] // 8 if j == 4 else shard[j].shape[0]
            return partial[j].at[pl.ds(pl.multiple_of((zz * 2 + yy) * size + first, count), count)]

        def send(k, n, src, s, to):
            flow.send(src, slot(s, k), ref["rs_send"].at[k, n], ref["rs_recv"].at[k, s], to)

        def arrived(k, s):
            flow.arrived(slot(s, k), ref["rs_recv"].at[k, s])

        def add(k, dst, *more):
            total = dst[...].astype(F)
            for s in more:
                total = total + slot(s, k)[...].astype(F)
            return total

        def issue(k):
            by_z = SUMS[k][3]
            send(k, 0, part(k, zn, 1 - y), NEAR, across)
            if by_z:
                send(k, 1, part(k, zon, 1 - y), ALT, other)
                send(k, 4, part(k, zon, y), OUTER, other)
            else:
                send(k, 1, part(k, zon, 1 - y), ALT, across)
                send(k, 6, part(k, zo, 1 - y), INNER, outer_one)
            send(k, 2, part(k, z, 1 - y), OWN, across)

        def middle(k):
            by_z = SUMS[k][3]
            dst = part(k, zn, y)
            arrived(k, NEAR)
            dst[...] = add(k, dst, NEAR).astype(dst.dtype)
            send(k, 3, dst, INNER, other)
            if not by_z:
                dst = part(k, zon, y)
                arrived(k, ALT)
                dst[...] = add(k, dst, ALT).astype(dst.dtype)
                send(k, 4, dst, OUTER, other)

        def last(k):
            by_z = SUMS[k][3]
            dst = part(k, zo, y)
            arrived(k, OUTER)
            dst[...] = add(k, dst, OUTER).astype(dst.dtype)
            send(k, 5, dst, OUTER, outer_one)
            if by_z:
                dst = part(k, zo, 1 - y)
                arrived(k, ALT)
                dst[...] = add(k, dst, ALT).astype(dst.dtype)
                send(k, 6, dst, INNER, outer_one)
            arrived(k, OWN)
            arrived(k, INNER)
            j, first, count, _ = SUMS[k]
            sums[j][pl.ds(first, count), :] = add(k, part(k, z, y), OWN, INNER)

        def pass_on(k):
            arrived(k, INNER)
            send(k, 0, slot(INNER, k), OWN, across)

        def collect(k):
            arrived(k, OUTER)
            arrived(k, OWN)
            j, first, count, _ = SUMS[k]
            sums[j][pl.ds(first, count), :] = slot(OUTER, k)[...].astype(F) + slot(OWN, k)[...].astype(F)

        def join_vectors():
            flow.send(ref["vs"], ref["vt"], ref["vec_sem"].at[0], ref["vec_sem"].at[1], sibling)
            flow.arrived(ref["vt"], ref["vec_sem"].at[1])
            ref["out4"][...] = ref["vs"][...] + ref["vt"][...]

        return issue, middle, last, pass_on, collect, join_vectors

    def hand_out(flow, src, out, n):
        flow.send(src.at[pl.ds(rows, rows)], out, ref["res_send"].at[n], ref["res_recv"].at[n], outer_one)
        out[...] = src[pl.ds(0, rows), :]

    def inner_program(sec):
        flow = Flow(sec)
        step = gather_steps(flow, True)
        issue, middle, last, _, _, join_vectors = reducer(flow)
        bias = ref["bias"]
        half = pl.ds(0, rows)
        own = [pltpu.make_async_copy(ref["bias_own"], bias.at[half], ref["tok_local"].at[0])]
        if sec == 0:
            own.append(pltpu.make_async_copy(ref["x_own"], x.at[half], ref["tok_local"].at[1]))
        else:
            own.append(pltpu.make_async_copy(ref["dy_own"], mine[DM].at[half], ref["tok_local"].at[1]))
        for copy in own:
            copy.start()

        def tokens():
            for copy in own:
                copy.wait()
            other_half = pl.ds(rows, rows)
            flow.arrived(bias.at[other_half], ref["tok_recv"].at[0])
            flow.arrived((x if sec == 0 else mine[DM]).at[other_half], ref["tok_recv"].at[1])

        if sec == 0:
            for k in range(2):
                step(k)
            gathered(flow, 4)
            spread_vectors()
            tokens()
            norm_into(mine[A], x, vec["g1"], vec["s1"])
            for k in range(2, 4):
                step(k)
            gathered(flow, 0)
            forward_attend(bias)
            for k in range(4, 5):
                step(k)
            gathered(flow, 1)
            forward_out()
            for k in range(5, 7):
                step(k)
            gathered(flow, 2)
            forward_up()
            for k in range(7, 9):
                step(k)
            gathered(flow, 3)
            forward_down()
            flow.send(result, x, ref["x_sem"].at[0], ref["x_sem"].at[1], p, sec=1)
        else:
            for k in range(9):
                step(k)
            for j in range(5):
                gathered(flow, j)
            spread_vectors()
            tokens()
            exchange(flow, DM)
            flow.arrived(x, ref["x_sem"].at[1])
            norm_into(mine[A], x, vec["g1"], vec["s1"])
            forward_attend(bias)
            forward_out()
            forward_up()
            forward_down()
        hand_out(flow, result, ref["y_out"], 0)
        for which in (A, O, C, G):
            exchange(flow, which)
        flow.finish()
        if sec == 0:
            flow.arrived(mine[DM], ref["x_sem"].at[3])
            exchange(flow, DM)
            backward_du()
            exchange(flow, DU)
            exchanged(flow, G, DM)
            grad_down()
            issue(0)
            issue(1)
            backward_dh()
            exchange(flow, DB)
            exchanged(flow, C, DU)
            grad_of(2, C, DU)
            issue(2)
            issue(3)
            backward_attend(bias)
            exchange(flow, DQKV)
            middle(0)
            exchanged(flow, O, DB)
            grad_of(1, O, DB)
            issue(4)
            backward_da()
            exchanged(flow, A, DQKV)
            grad_of(0, A, DQKV)
            issue(5)
            issue(6)
            backward_dx()
            grad_vectors()
            issue(7)
            hand_out(flow, x, ref["dx_out"], 1)
            todo = [(1, 0), (2, 1), (3, 2), (4, 3), (5, 4), (6, 5), (7, 6)]
        else:
            backward_du()
            exchange(flow, DU)
            backward_dh()
            exchange(flow, DB)
            backward_attend(bias)
            exchange(flow, DQKV)
            backward_da()
            backward_dx()
            flow.send(x, mine[DM], ref["x_sem"].at[2], ref["x_sem"].at[3], p, sec=0)
            exchanged(flow, G, DM)
            grad_down()
            issue(0)
            issue(1)
            exchanged(flow, C, DU)
            grad_of(2, C, DU)
            issue(2)
            issue(3)
            hand_out(flow, x, ref["dx_out"], 1)
            exchanged(flow, O, DB)
            grad_of(1, O, DB)
            issue(4)
            exchanged(flow, A, DQKV)
            grad_of(0, A, DQKV)
            issue(5)
            issue(6)
            grad_vectors()
            issue(7)
            middle(0)
            todo = [(1, 0), (2, 1), (3, 2), (4, 3), (5, 4), (6, 5), (7, 6)]
        for a, b in todo:
            middle(a)
            last(b)
        last(7)
        join_vectors()
        flow.finish()

    def outer_program(sec):
        flow = Flow(sec)
        step = gather_steps(flow, False)
        _, _, _, pass_on, collect, join_vectors = reducer(flow)
        half = pl.ds(rows, rows)
        flow.send(ref["bias_own"], ref["bias"].at[half], ref["tok_send"].at[0], ref["tok_recv"].at[0], inner_one)
        src, dst = (ref["x_own"], x) if sec == 0 else (ref["dy_own"], mine[DM])
        flow.send(src, dst.at[half], ref["tok_send"].at[1], ref["tok_recv"].at[1], inner_one)
        for k in range(len(PARTS)):
            step(k)
        for k in range(len(SUMS)):
            pass_on(k)
            if k:
                collect(k - 1)
        collect(len(SUMS) - 1)
        join_vectors()
        flow.arrived(ref["y_out"], ref["res_recv"].at[0])
        flow.arrived(ref["dx_out"], ref["res_recv"].at[1])
        flow.finish()

    for sec in range(2):
        pl.when(jnp.logical_and(inner, section == sec))(lambda sec=sec: inner_program(sec))
        pl.when(jnp.logical_and(jnp.logical_not(inner), section == sec))(lambda sec=sec: outer_program(sec))


def relay_call(x_own, dy_own, bias_own, shards, dp):
    rows, width = x_own.shape
    ff = shards[2].shape[1]
    count = 2 * rows
    inputs = {"x_own": x_own, "dy_own": dy_own, "bias_own": bias_own}
    inputs.update({f"own{j}": item for j, item in enumerate(shards)})
    outputs = {"y_out": ((rows, width), B), "dx_out": ((rows, width), B)}
    outputs.update({f"out{j}": (item.shape, F) for j, item in enumerate(shards[:4])})
    outputs["out4"] = ((16, 128), F)
    scratch = {f"w{j}": ((dp * item.shape[0], item.shape[1]), B) for j, item in enumerate(shards)}
    for name, cols in zip(("a", "o", "c", "g", "dm", "du", "db", "dqkv"), (1, 1, 1, 0, 1, 0, 1, 3)):
        scratch[name] = ((2 * count, cols * width or ff), B)
    scratch.update(x=((count, width), B), h=((count, width), F), wide=((count, width), F), do=((count, width), B))
    scratch.update(y=((count, width), B), bias=((count, 128), F), packed=((width // 2, 2 * count), B))
    for name in VECTORS:
        scratch["v_" + name] = scratch["d_" + name] = ((1, ff if name == "bu" else width), F)
    scratch.update(vp=((128, 128), F), vs=((16, 128), F), vt=((16, 128), F))
    for s in range(5):
        for j, item in enumerate(shards):
            scratch[f"r{s}_{j}"] = (item.shape, F if j == 4 else B)
    sems = dict(
        ag_send=(len(PARTS), 16), ag_recv=(len(PARTS), dp), ag_local=(len(PARTS),), tok_local=(2,), tok_send=(2,),
        tok_recv=(2,), x_sem=(4,), act_send=(8,), act_recv=(8,), res_send=(2,), res_recv=(2,),
        rs_send=(len(SUMS), 7), rs_recv=(len(SUMS), 5), vec_sem=(2,), idle_sem=(1,),
    )
    names = [*inputs, *outputs, *scratch, *sems]
    results = pl.pallas_call(
        functools.partial(relay, names),
        out_shape=[jax.ShapeDtypeStruct(*item) for item in outputs.values()],
        in_specs=[pl.BlockSpec(memory_space=pl.ANY)] * len(inputs),
        out_specs=[pl.BlockSpec(memory_space=pltpu.VMEM)] * len(outputs),
        scratch_shapes=[pltpu.VMEM(*item) for item in scratch.values()]
        + [pltpu.SemaphoreType.DMA(item) for item in sems.values()],
        compiler_params=pltpu.CompilerParams(has_side_effects=True, vmem_limit_bytes=62 << 20),
        name="relay",
    )(*inputs.values())
    return dict(zip(outputs, results))


def middle(
    block_input, crop_ids, out_grad, norm1_gain, norm1_shift, w_qkv, w_out, b_out,
    norm2_gain, norm2_shift, w_up, b_up, w_down, b_down,
):
    core = lax.axis_index("dp") % 2
    micro, rows, width = block_input.shape
    crops = crop_ids + 1024 * jnp.arange(micro)[:, None]
    crops = crops.reshape(-1)
    bias = jnp.where(crops[:, None] == crops[None, :], 0.0, -1e30).astype(F)
    narrow = jnp.concatenate([norm1_gain, norm1_shift, b_out, norm2_gain, norm2_shift, b_down])
    empty = jnp.zeros_like(narrow)
    narrow = jnp.where(core == 0, jnp.concatenate([narrow, empty], 1), jnp.concatenate([empty, narrow], 1))
    narrow = jnp.concatenate([narrow, b_up.reshape(2, 128), jnp.zeros((8, 128), B)])
    got = relay_call(
        block_input.reshape(-1, width), out_grad.reshape(-1, width), bias,
        (w_qkv[0], w_out[0], w_up[0], w_down[0], narrow), lax.axis_size("dp"),
    )
    sums = got["out4"]
    narrow = jnp.where(core == 0, sums[:6, :64], sums[:6, 64:])[:, None]
    grad_b_up = jnp.where(core == 0, sums[6:8], sums[8:10]).reshape(1, -1)
    shape = (1, micro, rows, width)
    return (
        got["y_out"].reshape(shape), got["dx_out"].reshape(shape), narrow[0], narrow[1], got["out0"][None],
        got["out1"][None], narrow[2], narrow[3], narrow[4], got["out2"][None], grad_b_up, got["out3"][None], narrow[5],
    )


def solution(mesh):
    in_specs = (
        P(None, "dp", None),
        P(None, "dp"),
        P(None, "dp", None),
        P("section", "dp"),
        P("section", "dp"),
        P("section", "dp", None),
        P("section", "dp", None),
        P("section", "dp"),
        P("section", "dp"),
        P("section", "dp"),
        P("section", "dp", None),
        P("section", "dp"),
        P("section", "dp", None),
        P("section", "dp"),
    )
    out_specs = (
        P("section", None, "dp", None),
        P("section", None, "dp", None),
        P("section", "dp"),
        P("section", "dp"),
        P("section", "dp", None),
        P("section", "dp", None),
        P("section", "dp"),
        P("section", "dp"),
        P("section", "dp"),
        P("section", "dp", None),
        P("section", "dp"),
        P("section", "dp", None),
        P("section", "dp"),
    )
    fits = mesh.shape["dp"] == 16 and mesh.shape["section"] == 2
    return jax.shard_map(middle if fits else local, mesh=mesh, in_specs=in_specs, out_specs=out_specs, check_vma=False)
```

```python
import functools

import jax
import jax.numpy as jnp
from jax import lax
from jax.experimental import pallas as pl
from jax.experimental.pallas import tpu as pltpu
from jax.sharding import PartitionSpec as P

HEAD = 64


def passed_along(x, axis, by):
    devices = lax.axis_size(axis)
    pairs = [(i, i + by) for i in range(devices) if 0 <= i + by < devices]
    return lax.ppermute(x, axis, pairs)


def norm_rows(values, gain, shift):
    centred = values - jnp.mean(values, axis=-1, keepdims=True)
    spread = jnp.mean(centred * centred, axis=-1, keepdims=True)
    return centred * lax.rsqrt(spread + 1e-06) * gain + shift


def gelu_exact(values):
    return jax.nn.gelu(values, approximate=False)


def inner_rows(left, right):
    return lax.dot_general(
        left, right, (((0,), (0,)), ((), ())), preferred_element_type=jnp.float32
    )


def times_transpose(left, right):
    return lax.dot_general(
        left, right, (((1,), (1,)), ((), ())), preferred_element_type=jnp.float32
    )


def split_heads(qkv_rows):
    model_width = qkv_rows.shape[1] // 3
    head_count = model_width // HEAD
    queries = qkv_rows[:, :model_width].reshape(-1, head_count, HEAD)
    key_rows = qkv_rows[:, model_width : 2 * model_width].reshape(-1, head_count, HEAD)
    value_rows = qkv_rows[:, 2 * model_width :].reshape(-1, head_count, HEAD)
    return (queries, key_rows, value_rows)


def head_scores(qkv_rows, crop_rows):
    queries, key_rows, value_rows = split_heads(qkv_rows)
    scores = jnp.einsum("qhd,khd->hqk", queries, key_rows, preferred_element_type=jnp.float32)
    scores = scores * HEAD ** (-0.5)
    same_crop = crop_rows[:, None] == crop_rows[None, :]
    return jnp.where(same_crop[None], scores, -1e30)


def forward_layer(layer_in, crop_rows, weights):
    gain_one, shift_one, w_qkv, w_out, b_out, gain_two, shift_two, w_up, b_up, w_down, b_down = (
        weights
    )
    row_count = layer_in.shape[0]
    normed = norm_rows(
        layer_in, gain_one.astype(jnp.float32), shift_one.astype(jnp.float32)
    ).astype(jnp.bfloat16)
    qkv_rows = jnp.dot(normed, w_qkv, preferred_element_type=jnp.float32).astype(jnp.bfloat16)
    scores = head_scores(qkv_rows, crop_rows)
    row_peak = jnp.max(scores, axis=-1, keepdims=True)
    log_total = row_peak + jnp.log(jnp.sum(jnp.exp(scores - row_peak), axis=-1, keepdims=True))
    softmax_low = jnp.exp(scores - log_total).astype(jnp.bfloat16)
    queries, key_rows, value_rows = split_heads(qkv_rows)
    mixed_heads = jnp.einsum(
        "hqk,khd->qhd", softmax_low, value_rows, preferred_element_type=jnp.float32
    )
    mixed_heads = mixed_heads.reshape(row_count, -1).astype(jnp.bfloat16)
    hidden = (
        layer_in
        + jnp.dot(mixed_heads, w_out, preferred_element_type=jnp.float32)
        + b_out.astype(jnp.float32)
    )
    squeezed = norm_rows(
        hidden, gain_two.astype(jnp.float32), shift_two.astype(jnp.float32)
    ).astype(jnp.bfloat16)
    up_rows = jnp.dot(squeezed, w_up, preferred_element_type=jnp.float32) + b_up.astype(jnp.float32)
    active = gelu_exact(up_rows).astype(jnp.bfloat16)
    result = (
        hidden
        + jnp.dot(active, w_down, preferred_element_type=jnp.float32)
        + b_down.astype(jnp.float32)
    )
    return (
        layer_in,
        normed,
        qkv_rows,
        log_total,
        mixed_heads,
        hidden,
        squeezed,
        up_rows,
        active,
        result,
    )


def backward_feed(grad_result, saved, weights):
    gain_one, shift_one, w_qkv, w_out, b_out, gain_two, shift_two, w_up, b_up, w_down, b_down = (
        weights
    )
    (
        layer_in,
        normed,
        qkv_rows,
        log_total,
        mixed_heads,
        hidden,
        squeezed,
        up_rows,
        active,
        result,
    ) = saved
    grad_branch = grad_result.astype(jnp.bfloat16)
    grad_w_down = inner_rows(active, grad_branch)
    grad_b_down = jnp.sum(grad_branch.astype(jnp.float32), axis=0)
    grad_active = times_transpose(grad_branch, w_down)
    gelu_value, gelu_pull = jax.vjp(gelu_exact, up_rows)
    grad_up = gelu_pull(grad_active)[0].astype(jnp.bfloat16)
    grad_w_up = inner_rows(squeezed, grad_up)
    grad_b_up = jnp.sum(grad_up.astype(jnp.float32), axis=0)
    grad_squeezed = times_transpose(grad_up, w_up)
    norm_value, norm_pull = jax.vjp(
        norm_rows, hidden, gain_two.astype(jnp.float32), shift_two.astype(jnp.float32)
    )
    grad_hid, grad_gain_two, grad_shift_two = norm_pull(grad_squeezed)
    grad_hidden = grad_result + grad_hid
    return (
        grad_hidden,
        (grad_gain_two, grad_shift_two, grad_w_up, grad_b_up, grad_w_down, grad_b_down),
    )


def backward_attend(grad_hidden, saved, crop_rows, weights):
    gain_one, shift_one, w_qkv, w_out, b_out, gain_two, shift_two, w_up, b_up, w_down, b_down = (
        weights
    )
    (
        layer_in,
        normed,
        qkv_rows,
        log_total,
        mixed_heads,
        hidden,
        squeezed,
        up_rows,
        active,
        result,
    ) = saved
    row_count = layer_in.shape[0]
    grad_attn = grad_hidden.astype(jnp.bfloat16)
    grad_w_out = inner_rows(mixed_heads, grad_attn)
    grad_b_out = jnp.sum(grad_attn.astype(jnp.float32), axis=0)
    grad_mixed = times_transpose(grad_attn, w_out).astype(jnp.bfloat16)
    queries, key_rows, value_rows = split_heads(qkv_rows)
    grad_mixed = grad_mixed.reshape(queries.shape)
    softmax_out = jnp.exp(head_scores(qkv_rows, crop_rows) - log_total)
    grad_soft = jnp.einsum(
        "qhd,khd->hqk", grad_mixed, value_rows, preferred_element_type=jnp.float32
    )
    grad_values = jnp.einsum(
        "hqk,qhd->khd",
        softmax_out.astype(jnp.bfloat16),
        grad_mixed,
        preferred_element_type=jnp.float32,
    )
    row_centre = jnp.sum(grad_soft * softmax_out, axis=-1, keepdims=True)
    grad_scores = (softmax_out * (grad_soft - row_centre)).astype(jnp.bfloat16)
    grad_queries = jnp.einsum(
        "hqk,khd->qhd", grad_scores, key_rows, preferred_element_type=jnp.float32
    ) * HEAD ** (-0.5)
    grad_keys = jnp.einsum(
        "hqk,qhd->khd", grad_scores, queries, preferred_element_type=jnp.float32
    ) * HEAD ** (-0.5)
    grad_qkv = jnp.concatenate(
        [
            grad_queries.reshape(row_count, -1),
            grad_keys.reshape(row_count, -1),
            grad_values.reshape(row_count, -1),
        ],
        axis=1,
    ).astype(jnp.bfloat16)
    grad_w_qkv = inner_rows(normed, grad_qkv)
    grad_normed = times_transpose(grad_qkv, w_qkv)
    first_value, first_pull = jax.vjp(
        norm_rows, layer_in, gain_one.astype(jnp.float32), shift_one.astype(jnp.float32)
    )
    grad_in, grad_gain_one, grad_shift_one = first_pull(grad_normed)
    return (
        grad_hidden + grad_in,
        (grad_gain_one, grad_shift_one, grad_w_qkv, grad_w_out, grad_b_out),
    )


def local(
    block_input,
    crop_ids,
    out_grad,
    norm1_gain,
    norm1_shift,
    w_qkv,
    w_out,
    b_out,
    norm2_gain,
    norm2_shift,
    w_up,
    b_up,
    w_down,
    b_down,
):
    is_first = lax.axis_index("section") == 0
    shards = (
        norm1_gain,
        norm1_shift,
        w_qkv,
        w_out,
        b_out,
        norm2_gain,
        norm2_shift,
        w_up,
        b_up,
        w_down,
        b_down,
    )
    gathered = (
        lax.all_gather(shards[0], "dp", axis=1, tiled=True),
        lax.all_gather(shards[1], "dp", axis=1, tiled=True),
        lax.all_gather(shards[2], "dp", axis=1, tiled=True),
        lax.all_gather(shards[3], "dp", axis=1, tiled=True),
        lax.all_gather(shards[4], "dp", axis=1, tiled=True),
        lax.all_gather(shards[5], "dp", axis=1, tiled=True),
        lax.all_gather(shards[6], "dp", axis=1, tiled=True),
        lax.all_gather(shards[7], "dp", axis=1, tiled=True),
        lax.all_gather(shards[8], "dp", axis=1, tiled=True),
        lax.all_gather(shards[9], "dp", axis=1, tiled=True),
        lax.all_gather(shards[10], "dp", axis=1, tiled=True),
    )
    weights = tuple((item[0] for item in gathered))
    micro_count = block_input.shape[0]

    def pick(upper, lower):
        return jax.tree.map(
            lambda later, earlier: jnp.where(is_first, earlier, later), upper, lower
        )

    incoming = jnp.zeros(block_input.shape[1:], jnp.bfloat16)
    records = []
    kept_saved = []
    forward_rows = []
    for step_index in range(micro_count + 1):
        own_rows = block_input[min(step_index, micro_count - 1)]
        source = jnp.where(is_first, own_rows, incoming)
        crop_rows = jnp.where(
            is_first, crop_ids[min(step_index, micro_count - 1)], crop_ids[max(step_index - 1, 0)]
        )
        saved = forward_layer(source.astype(jnp.float32), crop_rows, weights)
        sent_rows = saved[-1].astype(jnp.bfloat16)
        forward_rows.append(sent_rows)
        records.append((source, crop_rows))
        kept_saved.append(saved)
        if step_index < micro_count:
            incoming = passed_along(sent_rows, "section", 1)
    layer_outputs = jnp.where(
        is_first, jnp.stack(forward_rows[:micro_count]), jnp.stack(forward_rows[1:])
    )
    totals = jax.tree.map(lambda item: jnp.zeros(item.shape, jnp.float32), weights)
    back_in = jnp.zeros(block_input.shape[1:], jnp.bfloat16)
    backward_rows = []
    for step_index in range(micro_count + 1):
        late_tick = min(step_index + 1, micro_count)
        early_tick = max(step_index - 1, 0)
        source, crop_rows = pick(records[late_tick], records[early_tick])
        saved = pick(kept_saved[late_tick], kept_saved[early_tick])
        if step_index < micro_count:
            last_grad = out_grad[step_index]
        else:
            last_grad = jnp.zeros_like(out_grad[0])
        cotangent = jnp.where(is_first, back_in, last_grad)
        grad_hidden, feed_grads = backward_feed(cotangent.astype(jnp.float32), saved, weights)
        feed_totals = tuple((left + right for left, right in zip(totals[5:], feed_grads)))
        grad_in, attend_grads = backward_attend(grad_hidden, saved, crop_rows, weights)
        attend_totals = tuple((left + right for left, right in zip(totals[:5], attend_grads)))
        totals = attend_totals + feed_totals
        sent_grad = grad_in.astype(jnp.bfloat16)
        backward_rows.append(sent_grad)
        if step_index < micro_count:
            back_in = passed_along(sent_grad, "section", -1)
    input_grads = jnp.where(
        is_first, jnp.stack(backward_rows[1:]), jnp.stack(backward_rows[:micro_count])
    )
    summed = lax.psum_scatter(totals, "dp", scatter_dimension=0, tiled=True)
    outputs = tuple((item[None] for item in summed))
    return (layer_outputs[None], input_grads[None]) + outputs


MESH = pl.DeviceIdType.MESH
F = jnp.float32
B = jnp.bfloat16
VECTORS = ("g1", "s1", "bo", "g2", "s2", "bd", "bu")
PARTS = (
    (4, 0, 16, False),
    (0, 0, 32, False), (0, 32, 32, True),
    (1, 0, 64, False),
    (2, 0, 32, False), (2, 32, 32, True),
    (3, 0, 128, False), (3, 128, 128, True),
)
AHEAD = 4
SUMS = (
    (3, 0, 128, False), (3, 128, 128, True),
    (2, 0, 32, False), (2, 32, 32, True),
    (1, 0, 64, False),
    (0, 0, 32, False), (0, 32, 32, True),
    (4, 0, 16, False),
)
A, O, C, G, DM, DU, DB, DQKV = range(8)


def nt(left, right):
    return lax.dot_general(left, right, (((1,), (1,)), ((), ())), preferred_element_type=F)


def tn(left, right):
    return lax.dot_general(left, right, (((0,), (0,)), ((), ())), preferred_element_type=F)


def nn(left, right):
    return jnp.dot(left, right, preferred_element_type=F)


def tiles(total, step):
    def run(body):
        @pl.loop(0, total // step)
        def _(i):
            body(pl.ds(pl.multiple_of(i * step, step), step))

    return run


def normed(values):
    centred = values - jnp.mean(values, axis=-1, keepdims=True)
    scale = lax.rsqrt(jnp.mean(centred * centred, axis=-1, keepdims=True) + 1e-6)
    return centred * scale, scale


def norm_into(out, rows, gain, shift):
    @tiles(rows.shape[0], 64)
    def _(r):
        hat, _ = normed(rows[r, :].astype(F))
        out[r, :] = (hat * gain[...] + shift[...]).astype(B)


def norm_back(rows, grad, base, out, gain, gain_sum, shift_sum):
    @tiles(rows.shape[0], 64)
    def _(r):
        hat, scale = normed(rows[r, :].astype(F))
        d = grad[r, :]
        gain_sum[...] += jnp.sum(d * hat, axis=0, keepdims=True)
        shift_sum[...] += jnp.sum(d, axis=0, keepdims=True)
        d = d * gain[...]
        mean = jnp.mean(d, axis=-1, keepdims=True)
        along = jnp.mean(d * hat, axis=-1, keepdims=True)
        out[r, :] = (base[r, :].astype(F) + scale * (d - mean - hat * along)).astype(out.dtype)


def halves(pair):
    low = lax.broadcasted_iota(jnp.int32, pair.shape, 1) < HEAD
    zero = jnp.zeros_like(pair)
    return jnp.where(low, pair, zero), jnp.where(low, zero, pair)


def head_pairs(qkv, group, many):
    width = qkv.shape[1] // 3
    for i in range(many):
        for t in range(qkv.shape[0] // 128):
            cols = [pl.ds(pl.multiple_of(g * width + (group * many + i) * 128, 128), 128) for g in range(3)]
            yield pl.ds(t * 128, 128), cols


def softmaxes(items, bias):
    scores = [nt(qh, k) + bias[r, :] for r, q, k in items for qh in halves(q)]
    peaks = [jnp.max(s, axis=-1, keepdims=True) for s in scores]
    raised = [jnp.exp(s - m) for s, m in zip(scores, peaks)]
    totals = [1.0 / jnp.sum(e, axis=-1, keepdims=True) for e in raised]
    return [e * t for e, t in zip(raised, totals)]


def attend(qkv, mixed, bias):
    many = 1024 // qkv.shape[0]

    @pl.loop(0, qkv.shape[1] // 384 // many)
    def _(group):
        where = list(head_pairs(qkv, group, many))
        q, k, v = ([qkv[r, cols[g]] for r, cols in where] for g in range(3))
        q = [item * jnp.asarray(HEAD**-0.5, B) for item in q]
        probs = [p.astype(B) for p in softmaxes([(r, a, b) for (r, _), a, b in zip(where, q, k)], bias)]
        for n, (r, cols) in enumerate(where):
            low, high = halves(v[n])
            mixed[r, cols[0]] = (nn(probs[2 * n], low) + nn(probs[2 * n + 1], high)).astype(B)


def attend_back(qkv, grad, bias):
    many = 1024 // qkv.shape[0]

    def joined(items, axis):
        return jnp.concatenate(items, axis)

    @pl.loop(0, qkv.shape[1] // 384 // many)
    def _(group):
        where = list(head_pairs(qkv, group, many))
        q, k, v = ([qkv[r, cols[g]] for r, cols in where] for g in range(3))
        q = [item * jnp.asarray(HEAD**-0.5, B) for item in q]
        d = [grad[r, cols[0]] for r, cols in where]
        probs = softmaxes([(r, a, b) for (r, _), a, b in zip(where, q, k)], bias)
        slopes = [nt(dh, v[n]) for n in range(len(where)) for dh in halves(d[n])]
        centres = [jnp.sum(g * p, axis=-1, keepdims=True) for g, p in zip(slopes, probs)]
        slopes = [(p * (g - c)).astype(B) for p, g, c in zip(probs, slopes, centres)]
        probs = [p.astype(B) for p in probs]
        for n, (r, cols) in enumerate(where):
            pair = slice(2 * n, 2 * n + 2)
            grad_q = nn(joined(slopes[pair], 1), joined(halves(k[n]), 0))
            qkv[r, cols[0]] = (grad_q * HEAD**-0.5).astype(B)
            qkv[r, cols[1]] = tn(joined(slopes[pair], 0), joined(halves(q[n]), 0)).astype(B)
            qkv[r, cols[2]] = tn(joined(probs[pair], 0), joined(halves(d[n]), 0)).astype(B)


def relay(names, *refs):
    ref = dict(zip(names, refs))
    width = ref["x_own"].shape[1]
    rows = ref["x_own"].shape[0]
    ff = ref["w2"].shape[1]
    shard = [ref[f"own{j}"] for j in range(5)]
    full = [ref[f"w{j}"] for j in range(5)]
    both = [ref[n] for n in ("a", "o", "c", "g", "dm", "du", "db", "dqkv")]
    mine = [b.at[pl.ds(0, 2 * rows)] for b in both]
    theirs = [b.at[pl.ds(2 * rows, 2 * rows)] for b in both]
    vec = {n: ref["v_" + n] for n in VECTORS}
    vsum = {n: ref["d_" + n] for n in VECTORS}
    x, hidden, wide, dmixed, result = (ref[n] for n in ("x", "h", "wide", "do", "y"))
    for name in ("g1", "s1", "g2", "s2"):
        vsum[name][...] = jnp.zeros_like(vsum[name])
    p = lax.axis_index("dp")
    z, y, core = p // 4, (p // 2) % 2, p % 2
    inner = jnp.logical_or(z == 1, z == 2)
    section = lax.axis_index("section")
    zo, zn = jnp.where(z == 1, 0, 3), 3 - z
    zon = 3 - zo
    zi = jnp.where(z == 0, 1, 2)

    def idx(z, y, core):
        return (z * 2 + y) * 2 + core

    sibling, across, other = idx(z, y, 1 - core), idx(z, 1 - y, core), idx(zn, y, core)
    outer_one, inner_one = idx(zo, y, core), idx(zi, y, core)

    def remote(sec, src, dst, send_sem, recv_sem, to):
        return pltpu.make_async_remote_copy(
            src_ref=src, dst_ref=dst, send_sem=send_sem, recv_sem=recv_sem,
            device_id=(sec, to), device_id_type=MESH,
        )

    class Flow:
        def __init__(self, sec):
            self.sec = sec
            self.sent = []

        def send(self, *args, sec=None):
            copy = remote(self.sec if sec is None else sec, *args)
            copy.start()
            self.sent.append(copy)

        def arrived(self, dst, recv_sem):
            remote(self.sec, dst, dst, ref["idle_sem"].at[0], recv_sem, sibling).wait_recv()

        def finish(self):
            for copy in self.sent:
                copy.wait_send()
            self.sent = []

    def piece(k, b):
        j, first, count, _ = PARTS[k]
        size = shard[j].shape[0]
        return full[j].at[pl.ds(pl.multiple_of(b * size + first, count), count)]

    def own_piece(k):
        j, first, count, _ = PARTS[k]
        return shard[j].at[pl.ds(first, count)]

    def own_copy(k):
        return pltpu.make_async_copy(own_piece(k), piece(k, p), ref["ag_local"].at[k])

    def gather_steps(flow, is_inner):
        used = [0] * len(PARTS)

        def send(k, b, to, own=False):
            src = own_piece(k) if own else piece(k, b)
            flow.send(src, piece(k, b), ref["ag_send"].at[k, used[k]], ref["ag_recv"].at[k, b], to)
            used[k] += 1

        def take(k, b, *to):
            flow.arrived(piece(k, b), ref["ag_recv"].at[k, b])
            for target in to:
                send(k, b, target)

        def begin(k):
            if is_inner:
                for to in (across, other, sibling):
                    send(k, p, to, own=True)
                own_copy(k).start()
            else:
                send(k, p, inner_one, own=True)
                send(k, p, across, own=True)

        def early(k):
            if not is_inner:
                take(k, across, inner_one)
                return
            take(k, idx(zo, y, core), other, sibling)
            take(k, idx(zn, y, core), across, sibling)
            take(k, idx(z, 1 - y, core), sibling)

        def late(k):
            by_z = PARTS[k][3]
            take(k, idx(zon, y, core), *((sibling,) if by_z else (across, sibling)))
            take(k, idx(zo, 1 - y, core), *((other, sibling) if by_z else (sibling,)))

        def end(k):
            take(k, idx(zn, 1 - y, core), sibling)
            take(k, idx(zon, 1 - y, core), sibling)

        def step(k):
            if k == 0:
                for first in range(AHEAD):
                    begin(first)
            if k + AHEAD < len(PARTS):
                begin(k + AHEAD)
            if k < len(PARTS):
                early(k)
            if is_inner:
                if 0 <= k - 1 < len(PARTS):
                    late(k - 1)
                if 0 <= k - 2 < len(PARTS):
                    end(k - 2)

        return step

    def gathered(flow, j):
        for k, part in enumerate(PARTS):
            if part[0] == j:
                own_copy(k).wait()
                for b in range(8):
                    block = 2 * b + 1 - core
                    flow.arrived(piece(k, block), ref["ag_recv"].at[k, block])

    def write_small():
        stage = ref["stage"]
        stage[...] = jnp.zeros_like(stage)
        for c in range(2):
            @pl.when(core == c)
            def _():
                for n, name in enumerate(VECTORS[:6]):
                    stage[n : n + 1, 64 * c : 64 * c + 64] = ref["in_" + name][...].astype(F)
        for n in range(2):
            stage[6 + n : 7 + n, :] = ref["in_bu"][:, 128 * n : 128 * n + 128].astype(F)
        shard[4][...] = stage[...].astype(B)

    def write_crops():
        for m in range(2):
            ref["crops"][0:1, 64 * m : 64 * m + 64] = (ref["in_crop"][m : m + 1, :] + 1024 * m).astype(F)

    def write_bias(crops, first):
        along = jnp.broadcast_to(crops[0:1, :], (rows, rows))
        ref["bias"][pl.ds(first, rows), :] = jnp.where(along == along.T, 0.0, -1e30)

    def spread_vectors():
        for i in range(8):
            low = full[4][pl.ds(32 * i, 16), :].astype(F)
            high = full[4][pl.ds(32 * i + 16, 16), :].astype(F)
            joined = low + high
            for n, name in enumerate(VECTORS[:6]):
                vec[name][:, pl.ds(128 * i, 128)] = joined[n : n + 1]
            for n, part in enumerate((low[6:7], low[7:8], high[6:7], high[7:8])):
                vec["bu"][:, pl.ds(512 * i + 128 * n, 128)] = part

    def exchange(flow, which):
        flow.send(mine[which], theirs[which], ref["act_send"].at[which], ref["act_recv"].at[which], sibling)

    def exchanged(flow, *which):
        for w in which:
            flow.arrived(theirs[w], ref["act_recv"].at[w])

    def forward_attend(r):
        norm_into(mine[A].at[r], x.at[r], vec["g1"], vec["s1"])

        @tiles(3 * width, 1536)
        def _(c):
            mine[DQKV][r, c] = nn(mine[A][r, :], full[0][:, c]).astype(B)

        attend(mine[DQKV].at[r], mine[O].at[r], ref["bias"].at[r])

    def forward_out():
        hidden[...] = x[...].astype(F) + nn(mine[O][...], full[1][...]) + vec["bo"][...]
        norm_into(mine[C], hidden, vec["g2"], vec["s2"])

    def forward_up():
        @tiles(ff, 1024)
        def _(c):
            u = nn(mine[C][...], full[2][:, c]) + vec["bu"][:, c]
            phi = 0.5 + 0.5 * lax.erf(u * 0.5**0.5)
            mine[G][:, c] = (u * phi).astype(B)
            mine[DU][:, c] = (phi + u * (jnp.exp(-0.5 * u * u) * (0.5 / jnp.pi) ** 0.5)).astype(B)

    def forward_down(r):
        result[r, :] = (hidden[r, :] + nn(mine[G][r, :], full[3][...]) + vec["bd"][...]).astype(B)

    def backward_du():
        vsum["bd"][...] = jnp.sum(mine[DM][...].astype(F), axis=0, keepdims=True)

        @tiles(ff, 1024)
        def _(c):
            du = (nt(mine[DM][...], full[3][c, :]) * mine[DU][:, c].astype(F)).astype(B)
            mine[DU][:, c] = du
            vsum["bu"][:, c] = jnp.sum(du.astype(F), axis=0, keepdims=True)

    def backward_dh():
        wide[...] = nt(mine[DU][...], full[2][...])
        norm_back(hidden, wide, mine[DM], hidden, vec["g2"], vsum["g2"], vsum["s2"])
        mine[DB][...] = hidden[...].astype(B)
        vsum["bo"][...] = jnp.sum(mine[DB][...].astype(F), axis=0, keepdims=True)

    def backward_attend():
        dmixed[...] = nt(mine[DB][...], full[1][...]).astype(B)
        attend_back(mine[DQKV], dmixed, ref["bias"])

    def backward_da():
        wide[...] = nt(mine[DQKV][...], full[0][...])

    def backward_dx(r):
        norm_back(x.at[r], wide.at[r], hidden.at[r], x.at[r], vec["g1"], vsum["g1"], vsum["s1"])

    def packed(which):
        src, out = both[which], ref["packed"]
        for i in range(width // 256):
            first = src[:, pl.ds(256 * i, 128)].astype(F)
            second = src[:, pl.ds(256 * i + 128, 128)].astype(F)
            low = lax.broadcasted_iota(jnp.int32, first.shape, 1) < HEAD
            even = jnp.where(low, first, pltpu.roll(second, HEAD, 1))
            odd = jnp.where(low, pltpu.roll(first, HEAD, 1), second)
            out[pl.ds(128 * i, 128), :] = jnp.where(core == 0, even, odd).T.astype(B)

    def grad_down():
        size = shard[3].shape[0]
        for o in range(8):
            c = pl.ds(pl.multiple_of(size * (2 * o + core), size), size)
            full[3][pl.ds(size * o, size), :] = tn(both[G][:, c], both[DM][...]).astype(B)

    def grad_of(j, left, right):
        packed(left)

        @tiles(both[right].shape[1], 512)
        def _(c):
            full[j][pl.ds(0, 8 * shard[j].shape[0]), c] = nn(ref["packed"][...], both[right][:, c]).astype(B)

    def grad_vectors():
        for o in range(8):
            for n, name in enumerate(VECTORS[:6]):
                ref["vp"][pl.ds(16 * o + n, 1), :] = vsum[name][:, pl.ds(128 * o, 128)]
            for n in range(4):
                ref["vp"][pl.ds(16 * o + 6 + n, 1), :] = vsum["bu"][:, pl.ds(512 * o + 128 * n, 128)]
            ref["vp"][pl.ds(16 * o + 10, 6), :] = jnp.zeros((6, 128), F)

    partial = [full[0], full[1], full[2], full[3], ref["vp"]]
    sums = [ref[f"out{j}"] for j in range(4)] + [ref["vs"]]
    NEAR, OWN, ALT, INNER, OUTER = range(5)
    slots = [[ref[f"r{s}_{j}"] for j in range(5)] for s in range(5)]

    def reducer(flow):
        def slot(s, k):
            j, first, count, _ = SUMS[k]
            return slots[s][j].at[pl.ds(first, count)]

        def part(k, zz, yy):
            j, first, count, _ = SUMS[k]
            size = partial[j].shape[0] // 8 if j == 4 else shard[j].shape[0]
            return partial[j].at[pl.ds(pl.multiple_of((zz * 2 + yy) * size + first, count), count)]

        def send(k, n, src, s, to):
            flow.send(src, slot(s, k), ref["rs_send"].at[k, n], ref["rs_recv"].at[k, s], to)

        def arrived(k, s):
            flow.arrived(slot(s, k), ref["rs_recv"].at[k, s])

        def add(k, dst, *more):
            total = dst[...].astype(F)
            for s in more:
                total = total + slot(s, k)[...].astype(F)
            return total

        def issue(k):
            if SUMS[k][3]:
                send(k, 4, part(k, zon, y), OUTER, other)
                send(k, 1, part(k, zon, 1 - y), ALT, other)
            else:
                send(k, 1, part(k, zon, 1 - y), ALT, across)
                send(k, 6, part(k, zo, 1 - y), INNER, outer_one)
            send(k, 0, part(k, zn, 1 - y), NEAR, across)

        def issue_own(k):
            send(k, 2, part(k, z, 1 - y), OWN, across)

        def middle(k):
            if not SUMS[k][3]:
                dst = part(k, zon, y)
                arrived(k, ALT)
                dst[...] = add(k, dst, ALT).astype(dst.dtype)
                send(k, 4, dst, OUTER, other)
            dst = part(k, zn, y)
            arrived(k, NEAR)
            dst[...] = add(k, dst, NEAR).astype(dst.dtype)
            send(k, 3, dst, INNER, other)

        def outward(k):
            dst = part(k, zo, y)
            arrived(k, OUTER)
            dst[...] = add(k, dst, OUTER).astype(dst.dtype)
            send(k, 5, dst, OUTER, outer_one)
            if SUMS[k][3]:
                dst = part(k, zo, 1 - y)
                arrived(k, ALT)
                dst[...] = add(k, dst, ALT).astype(dst.dtype)
                send(k, 6, dst, INNER, outer_one)

        def last(k):
            arrived(k, INNER)
            arrived(k, OWN)
            j, first, count, _ = SUMS[k]
            sums[j][pl.ds(first, count), :] = add(k, part(k, z, y), OWN, INNER)

        def pass_on(k):
            arrived(k, INNER)
            send(k, 0, slot(INNER, k), OWN, across)

        def collect(k):
            arrived(k, OUTER)
            arrived(k, OWN)
            j, first, count, _ = SUMS[k]
            sums[j][pl.ds(first, count), :] = slot(OUTER, k)[...].astype(F) + slot(OWN, k)[...].astype(F)

        def join_vectors():
            flow.send(ref["vs"], ref["vt"], ref["vec_sem"].at[0], ref["vec_sem"].at[1], sibling)
            flow.arrived(ref["vt"], ref["vec_sem"].at[1])
            ref["out4"][...] = ref["vs"][...] + ref["vt"][...]

        return issue, issue_own, middle, outward, last, pass_on, collect, join_vectors

    def hand_out(flow, src, out, n):
        flow.send(src.at[pl.ds(rows, rows)], out, ref["res_send"].at[n], ref["res_recv"].at[n], outer_one)
        out[...] = src[pl.ds(0, rows), :]

    every = pl.ds(0, 2 * rows)
    near, far = pl.ds(0, rows), pl.ds(rows, rows)

    def inner_program(sec):
        flow = Flow(sec)
        step = gather_steps(flow, True)
        issue, issue_own, middle, outward, last, _, _, join_vectors = reducer(flow)
        step(0)
        src, dst = (ref["x_own"], x) if sec == 0 else (ref["dy_own"], mine[DM])
        own = pltpu.make_async_copy(src, dst.at[near], ref["tok_local"].at[0])
        own.start()
        write_bias(ref["crops"], 0)

        def tokens():
            own.wait()
            flow.arrived(ref["far_crops"], ref["tok_recv"].at[0])
            flow.arrived(dst.at[far], ref["tok_recv"].at[1])
            write_bias(ref["far_crops"], rows)

        def steps(first, end):
            for k in range(first, end):
                step(k)

        if sec == 0:
            steps(1, 6)
            gathered(flow, 4)
            spread_vectors()
            tokens()
            gathered(flow, 0)
            forward_attend(every)
            steps(6, 7)
            gathered(flow, 1)
            forward_out()
            steps(7, 9)
            gathered(flow, 2)
            forward_up()
            steps(9, len(PARTS) + 2)
            gathered(flow, 3)
            for n, r in enumerate((near, far)):
                forward_down(r)
                flow.send(result.at[r], x.at[r], ref["x_send"].at[n], ref["x_recv"].at[n], p, sec=1)
        else:
            steps(1, len(PARTS) + 2)
            for j in range(5):
                gathered(flow, j)
            spread_vectors()
            tokens()
            flow.finish()
            exchange(flow, DM)
            for n, r in enumerate((near, far)):
                flow.arrived(x.at[r], ref["x_recv"].at[n])
                forward_attend(r)
            forward_out()
            forward_up()
            forward_down(every)
        for which in (G, C, O, A):
            exchange(flow, which)
        hand_out(flow, result, ref["y_out"], 0)
        if sec == 0:
            flow.finish()
            for n, r in enumerate((near, far)):
                flow.arrived(mine[DM].at[r], ref["x_recv"].at[2 + n])
            exchange(flow, DM)
            backward_du()
            exchange(flow, DU)
            exchanged(flow, G, DM)
            grad_down()
            issue(0)
            issue(1)
            backward_dh()
            exchange(flow, DB)
            exchanged(flow, C, DU)
            grad_of(2, C, DU)
            issue(2)
            issue(3)
            backward_attend()
            exchange(flow, DQKV)
            middle(0)
            exchanged(flow, O, DB)
            grad_of(1, O, DB)
            issue(4)
            backward_da()
            exchanged(flow, A, DQKV)
            grad_of(0, A, DQKV)
            issue(5)
            issue(6)
            backward_dx(every)
            grad_vectors()
            issue(7)
        else:
            backward_du()
            backward_dh()
            backward_attend()
            backward_da()
            for n, r in enumerate((near, far)):
                backward_dx(r)
                flow.send(x.at[r], mine[DM].at[r], ref["x_send"].at[2 + n], ref["x_recv"].at[2 + n], p, sec=0)
            for which in (DU, DB, DQKV):
                exchange(flow, which)
            exchanged(flow, G, DM)
            grad_down()
            issue(0)
            issue(1)
            exchanged(flow, C, DU)
            grad_of(2, C, DU)
            issue(2)
            issue(3)
            exchanged(flow, O, DB)
            grad_of(1, O, DB)
            issue(4)
            exchanged(flow, A, DQKV)
            grad_of(0, A, DQKV)
            issue(5)
            issue(6)
            grad_vectors()
            issue(7)
            middle(0)
        hand_out(flow, x, ref["dx_out"], 1)
        count = len(SUMS)
        own_next = 0
        for k in range(1, count + 2):
            if k < count:
                middle(k)
            while own_next < min(count, 2 * (k - 3)):
                issue_own(own_next)
                own_next += 1
            if 0 <= k - 2 < count:
                outward(k - 2)
        for k in range(count):
            last(k)
        join_vectors()
        flow.finish()

    def outer_program(sec):
        flow = Flow(sec)
        step = gather_steps(flow, False)
        pass_on, collect, join_vectors = reducer(flow)[-3:]
        src, dst = (ref["x_own"], x) if sec == 0 else (ref["dy_own"], mine[DM])
        for k in range(len(PARTS)):
            step(k)
            if k == (1 if sec == 0 else 7):
                flow.send(ref["crops"], ref["far_crops"], ref["tok_send"].at[0], ref["tok_recv"].at[0], inner_one)
                flow.send(src, dst.at[far], ref["tok_send"].at[1], ref["tok_recv"].at[1], inner_one)
        for k in range(len(SUMS)):
            pass_on(k)
            if k:
                collect(k - 1)
        collect(len(SUMS) - 1)
        join_vectors()
        flow.arrived(ref["y_out"], ref["res_recv"].at[0])
        flow.arrived(ref["dx_out"], ref["res_recv"].at[1])
        flow.finish()

    write_small()
    write_crops()
    for sec in range(2):
        pl.when(jnp.logical_and(inner, section == sec))(lambda sec=sec: inner_program(sec))
        pl.when(jnp.logical_and(jnp.logical_not(inner), section == sec))(lambda sec=sec: outer_program(sec))


def relay_call(x_own, dy_own, small, shards, dp):
    rows, width = x_own.shape
    ff = shards[2].shape[1]
    count = 2 * rows
    shapes = [item.shape for item in shards] + [(16, 128)]
    inputs = {"x_own": x_own, "dy_own": dy_own}
    inputs.update({f"own{j}": item for j, item in enumerate(shards)})
    outputs = {"y_out": ((rows, width), B), "dx_out": ((rows, width), B)}
    outputs.update({f"out{j}": (item.shape, F) for j, item in enumerate(shards)})
    outputs["out4"] = ((16, 128), F)
    scratch = {f"w{j}": ((dp * shape[0], shape[1]), B) for j, shape in enumerate(shapes)}
    for name, cols in zip(("a", "o", "c", "g", "dm", "du", "db", "dqkv"), (1, 1, 1, 0, 1, 0, 1, 3)):
        scratch[name] = ((2 * count, cols * width or ff), B)
    scratch.update(x=((count, width), B), h=((count, width), F), wide=((count, width), F), do=((count, width), B))
    scratch.update(y=((count, width), B), bias=((count, 128), F), packed=((width // 2, 2 * count), B))
    for name in VECTORS:
        scratch["v_" + name] = scratch["d_" + name] = ((1, ff if name == "bu" else width), F)
    scratch.update(vp=((128, 128), F), vs=((16, 128), F), vt=((16, 128), F), stage=((16, 128), F), crops=((8, 128), F), far_crops=((8, 128), F), own4=((16, 128), B))
    for s in range(5):
        for j, shape in enumerate(shapes):
            scratch[f"r{s}_{j}"] = (shape, F if j == 4 else B)
    sems = dict(
        ag_send=(len(PARTS), 16), ag_recv=(len(PARTS), dp), ag_local=(len(PARTS),), tok_local=(1,), tok_send=(2,),
        tok_recv=(2,), x_send=(4,), x_recv=(4,), act_send=(8,), act_recv=(8,), res_send=(2,), res_recv=(2,),
        rs_send=(len(SUMS), 7), rs_recv=(len(SUMS), 5), vec_sem=(2,), idle_sem=(1,),
    )
    names = [*inputs, *small, *outputs, *scratch, *sems]
    whole, anywhere = pl.BlockSpec(memory_space=pltpu.VMEM), pl.BlockSpec(memory_space=pl.ANY)
    return pl.pallas_call(
        functools.partial(relay, names),
        out_shape=[jax.ShapeDtypeStruct(*item) for item in outputs.values()],
        in_specs=[anywhere] * len(inputs) + [whole] * len(small),
        out_specs=[whole] * len(outputs),
        scratch_shapes=[pltpu.VMEM(*item) for item in scratch.values()]
        + [pltpu.SemaphoreType.DMA(item) for item in sems.values()],
        compiler_params=pltpu.CompilerParams(has_side_effects=True, vmem_limit_bytes=62 << 20),
        name="relay",
    )(*inputs.values(), *small.values())


def hand_over(*refs):
    rows, vectors, out, small = refs[:6], refs[6], refs[7:13], refs[13:20]
    for n in range(2):
        size = out[n].shape[2]
        for m in range(out[n].shape[1]):
            out[n][0, m] = rows[n][pl.ds(m * size, size), :]
    for n in range(2, 6):
        out[n][0] = rows[n][...]
    core = lax.axis_index("dp") % 2
    for c in range(2):
        @pl.when(core == c)
        def _():
            for n in range(6):
                small[n][...] = vectors[n : n + 1, 64 * c : 64 * c + 64]
            for n in range(2):
                small[6][:, 128 * n : 128 * n + 128] = vectors[6 + 2 * c + n : 7 + 2 * c + n, :]


def middle(
    block_input, crop_ids, out_grad, norm1_gain, norm1_shift, w_qkv, w_out, b_out,
    norm2_gain, norm2_shift, w_up, b_up, w_down, b_down,
):
    micro, rows, width = block_input.shape
    small = dict(zip(VECTORS, (norm1_gain, norm1_shift, b_out, norm2_gain, norm2_shift, b_down, b_up)))
    small = {"in_" + name: item for name, item in small.items()} | {"in_crop": crop_ids}
    got = relay_call(
        block_input.reshape(-1, width), out_grad.reshape(-1, width), small,
        (w_qkv[0], w_out[0], w_up[0], w_down[0]), lax.axis_size("dp"),
    )
    whole = pl.BlockSpec(memory_space=pltpu.VMEM)
    shapes = [((1, micro, rows, width), B)] * 2 + [((1,) + item.shape, F) for item in got[2:6]]
    shapes += [((1, 64), F)] * 6 + [((1, 256), F)]
    y, dx, g_qkv, g_out, g_up, g_down, g1, s1, bo, g2, s2, bd, bu = pl.pallas_call(
        hand_over,
        out_shape=[jax.ShapeDtypeStruct(*item) for item in shapes],
        in_specs=[whole] * 7,
        out_specs=[whole] * 13,
        compiler_params=pltpu.CompilerParams(vmem_limit_bytes=62 << 20),
        name="hand_over",
    )(*got)
    return y, dx, g1, s1, g_qkv, g_out, bo, g2, s2, g_up, bu, g_down, bd


def solution(mesh):
    in_specs = (
        P(None, "dp", None),
        P(None, "dp"),
        P(None, "dp", None),
        P("section", "dp"),
        P("section", "dp"),
        P("section", "dp", None),
        P("section", "dp", None),
        P("section", "dp"),
        P("section", "dp"),
        P("section", "dp"),
        P("section", "dp", None),
        P("section", "dp"),
        P("section", "dp", None),
        P("section", "dp"),
    )
    out_specs = (
        P("section", None, "dp", None),
        P("section", None, "dp", None),
        P("section", "dp"),
        P("section", "dp"),
        P("section", "dp", None),
        P("section", "dp", None),
        P("section", "dp"),
        P("section", "dp"),
        P("section", "dp"),
        P("section", "dp", None),
        P("section", "dp"),
        P("section", "dp", None),
        P("section", "dp"),
    )
    fits = mesh.shape["dp"] == 16 and mesh.shape["section"] == 2
    return jax.shard_map(middle if fits else local, mesh=mesh, in_specs=in_specs, out_specs=out_specs, check_vma=False)
```

```python
import functools

import jax
import jax.numpy as jnp
from jax import lax
from jax.experimental import pallas as pl
from jax.experimental.pallas import tpu as pltpu
from jax.sharding import PartitionSpec as P

HEAD = 64


def passed_along(x, axis, by):
    devices = lax.axis_size(axis)
    pairs = [(i, i + by) for i in range(devices) if 0 <= i + by < devices]
    return lax.ppermute(x, axis, pairs)


def norm_rows(values, gain, shift):
    centred = values - jnp.mean(values, axis=-1, keepdims=True)
    spread = jnp.mean(centred * centred, axis=-1, keepdims=True)
    return centred * lax.rsqrt(spread + 1e-06) * gain + shift


def gelu_exact(values):
    return jax.nn.gelu(values, approximate=False)


def inner_rows(left, right):
    return lax.dot_general(
        left, right, (((0,), (0,)), ((), ())), preferred_element_type=jnp.float32
    )


def times_transpose(left, right):
    return lax.dot_general(
        left, right, (((1,), (1,)), ((), ())), preferred_element_type=jnp.float32
    )


def split_heads(qkv_rows):
    model_width = qkv_rows.shape[1] // 3
    head_count = model_width // HEAD
    queries = qkv_rows[:, :model_width].reshape(-1, head_count, HEAD)
    key_rows = qkv_rows[:, model_width : 2 * model_width].reshape(-1, head_count, HEAD)
    value_rows = qkv_rows[:, 2 * model_width :].reshape(-1, head_count, HEAD)
    return (queries, key_rows, value_rows)


def head_scores(qkv_rows, crop_rows):
    queries, key_rows, value_rows = split_heads(qkv_rows)
    scores = jnp.einsum("qhd,khd->hqk", queries, key_rows, preferred_element_type=jnp.float32)
    scores = scores * HEAD ** (-0.5)
    same_crop = crop_rows[:, None] == crop_rows[None, :]
    return jnp.where(same_crop[None], scores, -1e30)


def forward_layer(layer_in, crop_rows, weights):
    gain_one, shift_one, w_qkv, w_out, b_out, gain_two, shift_two, w_up, b_up, w_down, b_down = (
        weights
    )
    row_count = layer_in.shape[0]
    normed = norm_rows(
        layer_in, gain_one.astype(jnp.float32), shift_one.astype(jnp.float32)
    ).astype(jnp.bfloat16)
    qkv_rows = jnp.dot(normed, w_qkv, preferred_element_type=jnp.float32).astype(jnp.bfloat16)
    scores = head_scores(qkv_rows, crop_rows)
    row_peak = jnp.max(scores, axis=-1, keepdims=True)
    log_total = row_peak + jnp.log(jnp.sum(jnp.exp(scores - row_peak), axis=-1, keepdims=True))
    softmax_low = jnp.exp(scores - log_total).astype(jnp.bfloat16)
    queries, key_rows, value_rows = split_heads(qkv_rows)
    mixed_heads = jnp.einsum(
        "hqk,khd->qhd", softmax_low, value_rows, preferred_element_type=jnp.float32
    )
    mixed_heads = mixed_heads.reshape(row_count, -1).astype(jnp.bfloat16)
    hidden = (
        layer_in
        + jnp.dot(mixed_heads, w_out, preferred_element_type=jnp.float32)
        + b_out.astype(jnp.float32)
    )
    squeezed = norm_rows(
        hidden, gain_two.astype(jnp.float32), shift_two.astype(jnp.float32)
    ).astype(jnp.bfloat16)
    up_rows = jnp.dot(squeezed, w_up, preferred_element_type=jnp.float32) + b_up.astype(jnp.float32)
    active = gelu_exact(up_rows).astype(jnp.bfloat16)
    result = (
        hidden
        + jnp.dot(active, w_down, preferred_element_type=jnp.float32)
        + b_down.astype(jnp.float32)
    )
    return (
        layer_in,
        normed,
        qkv_rows,
        log_total,
        mixed_heads,
        hidden,
        squeezed,
        up_rows,
        active,
        result,
    )


def backward_feed(grad_result, saved, weights):
    gain_one, shift_one, w_qkv, w_out, b_out, gain_two, shift_two, w_up, b_up, w_down, b_down = (
        weights
    )
    (
        layer_in,
        normed,
        qkv_rows,
        log_total,
        mixed_heads,
        hidden,
        squeezed,
        up_rows,
        active,
        result,
    ) = saved
    grad_branch = grad_result.astype(jnp.bfloat16)
    grad_w_down = inner_rows(active, grad_branch)
    grad_b_down = jnp.sum(grad_branch.astype(jnp.float32), axis=0)
    grad_active = times_transpose(grad_branch, w_down)
    gelu_value, gelu_pull = jax.vjp(gelu_exact, up_rows)
    grad_up = gelu_pull(grad_active)[0].astype(jnp.bfloat16)
    grad_w_up = inner_rows(squeezed, grad_up)
    grad_b_up = jnp.sum(grad_up.astype(jnp.float32), axis=0)
    grad_squeezed = times_transpose(grad_up, w_up)
    norm_value, norm_pull = jax.vjp(
        norm_rows, hidden, gain_two.astype(jnp.float32), shift_two.astype(jnp.float32)
    )
    grad_hid, grad_gain_two, grad_shift_two = norm_pull(grad_squeezed)
    grad_hidden = grad_result + grad_hid
    return (
        grad_hidden,
        (grad_gain_two, grad_shift_two, grad_w_up, grad_b_up, grad_w_down, grad_b_down),
    )


def backward_attend(grad_hidden, saved, crop_rows, weights):
    gain_one, shift_one, w_qkv, w_out, b_out, gain_two, shift_two, w_up, b_up, w_down, b_down = (
        weights
    )
    (
        layer_in,
        normed,
        qkv_rows,
        log_total,
        mixed_heads,
        hidden,
        squeezed,
        up_rows,
        active,
        result,
    ) = saved
    row_count = layer_in.shape[0]
    grad_attn = grad_hidden.astype(jnp.bfloat16)
    grad_w_out = inner_rows(mixed_heads, grad_attn)
    grad_b_out = jnp.sum(grad_attn.astype(jnp.float32), axis=0)
    grad_mixed = times_transpose(grad_attn, w_out).astype(jnp.bfloat16)
    queries, key_rows, value_rows = split_heads(qkv_rows)
    grad_mixed = grad_mixed.reshape(queries.shape)
    softmax_out = jnp.exp(head_scores(qkv_rows, crop_rows) - log_total)
    grad_soft = jnp.einsum(
        "qhd,khd->hqk", grad_mixed, value_rows, preferred_element_type=jnp.float32
    )
    grad_values = jnp.einsum(
        "hqk,qhd->khd",
        softmax_out.astype(jnp.bfloat16),
        grad_mixed,
        preferred_element_type=jnp.float32,
    )
    row_centre = jnp.sum(grad_soft * softmax_out, axis=-1, keepdims=True)
    grad_scores = (softmax_out * (grad_soft - row_centre)).astype(jnp.bfloat16)
    grad_queries = jnp.einsum(
        "hqk,khd->qhd", grad_scores, key_rows, preferred_element_type=jnp.float32
    ) * HEAD ** (-0.5)
    grad_keys = jnp.einsum(
        "hqk,qhd->khd", grad_scores, queries, preferred_element_type=jnp.float32
    ) * HEAD ** (-0.5)
    grad_qkv = jnp.concatenate(
        [
            grad_queries.reshape(row_count, -1),
            grad_keys.reshape(row_count, -1),
            grad_values.reshape(row_count, -1),
        ],
        axis=1,
    ).astype(jnp.bfloat16)
    grad_w_qkv = inner_rows(normed, grad_qkv)
    grad_normed = times_transpose(grad_qkv, w_qkv)
    first_value, first_pull = jax.vjp(
        norm_rows, layer_in, gain_one.astype(jnp.float32), shift_one.astype(jnp.float32)
    )
    grad_in, grad_gain_one, grad_shift_one = first_pull(grad_normed)
    return (
        grad_hidden + grad_in,
        (grad_gain_one, grad_shift_one, grad_w_qkv, grad_w_out, grad_b_out),
    )


def local(
    block_input,
    crop_ids,
    out_grad,
    norm1_gain,
    norm1_shift,
    w_qkv,
    w_out,
    b_out,
    norm2_gain,
    norm2_shift,
    w_up,
    b_up,
    w_down,
    b_down,
):
    is_first = lax.axis_index("section") == 0
    shards = (
        norm1_gain,
        norm1_shift,
        w_qkv,
        w_out,
        b_out,
        norm2_gain,
        norm2_shift,
        w_up,
        b_up,
        w_down,
        b_down,
    )
    gathered = (
        lax.all_gather(shards[0], "dp", axis=1, tiled=True),
        lax.all_gather(shards[1], "dp", axis=1, tiled=True),
        lax.all_gather(shards[2], "dp", axis=1, tiled=True),
        lax.all_gather(shards[3], "dp", axis=1, tiled=True),
        lax.all_gather(shards[4], "dp", axis=1, tiled=True),
        lax.all_gather(shards[5], "dp", axis=1, tiled=True),
        lax.all_gather(shards[6], "dp", axis=1, tiled=True),
        lax.all_gather(shards[7], "dp", axis=1, tiled=True),
        lax.all_gather(shards[8], "dp", axis=1, tiled=True),
        lax.all_gather(shards[9], "dp", axis=1, tiled=True),
        lax.all_gather(shards[10], "dp", axis=1, tiled=True),
    )
    weights = tuple((item[0] for item in gathered))
    micro_count = block_input.shape[0]

    def pick(upper, lower):
        return jax.tree.map(
            lambda later, earlier: jnp.where(is_first, earlier, later), upper, lower
        )

    incoming = jnp.zeros(block_input.shape[1:], jnp.bfloat16)
    records = []
    kept_saved = []
    forward_rows = []
    for step_index in range(micro_count + 1):
        own_rows = block_input[min(step_index, micro_count - 1)]
        source = jnp.where(is_first, own_rows, incoming)
        crop_rows = jnp.where(
            is_first, crop_ids[min(step_index, micro_count - 1)], crop_ids[max(step_index - 1, 0)]
        )
        saved = forward_layer(source.astype(jnp.float32), crop_rows, weights)
        sent_rows = saved[-1].astype(jnp.bfloat16)
        forward_rows.append(sent_rows)
        records.append((source, crop_rows))
        kept_saved.append(saved)
        if step_index < micro_count:
            incoming = passed_along(sent_rows, "section", 1)
    layer_outputs = jnp.where(
        is_first, jnp.stack(forward_rows[:micro_count]), jnp.stack(forward_rows[1:])
    )
    totals = jax.tree.map(lambda item: jnp.zeros(item.shape, jnp.float32), weights)
    back_in = jnp.zeros(block_input.shape[1:], jnp.bfloat16)
    backward_rows = []
    for step_index in range(micro_count + 1):
        late_tick = min(step_index + 1, micro_count)
        early_tick = max(step_index - 1, 0)
        source, crop_rows = pick(records[late_tick], records[early_tick])
        saved = pick(kept_saved[late_tick], kept_saved[early_tick])
        if step_index < micro_count:
            last_grad = out_grad[step_index]
        else:
            last_grad = jnp.zeros_like(out_grad[0])
        cotangent = jnp.where(is_first, back_in, last_grad)
        grad_hidden, feed_grads = backward_feed(cotangent.astype(jnp.float32), saved, weights)
        feed_totals = tuple((left + right for left, right in zip(totals[5:], feed_grads)))
        grad_in, attend_grads = backward_attend(grad_hidden, saved, crop_rows, weights)
        attend_totals = tuple((left + right for left, right in zip(totals[:5], attend_grads)))
        totals = attend_totals + feed_totals
        sent_grad = grad_in.astype(jnp.bfloat16)
        backward_rows.append(sent_grad)
        if step_index < micro_count:
            back_in = passed_along(sent_grad, "section", -1)
    input_grads = jnp.where(
        is_first, jnp.stack(backward_rows[1:]), jnp.stack(backward_rows[:micro_count])
    )
    summed = lax.psum_scatter(totals, "dp", scatter_dimension=0, tiled=True)
    outputs = tuple((item[None] for item in summed))
    return (layer_outputs[None], input_grads[None]) + outputs


MESH = pl.DeviceIdType.MESH
F = jnp.float32
B = jnp.bfloat16
VECTORS = ("g1", "s1", "bo", "g2", "s2", "bd", "bu")
PARTS = (
    (4, 0, 16, False, False),
    (0, 0, 32, False, False), (0, 32, 32, False, False),
    (1, 0, 64, True, False),
    (2, 0, 32, False, True), (2, 32, 32, True, False),
    (3, 0, 128, False, False), (3, 128, 128, True, False),
)
AHEAD = 4
SUMS = (
    (3, 0, 128, True, False), (3, 128, 128, False, True),
    (2, 0, 32, True, False), (2, 32, 32, False, False),
    (1, 0, 64, True, False),
    (0, 0, 32, False, False), (0, 32, 32, False, False),
    (4, 0, 16, False, False),
)
A, O, C, G, DM, DU, DB, DQKV = range(8)


def nt(left, right):
    return lax.dot_general(left, right, (((1,), (1,)), ((), ())), preferred_element_type=F)


def tn(left, right):
    return lax.dot_general(left, right, (((0,), (0,)), ((), ())), preferred_element_type=F)


def nn(left, right):
    return jnp.dot(left, right, preferred_element_type=F)


def tiles(total, step):
    def run(body):
        @pl.loop(0, total // step)
        def _(i):
            body(pl.ds(pl.multiple_of(i * step, step), step))

    return run


def normed(values):
    centred = values - jnp.mean(values, axis=-1, keepdims=True)
    scale = lax.rsqrt(jnp.mean(centred * centred, axis=-1, keepdims=True) + 1e-6)
    return centred * scale, scale


def norm_into(out, rows, gain, shift):
    @tiles(rows.shape[0], 64)
    def _(r):
        hat, _ = normed(rows[r, :].astype(F))
        out[r, :] = (hat * gain[...] + shift[...]).astype(B)


def norm_back(rows, grad, base, out, gain, gain_sum, shift_sum):
    @tiles(rows.shape[0], 64)
    def _(r):
        hat, scale = normed(rows[r, :].astype(F))
        d = grad[r, :]
        gain_sum[...] += jnp.sum(d * hat, axis=0, keepdims=True)
        shift_sum[...] += jnp.sum(d, axis=0, keepdims=True)
        d = d * gain[...]
        mean = jnp.mean(d, axis=-1, keepdims=True)
        along = jnp.mean(d * hat, axis=-1, keepdims=True)
        out[r, :] = (base[r, :].astype(F) + scale * (d - mean - hat * along)).astype(out.dtype)


def halves(pair):
    low = lax.broadcasted_iota(jnp.int32, pair.shape, 1) < HEAD
    zero = jnp.zeros_like(pair)
    return jnp.where(low, pair, zero), jnp.where(low, zero, pair)


def head_pairs(qkv, group, many):
    width = qkv.shape[1] // 3
    for i in range(many):
        for t in range(qkv.shape[0] // 128):
            cols = [pl.ds(pl.multiple_of(g * width + (group * many + i) * 128, 128), 128) for g in range(3)]
            yield pl.ds(t * 128, 128), cols


def softmaxes(items, bias):
    scores = [nt(qh, k) + bias[r, :] for r, q, k in items for qh in halves(q)]
    peaks = [jnp.max(s, axis=-1, keepdims=True) for s in scores]
    raised = [jnp.exp(s - m) for s, m in zip(scores, peaks)]
    totals = [1.0 / jnp.sum(e, axis=-1, keepdims=True) for e in raised]
    return [e * t for e, t in zip(raised, totals)]


def attend(qkv, mixed, bias):
    many = 1024 // qkv.shape[0]

    @pl.loop(0, qkv.shape[1] // 384 // many)
    def _(group):
        where = list(head_pairs(qkv, group, many))
        q, k, v = ([qkv[r, cols[g]] for r, cols in where] for g in range(3))
        q = [item * jnp.asarray(HEAD**-0.5, B) for item in q]
        probs = [p.astype(B) for p in softmaxes([(r, a, b) for (r, _), a, b in zip(where, q, k)], bias)]
        for n, (r, cols) in enumerate(where):
            low, high = halves(v[n])
            mixed[r, cols[0]] = (nn(probs[2 * n], low) + nn(probs[2 * n + 1], high)).astype(B)


def attend_back(qkv, grad, bias):
    many = 1024 // qkv.shape[0]

    def joined(items, axis):
        return jnp.concatenate(items, axis)

    @pl.loop(0, qkv.shape[1] // 384 // many)
    def _(group):
        where = list(head_pairs(qkv, group, many))
        q, k, v = ([qkv[r, cols[g]] for r, cols in where] for g in range(3))
        q = [item * jnp.asarray(HEAD**-0.5, B) for item in q]
        d = [grad[r, cols[0]] for r, cols in where]
        probs = softmaxes([(r, a, b) for (r, _), a, b in zip(where, q, k)], bias)
        slopes = [nt(dh, v[n]) for n in range(len(where)) for dh in halves(d[n])]
        centres = [jnp.sum(g * p, axis=-1, keepdims=True) for g, p in zip(slopes, probs)]
        slopes = [(p * (g - c)).astype(B) for p, g, c in zip(probs, slopes, centres)]
        probs = [p.astype(B) for p in probs]
        for n, (r, cols) in enumerate(where):
            pair = slice(2 * n, 2 * n + 2)
            grad_q = nn(joined(slopes[pair], 1), joined(halves(k[n]), 0))
            qkv[r, cols[0]] = (grad_q * HEAD**-0.5).astype(B)
            qkv[r, cols[1]] = tn(joined(slopes[pair], 0), joined(halves(q[n]), 0)).astype(B)
            qkv[r, cols[2]] = tn(joined(probs[pair], 0), joined(halves(d[n]), 0)).astype(B)


def relay(names, *refs):
    ref = dict(zip(names, refs))
    width = ref["x_own"].shape[1]
    rows = ref["x_own"].shape[0]
    ff = ref["w2"].shape[1]
    shard = [ref[f"own{j}"] for j in range(5)]
    full = [ref[f"w{j}"] for j in range(5)]
    both = [ref[n] for n in ("a", "o", "c", "g", "dm", "du", "db", "dqkv")]
    mine = [b.at[pl.ds(0, 2 * rows)] for b in both]
    theirs = [b.at[pl.ds(2 * rows, 2 * rows)] for b in both]
    vec = {n: ref["v_" + n] for n in VECTORS}
    vsum = {n: ref["d_" + n] for n in VECTORS}
    x, hidden, wide, dmixed, result = (ref[n] for n in ("x", "h", "wide", "do", "y"))
    for name in ("g1", "s1", "g2", "s2"):
        vsum[name][...] = jnp.zeros_like(vsum[name])
    p = lax.axis_index("dp")
    z, y, core = p // 4, (p // 2) % 2, p % 2
    inner = jnp.logical_or(z == 1, z == 2)
    section = lax.axis_index("section")
    zo, zn = jnp.where(z == 1, 0, 3), 3 - z
    zon = 3 - zo
    zi = jnp.where(z == 0, 1, 2)

    def idx(z, y, core):
        return (z * 2 + y) * 2 + core

    sibling, across, other = idx(z, y, 1 - core), idx(z, 1 - y, core), idx(zn, y, core)
    outer_one, inner_one = idx(zo, y, core), idx(zi, y, core)

    def remote(sec, src, dst, send_sem, recv_sem, to):
        return pltpu.make_async_remote_copy(
            src_ref=src, dst_ref=dst, send_sem=send_sem, recv_sem=recv_sem,
            device_id=(sec, to), device_id_type=MESH,
        )

    first = section == 0

    def only(condition):
        return lambda body: pl.when(condition)(body)

    class Flow:
        def __init__(self):
            self.sent = []

        def send(self, src, dst, made, recv_sem, to, sec=section):
            remote(sec, src, dst, made()[1], recv_sem, to).start()
            self.note(made)

        def note(self, made, condition=None):
            self.sent.append((made, condition))

        def arrived(self, dst, recv_sem):
            remote(section, dst, dst, ref["idle_sem"].at[0], recv_sem, sibling).wait_recv()

        def finish(self):
            for made, condition in self.sent:
                def wait():
                    like, send_sem = made()
                    remote(section, like, like, send_sem, ref["idle_sem"].at[0], sibling).wait_send()

                wait() if condition is None else pl.when(condition)(wait)
            self.sent = []

    def piece(k, b):
        j, first, count = PARTS[k][:3]
        size = shard[j].shape[0]
        return full[j].at[pl.ds(pl.multiple_of(b * size + first, count), count)]

    def own_piece(k):
        j, first, count = PARTS[k][:3]
        return shard[j].at[pl.ds(first, count)]

    def own_copy(k):
        return pltpu.make_async_copy(own_piece(k), piece(k, p), ref["ag_local"].at[k])

    def gather_steps(flow, is_inner):
        used = [0] * len(PARTS)

        def send(k, b, to, own=False):
            src = own_piece(k) if own else piece(k, b)
            n = used[k]

            def made():
                return full[PARTS[k][0]].at[pl.ds(0, PARTS[k][2])], ref["ag_send"].at[k, n]

            flow.send(src, piece(k, b), made, ref["ag_recv"].at[k, b], to)
            used[k] += 1

        def take(k, b, *to):
            flow.arrived(piece(k, b), ref["ag_recv"].at[k, b])
            for target in to:
                send(k, b, target)

        def begin(k):
            if is_inner:
                for to in (outer_one if PARTS[k][4] else across, other, sibling):
                    send(k, p, to, own=True)
                own_copy(k).start()
            else:
                send(k, p, inner_one, own=True)
                send(k, p, across, own=True)

        def early(k):
            take(k, idx(zo, y, core), other, sibling)
            take(k, idx(zn, y, core), across, sibling)
            if not PARTS[k][4]:
                take(k, idx(z, 1 - y, core), sibling)

        def late(k):
            by_z = PARTS[k][3]
            take(k, idx(zon, y, core), *((sibling,) if by_z else (across, sibling)))
            take(k, idx(zo, 1 - y, core), *((other, sibling) if by_z else (sibling,)))

        def end(k):
            if PARTS[k][4]:
                take(k, idx(z, 1 - y, core), sibling)
            take(k, idx(zn, 1 - y, core), sibling)
            take(k, idx(zon, 1 - y, core), sibling)

        def step(k):
            if k == 0:
                for first in range(AHEAD):
                    begin(first)
            if k + AHEAD < len(PARTS):
                begin(k + AHEAD)
            if is_inner:
                for stage, n in ((early, k), (late, k - 1), (end, k - 2)):
                    if 0 <= n < len(PARTS):
                        stage(n)
            else:
                take(k, across, inner_one)
                if PARTS[k][4]:
                    take(k, idx(zi, y, core), across)
                if k and PARTS[k - 1][4]:
                    take(k - 1, idx(zi, 1 - y, core), inner_one)

        return step

    def gathered(flow, j):
        for k, part in enumerate(PARTS):
            if part[0] == j:
                own_copy(k).wait()
                for b in range(8):
                    block = 2 * b + 1 - core
                    flow.arrived(piece(k, block), ref["ag_recv"].at[k, block])

    def write_small():
        stage = ref["stage"]
        stage[...] = jnp.zeros_like(stage)
        for c in range(2):
            @pl.when(core == c)
            def _():
                for n, name in enumerate(VECTORS[:6]):
                    stage[n : n + 1, 64 * c : 64 * c + 64] = ref["in_" + name][...].astype(F)
        for n in range(2):
            stage[6 + n : 7 + n, :] = ref["in_bu"][:, 128 * n : 128 * n + 128].astype(F)
        shard[4][...] = stage[...].astype(B)

    def write_crops():
        for m in range(2):
            ref["crops"][0:1, 64 * m : 64 * m + 64] = (ref["in_crop"][m : m + 1, :] + 1024 * m).astype(F)

    def write_bias(crops, first):
        along = jnp.broadcast_to(crops[0:1, :], (rows, rows))
        ref["bias"][pl.ds(first, rows), :] = jnp.where(along == along.T, 0.0, -1e30)

    def spread_vectors():
        for i in range(8):
            low = full[4][pl.ds(32 * i, 16), :].astype(F)
            high = full[4][pl.ds(32 * i + 16, 16), :].astype(F)
            joined = low + high
            for n, name in enumerate(VECTORS[:6]):
                vec[name][:, pl.ds(128 * i, 128)] = joined[n : n + 1]
            for n, part in enumerate((low[6:7], low[7:8], high[6:7], high[7:8])):
                vec["bu"][:, pl.ds(512 * i + 128 * n, 128)] = part

    def exchange(flow, which):
        pair = ref["act_send"].at[which], ref["act_recv"].at[which]
        remote(section, mine[which], theirs[which], *pair, sibling).start()

    def exchanged(flow, *which):
        for w in which:
            flow.arrived(theirs[w], ref["act_recv"].at[w])

    def forward_attend(r):
        norm_into(mine[A].at[r], x.at[r], vec["g1"], vec["s1"])

        @tiles(3 * width, 1536)
        def _(c):
            mine[DQKV][r, c] = nn(mine[A][r, :], full[0][:, c]).astype(B)

        attend(mine[DQKV].at[r], mine[O].at[r], ref["bias"].at[r])

    def forward_out(r):
        hidden[r, :] = x[r, :].astype(F) + nn(mine[O][r, :], full[1][...]) + vec["bo"][...]
        norm_into(mine[C].at[r], hidden.at[r], vec["g2"], vec["s2"])

    def forward_up(r):
        @tiles(ff, 1024)
        def _(c):
            u = nn(mine[C][r, :], full[2][:, c]) + vec["bu"][:, c]
            phi = 0.5 + 0.5 * lax.erf(u * 0.5**0.5)
            mine[G][r, c] = (u * phi).astype(B)
            mine[DU][r, c] = (phi + u * (jnp.exp(-0.5 * u * u) * (0.5 / jnp.pi) ** 0.5)).astype(B)

    def forward_down(r):
        result[r, :] = (hidden[r, :] + nn(mine[G][r, :], full[3][...]) + vec["bd"][...]).astype(B)

    def backward_du():
        vsum["bd"][...] = jnp.sum(mine[DM][...].astype(F), axis=0, keepdims=True)

        @tiles(ff, 1024)
        def _(c):
            du = (nt(mine[DM][...], full[3][c, :]) * mine[DU][:, c].astype(F)).astype(B)
            mine[DU][:, c] = du
            vsum["bu"][:, c] = jnp.sum(du.astype(F), axis=0, keepdims=True)

    def backward_dh():
        wide[...] = nt(mine[DU][...], full[2][...])
        norm_back(hidden, wide, mine[DM], hidden, vec["g2"], vsum["g2"], vsum["s2"])
        mine[DB][...] = hidden[...].astype(B)
        vsum["bo"][...] = jnp.sum(mine[DB][...].astype(F), axis=0, keepdims=True)

    def backward_attend():
        dmixed[...] = nt(mine[DB][...], full[1][...]).astype(B)
        attend_back(mine[DQKV], dmixed, ref["bias"])

    def backward_da():
        wide[...] = nt(mine[DQKV][...], full[0][...])

    def backward_dx(r):
        norm_back(x.at[r], wide.at[r], hidden.at[r], x.at[r], vec["g1"], vsum["g1"], vsum["s1"])

    def packed(which):
        src, out = both[which], ref["packed"]
        for i in range(width // 256):
            first = src[:, pl.ds(256 * i, 128)].astype(F)
            second = src[:, pl.ds(256 * i + 128, 128)].astype(F)
            low = lax.broadcasted_iota(jnp.int32, first.shape, 1) < HEAD
            even = jnp.where(low, first, pltpu.roll(second, HEAD, 1))
            odd = jnp.where(low, pltpu.roll(first, HEAD, 1), second)
            out[pl.ds(128 * i, 128), :] = jnp.where(core == 0, even, odd).T.astype(B)

    def grad_down():
        size = shard[3].shape[0]
        for o in range(8):
            c = pl.ds(pl.multiple_of(size * (2 * o + core), size), size)
            full[3][pl.ds(size * o, size), :] = tn(both[G][:, c], both[DM][...]).astype(B)

    def grad_of(j, left, right):
        packed(left)

        @tiles(both[right].shape[1], 512)
        def _(c):
            full[j][pl.ds(0, 8 * shard[j].shape[0]), c] = nn(ref["packed"][...], both[right][:, c]).astype(B)

    def grad_vectors():
        for o in range(8):
            for n, name in enumerate(VECTORS[:6]):
                ref["vp"][pl.ds(16 * o + n, 1), :] = vsum[name][:, pl.ds(128 * o, 128)]
            for n in range(4):
                ref["vp"][pl.ds(16 * o + 6 + n, 1), :] = vsum["bu"][:, pl.ds(512 * o + 128 * n, 128)]
            ref["vp"][pl.ds(16 * o + 10, 6), :] = jnp.zeros((6, 128), F)

    partial = [full[0], full[1], full[2], full[3], ref["vp"]]
    sums = [ref[f"out{j}"] for j in range(4)] + [ref["vs"]]
    NEAR, OWN, ALT, INNER, OUTER = range(5)
    slots = [[ref[f"r{s}_{j}"] for j in range(5)] for s in range(5)]

    def reducer(flow):
        def slot(s, k):
            j, first, count = SUMS[k][:3]
            return slots[s][j].at[pl.ds(first, count)]

        def part(k, zz, yy):
            j, first, count = SUMS[k][:3]
            size = partial[j].shape[0] // 8 if j == 4 else shard[j].shape[0]
            return partial[j].at[pl.ds(pl.multiple_of((zz * 2 + yy) * size + first, count), count)]

        def send(k, n, src, s, to):
            def made():
                return slot(s, k), ref["rs_send"].at[k, n]

            flow.send(src, slot(s, k), made, ref["rs_recv"].at[k, s], to)

        def arrived(k, s):
            flow.arrived(slot(s, k), ref["rs_recv"].at[k, s])

        def add(k, dst, *more):
            total = dst[...].astype(F)
            for s in more:
                total = total + slot(s, k)[...].astype(F)
            return total

        def issue(k):
            if SUMS[k][3]:
                send(k, 4, part(k, zon, y), OUTER, other)
                send(k, 1, part(k, zon, 1 - y), ALT, other)
            else:
                send(k, 1, part(k, zon, 1 - y), ALT, across)
                send(k, 6, part(k, zo, 1 - y), INNER, outer_one)

        def issue_near(k):
            send(k, 0, part(k, zn, 1 - y), NEAR, across)

        def issue_own(k):
            if SUMS[k][4]:
                send(k, 2, part(k, z, 1 - y), NEAR, outer_one)
            else:
                send(k, 2, part(k, z, 1 - y), OWN, across)

        def far_on(k):
            if not SUMS[k][3]:
                dst = part(k, zon, y)
                arrived(k, ALT)
                dst[...] = add(k, dst, ALT).astype(dst.dtype)
                send(k, 4, dst, OUTER, other)

        def near_on(k):
            dst = part(k, zn, y)
            arrived(k, NEAR)
            dst[...] = add(k, dst, NEAR).astype(dst.dtype)
            send(k, 3, dst, INNER, other)

        def outward(k):
            dst = part(k, zo, y)
            arrived(k, OUTER)
            dst[...] = add(k, dst, OUTER).astype(dst.dtype)
            send(k, 5, dst, OUTER, outer_one)
            if SUMS[k][3]:
                dst = part(k, zo, 1 - y)
                arrived(k, ALT)
                dst[...] = add(k, dst, ALT).astype(dst.dtype)
                send(k, 6, dst, INNER, outer_one)

        def last(k):
            arrived(k, INNER)
            arrived(k, OWN)
            j, first, count = SUMS[k][:3]
            sums[j][pl.ds(first, count), :] = add(k, part(k, z, y), OWN, INNER)

        def pass_on(k):
            arrived(k, INNER)
            send(k, 0, slot(INNER, k), OWN, across)

        def around(k, end):
            arrived(k, ALT if end else NEAR)
            if end:
                send(k, 2, slot(ALT, k), OWN, inner_one)
            else:
                send(k, 1, slot(NEAR, k), ALT, across)

        def collect(k):
            arrived(k, OUTER)
            arrived(k, OWN)
            j, first, count = SUMS[k][:3]
            sums[j][pl.ds(first, count), :] = slot(OUTER, k)[...].astype(F) + slot(OWN, k)[...].astype(F)

        def join_vectors():
            made = lambda: (ref["vs"], ref["vec_sem"].at[0])
            flow.send(ref["vs"], ref["vt"], made, ref["vec_sem"].at[1], sibling)
            flow.arrived(ref["vt"], ref["vec_sem"].at[1])
            ref["out4"][...] = ref["vs"][...] + ref["vt"][...]

        inner_steps = issue, issue_near, issue_own, far_on, near_on, outward, last
        return inner_steps, (pass_on, around, collect), join_vectors

    def hand_out(flow, src, out, n):
        made = lambda: (out, ref["res_send"].at[n])
        flow.send(src.at[pl.ds(rows, rows)], out, made, ref["res_recv"].at[n], outer_one)
        out[...] = src[pl.ds(0, rows), :]

    every = pl.ds(0, 2 * rows)
    near, far = pl.ds(0, rows), pl.ds(rows, rows)

    def half(h):
        return pl.ds(pl.multiple_of(h * rows, rows), rows)

    def inner_program():
        flow = Flow()
        step = gather_steps(flow, True)
        inner_steps, _, join_vectors = reducer(flow)
        issue, issue_near, issue_own, far_on, near_on, outward, last = inner_steps
        step(0)
        own = [
            pltpu.make_async_copy(src, dst.at[near], ref["tok_local"].at[0])
            for src, dst in ((ref["x_own"], x), (ref["dy_own"], mine[DM]))
        ]
        for n, copy in enumerate(own):
            pl.when(section == n)(copy.start)
        write_bias(ref["crops"], 0)

        def tokens():
            for n, (copy, dst) in enumerate(zip(own, (x, mine[DM]))):
                @pl.when(section == n)
                def _():
                    copy.wait()
                    flow.arrived(dst.at[far], ref["tok_recv"].at[1])
            flow.arrived(ref["far_crops"], ref["tok_recv"].at[0])
            write_bias(ref["far_crops"], rows)

        def steps(begin, end):
            for k in range(begin, end):
                step(k)

        @pl.loop(0, 2)
        def _(turn):
            gathering, active = only(turn == 0), only(section == turn)

            @gathering
            def _():
                steps(1, 6)
                gathered(flow, 4)
                spread_vectors()
                tokens()
                gathered(flow, 0)

            @active
            def _():
                @pl.loop(0, 2)
                def _(h):
                    @pl.when(jnp.logical_not(first))
                    def _():
                        flow.arrived(x.at[half(h)], ref["x_recv"].at[h])

                    forward_attend(half(h))

            @gathering
            def _():
                steps(6, 7)
                gathered(flow, 1)

            @active
            def _():
                forward_out(every)

            @gathering
            def _():
                steps(7, 9)
                gathered(flow, 2)

            @active
            def _():
                forward_up(every)

            @gathering
            def _():
                steps(9, len(PARTS) + 2)
                gathered(flow, 3)

            @active
            def _():
                forward_down(every)

        @pl.when(first)
        def _():
            for n, r in enumerate((near, far)):
                remote(1, result.at[r], x.at[r], ref["x_send"].at[n], ref["x_recv"].at[n], p).start()

        for n in range(2):
            flow.note(lambda n=n: (result.at[near], ref["x_send"].at[n]), first)
        flow.finish()
        for which in (G, C, O, A):
            exchange(flow, which)
        hand_out(flow, result, ref["y_out"], 0)

        def exchange_when(condition, *which):
            @pl.when(condition)
            def _():
                for w in which:
                    exchange(flow, w)

        @pl.loop(0, 2)
        def _(turn):
            main, grads = only(turn == 0), only(section == turn)
            leading = jnp.logical_and(turn == 0, first)
            trailing = jnp.logical_and(turn == 1, section == 1)

            @pl.when(leading)
            def _():
                for n, r in enumerate((near, far)):
                    flow.arrived(mine[DM].at[r], ref["x_recv"].at[2 + n])

            exchange_when(turn == 0, DM)
            main(backward_du)
            exchange_when(leading, DU)
            exchange_when(trailing, DU, DB, DQKV)

            @grads
            def _():
                exchanged(flow, G, DM)
                grad_down()
                issue(0)
                issue_near(0)

            main(backward_dh)
            exchange_when(leading, DB)

            @grads
            def _():
                issue(1)
                issue_near(1)
                exchanged(flow, C, DU)
                grad_of(2, C, DU)

            main(backward_attend)
            exchange_when(leading, DQKV)

            @grads
            def _():
                issue(2)
                issue(3)
                issue_near(2)
                exchanged(flow, O, DB)
                grad_of(1, O, DB)
                issue(4)

            main(backward_da)

            @grads
            def _():
                far_on(1)
                near_on(0)
                exchanged(flow, A, DQKV)
                grad_of(0, A, DQKV)
                issue(5)
                issue(6)
                issue_near(3)

            @main
            def _():
                @pl.loop(0, 2)
                def _(h):
                    r = half(h)
                    backward_dx(r)

                    @pl.when(jnp.logical_not(first))
                    def _():
                        to = mine[DM].at[r]
                        remote(0, x.at[r], to, ref["x_send"].at[2 + h], ref["x_recv"].at[2 + h], p).start()

        for n in range(2):
            flow.note(lambda n=n: (x.at[near], ref["x_send"].at[2 + n]), jnp.logical_not(first))
        for which in range(8):
            flow.note(lambda w=which: (mine[w], ref["act_send"].at[w]))
        grad_vectors()
        issue(7)
        hand_out(flow, x, ref["dx_out"], 1)
        count = len(SUMS)
        for k in range(2, count + 3):
            for turn, n in ((far_on, k), (issue_near, k + 2), (near_on, k - 1), (outward, k - 2), (issue_own, k - 3)):
                if 0 <= n < count:
                    turn(n)
        for k in range(count):
            last(k)
        join_vectors()
        flow.finish()

    def outer_program():
        flow = Flow()
        step = gather_steps(flow, False)
        _, (pass_on, around, collect), join_vectors = reducer(flow)
        for k in range(len(PARTS)):
            step(k)
            if k == 1:
                made = lambda: (ref["crops"], ref["tok_send"].at[0])
                flow.send(ref["crops"], ref["far_crops"], made, ref["tok_recv"].at[0], inner_one)
                for n, (src, dst) in enumerate(((ref["x_own"], x), (ref["dy_own"], mine[DM]))):
                    pl.when(section == n)(
                        remote(section, src, dst.at[far], ref["tok_send"].at[1], ref["tok_recv"].at[1], inner_one).start
                    )
                flow.note(lambda: (x.at[far], ref["tok_send"].at[1]))
        for k in range(len(SUMS) + 3):
            for turn, n in ((pass_on, k), (collect, k - 1)):
                if 0 <= n < len(SUMS) and (k < len(SUMS) or turn is pass_on):
                    turn(n)
            for end in range(2):
                n = k - 3 - end
                if 0 <= n < len(SUMS) and SUMS[n][4]:
                    around(n, end)
        collect(len(SUMS) - 1)
        join_vectors()
        flow.arrived(ref["y_out"], ref["res_recv"].at[0])
        flow.arrived(ref["dx_out"], ref["res_recv"].at[1])
        flow.finish()

    write_small()
    write_crops()
    pl.when(inner)(inner_program)
    pl.when(jnp.logical_not(inner))(outer_program)


def relay_call(x_own, dy_own, small, shards, dp):
    rows, width = x_own.shape
    ff = shards[2].shape[1]
    count = 2 * rows
    shapes = [item.shape for item in shards] + [(16, 128)]
    inputs = {"x_own": x_own, "dy_own": dy_own}
    inputs.update({f"own{j}": item for j, item in enumerate(shards)})
    outputs = {"y_out": ((rows, width), B), "dx_out": ((rows, width), B)}
    outputs.update({f"out{j}": (item.shape, F) for j, item in enumerate(shards)})
    outputs["out4"] = ((16, 128), F)
    scratch = {f"w{j}": ((dp * shape[0], shape[1]), B) for j, shape in enumerate(shapes)}
    for name, cols in zip(("a", "o", "c", "g", "dm", "du", "db", "dqkv"), (1, 1, 1, 0, 1, 0, 1, 3)):
        scratch[name] = ((2 * count, cols * width or ff), B)
    scratch.update(x=((count, width), B), h=((count, width), F), wide=((count, width), F), do=((count, width), B))
    scratch.update(y=((count, width), B), bias=((count, 128), F), packed=((width // 2, 2 * count), B))
    for name in VECTORS:
        scratch["v_" + name] = scratch["d_" + name] = ((1, ff if name == "bu" else width), F)
    scratch.update(vp=((128, 128), F), vs=((16, 128), F), vt=((16, 128), F), stage=((16, 128), F), crops=((8, 128), F), far_crops=((8, 128), F), own4=((16, 128), B))
    for s in range(5):
        for j, shape in enumerate(shapes):
            scratch[f"r{s}_{j}"] = (shape, F if j == 4 else B)
    sems = dict(
        ag_send=(len(PARTS), 16), ag_recv=(len(PARTS), dp), ag_local=(len(PARTS),), tok_local=(1,), tok_send=(2,),
        tok_recv=(2,), x_send=(4,), x_recv=(4,), act_send=(8,), act_recv=(8,), res_send=(2,), res_recv=(2,),
        rs_send=(len(SUMS), 7), rs_recv=(len(SUMS), 5), vec_sem=(2,), idle_sem=(1,),
    )
    names = [*inputs, *small, *outputs, *scratch, *sems]
    whole, anywhere = pl.BlockSpec(memory_space=pltpu.VMEM), pl.BlockSpec(memory_space=pl.ANY)
    return pl.pallas_call(
        functools.partial(relay, names),
        out_shape=[jax.ShapeDtypeStruct(*item) for item in outputs.values()],
        in_specs=[anywhere] * len(inputs) + [whole] * len(small),
        out_specs=[whole] * len(outputs),
        scratch_shapes=[pltpu.VMEM(*item) for item in scratch.values()]
        + [pltpu.SemaphoreType.DMA(item) for item in sems.values()],
        compiler_params=pltpu.CompilerParams(has_side_effects=True, vmem_limit_bytes=62 << 20),
        name="relay",
    )(*inputs.values(), *small.values())


def hand_over(*refs):
    rows, vectors, out, small = refs[:6], refs[6], refs[7:13], refs[13:20]
    for n in range(2):
        size = out[n].shape[2]
        for m in range(out[n].shape[1]):
            out[n][0, m] = rows[n][pl.ds(m * size, size), :]
    for n in range(2, 6):
        out[n][0] = rows[n][...]
    core = lax.axis_index("dp") % 2
    for c in range(2):
        @pl.when(core == c)
        def _():
            for n in range(6):
                small[n][...] = vectors[n : n + 1, 64 * c : 64 * c + 64]
            small[6][...] = vectors[6 + 2 * c : 8 + 2 * c, :]


def middle(
    block_input, crop_ids, out_grad, norm1_gain, norm1_shift, w_qkv, w_out, b_out,
    norm2_gain, norm2_shift, w_up, b_up, w_down, b_down,
):
    micro, rows, width = block_input.shape
    small = dict(zip(VECTORS, (norm1_gain, norm1_shift, b_out, norm2_gain, norm2_shift, b_down, b_up)))
    small = {"in_" + name: item for name, item in small.items()} | {"in_crop": crop_ids}
    got = relay_call(
        block_input.reshape(-1, width), out_grad.reshape(-1, width), small,
        (w_qkv[0], w_out[0], w_up[0], w_down[0]), lax.axis_size("dp"),
    )
    whole = pl.BlockSpec(memory_space=pltpu.VMEM)
    shapes = [((1, micro, rows, width), B)] * 2 + [((1,) + item.shape, F) for item in got[2:6]]
    shapes += [((1, 64), F)] * 6 + [((2, 128), F)]
    y, dx, g_qkv, g_out, g_up, g_down, g1, s1, bo, g2, s2, bd, bu = pl.pallas_call(
        hand_over,
        out_shape=[jax.ShapeDtypeStruct(*item) for item in shapes],
        in_specs=[whole] * 7,
        out_specs=[whole] * 13,
        compiler_params=pltpu.CompilerParams(vmem_limit_bytes=62 << 20),
        name="hand_over",
    )(*got)
    return y, dx, g1, s1, g_qkv, g_out, bo, g2, s2, g_up, bu.reshape(1, -1), g_down, bd


def solution(mesh):
    in_specs = (
        P(None, "dp", None),
        P(None, "dp"),
        P(None, "dp", None),
        P("section", "dp"),
        P("section", "dp"),
        P("section", "dp", None),
        P("section", "dp", None),
        P("section", "dp"),
        P("section", "dp"),
        P("section", "dp"),
        P("section", "dp", None),
        P("section", "dp"),
        P("section", "dp", None),
        P("section", "dp"),
    )
    out_specs = (
        P("section", None, "dp", None),
        P("section", None, "dp", None),
        P("section", "dp"),
        P("section", "dp"),
        P("section", "dp", None),
        P("section", "dp", None),
        P("section", "dp"),
        P("section", "dp"),
        P("section", "dp"),
        P("section", "dp", None),
        P("section", "dp"),
        P("section", "dp", None),
        P("section", "dp"),
    )
    fits = mesh.shape["dp"] == 16 and mesh.shape["section"] == 2
    return jax.shard_map(middle if fits else local, mesh=mesh, in_specs=in_specs, out_specs=out_specs, check_vma=False)
```

```python
import functools

import jax
import jax.numpy as jnp
from jax import lax
from jax.experimental import pallas as pl
from jax.experimental.pallas import tpu as pltpu
from jax.sharding import PartitionSpec as P

HEAD = 64


def passed_along(x, axis, by):
    devices = lax.axis_size(axis)
    pairs = [(i, i + by) for i in range(devices) if 0 <= i + by < devices]
    return lax.ppermute(x, axis, pairs)


def norm_rows(values, gain, shift):
    centred = values - jnp.mean(values, axis=-1, keepdims=True)
    spread = jnp.mean(centred * centred, axis=-1, keepdims=True)
    return centred * lax.rsqrt(spread + 1e-06) * gain + shift


def gelu_exact(values):
    return jax.nn.gelu(values, approximate=False)


def inner_rows(left, right):
    return lax.dot_general(
        left, right, (((0,), (0,)), ((), ())), preferred_element_type=jnp.float32
    )


def times_transpose(left, right):
    return lax.dot_general(
        left, right, (((1,), (1,)), ((), ())), preferred_element_type=jnp.float32
    )


def split_heads(qkv_rows):
    model_width = qkv_rows.shape[1] // 3
    head_count = model_width // HEAD
    queries = qkv_rows[:, :model_width].reshape(-1, head_count, HEAD)
    key_rows = qkv_rows[:, model_width : 2 * model_width].reshape(-1, head_count, HEAD)
    value_rows = qkv_rows[:, 2 * model_width :].reshape(-1, head_count, HEAD)
    return (queries, key_rows, value_rows)


def head_scores(qkv_rows, crop_rows):
    queries, key_rows, value_rows = split_heads(qkv_rows)
    scores = jnp.einsum("qhd,khd->hqk", queries, key_rows, preferred_element_type=jnp.float32)
    scores = scores * HEAD ** (-0.5)
    same_crop = crop_rows[:, None] == crop_rows[None, :]
    return jnp.where(same_crop[None], scores, -1e30)


def forward_layer(layer_in, crop_rows, weights):
    gain_one, shift_one, w_qkv, w_out, b_out, gain_two, shift_two, w_up, b_up, w_down, b_down = (
        weights
    )
    row_count = layer_in.shape[0]
    normed = norm_rows(
        layer_in, gain_one.astype(jnp.float32), shift_one.astype(jnp.float32)
    ).astype(jnp.bfloat16)
    qkv_rows = jnp.dot(normed, w_qkv, preferred_element_type=jnp.float32).astype(jnp.bfloat16)
    scores = head_scores(qkv_rows, crop_rows)
    row_peak = jnp.max(scores, axis=-1, keepdims=True)
    log_total = row_peak + jnp.log(jnp.sum(jnp.exp(scores - row_peak), axis=-1, keepdims=True))
    softmax_low = jnp.exp(scores - log_total).astype(jnp.bfloat16)
    queries, key_rows, value_rows = split_heads(qkv_rows)
    mixed_heads = jnp.einsum(
        "hqk,khd->qhd", softmax_low, value_rows, preferred_element_type=jnp.float32
    )
    mixed_heads = mixed_heads.reshape(row_count, -1).astype(jnp.bfloat16)
    hidden = (
        layer_in
        + jnp.dot(mixed_heads, w_out, preferred_element_type=jnp.float32)
        + b_out.astype(jnp.float32)
    )
    squeezed = norm_rows(
        hidden, gain_two.astype(jnp.float32), shift_two.astype(jnp.float32)
    ).astype(jnp.bfloat16)
    up_rows = jnp.dot(squeezed, w_up, preferred_element_type=jnp.float32) + b_up.astype(jnp.float32)
    active = gelu_exact(up_rows).astype(jnp.bfloat16)
    result = (
        hidden
        + jnp.dot(active, w_down, preferred_element_type=jnp.float32)
        + b_down.astype(jnp.float32)
    )
    return (
        layer_in,
        normed,
        qkv_rows,
        log_total,
        mixed_heads,
        hidden,
        squeezed,
        up_rows,
        active,
        result,
    )


def backward_feed(grad_result, saved, weights):
    gain_one, shift_one, w_qkv, w_out, b_out, gain_two, shift_two, w_up, b_up, w_down, b_down = (
        weights
    )
    (
        layer_in,
        normed,
        qkv_rows,
        log_total,
        mixed_heads,
        hidden,
        squeezed,
        up_rows,
        active,
        result,
    ) = saved
    grad_branch = grad_result.astype(jnp.bfloat16)
    grad_w_down = inner_rows(active, grad_branch)
    grad_b_down = jnp.sum(grad_branch.astype(jnp.float32), axis=0)
    grad_active = times_transpose(grad_branch, w_down)
    gelu_value, gelu_pull = jax.vjp(gelu_exact, up_rows)
    grad_up = gelu_pull(grad_active)[0].astype(jnp.bfloat16)
    grad_w_up = inner_rows(squeezed, grad_up)
    grad_b_up = jnp.sum(grad_up.astype(jnp.float32), axis=0)
    grad_squeezed = times_transpose(grad_up, w_up)
    norm_value, norm_pull = jax.vjp(
        norm_rows, hidden, gain_two.astype(jnp.float32), shift_two.astype(jnp.float32)
    )
    grad_hid, grad_gain_two, grad_shift_two = norm_pull(grad_squeezed)
    grad_hidden = grad_result + grad_hid
    return (
        grad_hidden,
        (grad_gain_two, grad_shift_two, grad_w_up, grad_b_up, grad_w_down, grad_b_down),
    )


def backward_attend(grad_hidden, saved, crop_rows, weights):
    gain_one, shift_one, w_qkv, w_out, b_out, gain_two, shift_two, w_up, b_up, w_down, b_down = (
        weights
    )
    (
        layer_in,
        normed,
        qkv_rows,
        log_total,
        mixed_heads,
        hidden,
        squeezed,
        up_rows,
        active,
        result,
    ) = saved
    row_count = layer_in.shape[0]
    grad_attn = grad_hidden.astype(jnp.bfloat16)
    grad_w_out = inner_rows(mixed_heads, grad_attn)
    grad_b_out = jnp.sum(grad_attn.astype(jnp.float32), axis=0)
    grad_mixed = times_transpose(grad_attn, w_out).astype(jnp.bfloat16)
    queries, key_rows, value_rows = split_heads(qkv_rows)
    grad_mixed = grad_mixed.reshape(queries.shape)
    softmax_out = jnp.exp(head_scores(qkv_rows, crop_rows) - log_total)
    grad_soft = jnp.einsum(
        "qhd,khd->hqk", grad_mixed, value_rows, preferred_element_type=jnp.float32
    )
    grad_values = jnp.einsum(
        "hqk,qhd->khd",
        softmax_out.astype(jnp.bfloat16),
        grad_mixed,
        preferred_element_type=jnp.float32,
    )
    row_centre = jnp.sum(grad_soft * softmax_out, axis=-1, keepdims=True)
    grad_scores = (softmax_out * (grad_soft - row_centre)).astype(jnp.bfloat16)
    grad_queries = jnp.einsum(
        "hqk,khd->qhd", grad_scores, key_rows, preferred_element_type=jnp.float32
    ) * HEAD ** (-0.5)
    grad_keys = jnp.einsum(
        "hqk,qhd->khd", grad_scores, queries, preferred_element_type=jnp.float32
    ) * HEAD ** (-0.5)
    grad_qkv = jnp.concatenate(
        [
            grad_queries.reshape(row_count, -1),
            grad_keys.reshape(row_count, -1),
            grad_values.reshape(row_count, -1),
        ],
        axis=1,
    ).astype(jnp.bfloat16)
    grad_w_qkv = inner_rows(normed, grad_qkv)
    grad_normed = times_transpose(grad_qkv, w_qkv)
    first_value, first_pull = jax.vjp(
        norm_rows, layer_in, gain_one.astype(jnp.float32), shift_one.astype(jnp.float32)
    )
    grad_in, grad_gain_one, grad_shift_one = first_pull(grad_normed)
    return (
        grad_hidden + grad_in,
        (grad_gain_one, grad_shift_one, grad_w_qkv, grad_w_out, grad_b_out),
    )


def local(
    block_input,
    crop_ids,
    out_grad,
    norm1_gain,
    norm1_shift,
    w_qkv,
    w_out,
    b_out,
    norm2_gain,
    norm2_shift,
    w_up,
    b_up,
    w_down,
    b_down,
):
    is_first = lax.axis_index("section") == 0
    shards = (
        norm1_gain,
        norm1_shift,
        w_qkv,
        w_out,
        b_out,
        norm2_gain,
        norm2_shift,
        w_up,
        b_up,
        w_down,
        b_down,
    )
    gathered = (
        lax.all_gather(shards[0], "dp", axis=1, tiled=True),
        lax.all_gather(shards[1], "dp", axis=1, tiled=True),
        lax.all_gather(shards[2], "dp", axis=1, tiled=True),
        lax.all_gather(shards[3], "dp", axis=1, tiled=True),
        lax.all_gather(shards[4], "dp", axis=1, tiled=True),
        lax.all_gather(shards[5], "dp", axis=1, tiled=True),
        lax.all_gather(shards[6], "dp", axis=1, tiled=True),
        lax.all_gather(shards[7], "dp", axis=1, tiled=True),
        lax.all_gather(shards[8], "dp", axis=1, tiled=True),
        lax.all_gather(shards[9], "dp", axis=1, tiled=True),
        lax.all_gather(shards[10], "dp", axis=1, tiled=True),
    )
    weights = tuple((item[0] for item in gathered))
    micro_count = block_input.shape[0]

    def pick(upper, lower):
        return jax.tree.map(
            lambda later, earlier: jnp.where(is_first, earlier, later), upper, lower
        )

    incoming = jnp.zeros(block_input.shape[1:], jnp.bfloat16)
    records = []
    kept_saved = []
    forward_rows = []
    for step_index in range(micro_count + 1):
        own_rows = block_input[min(step_index, micro_count - 1)]
        source = jnp.where(is_first, own_rows, incoming)
        crop_rows = jnp.where(
            is_first, crop_ids[min(step_index, micro_count - 1)], crop_ids[max(step_index - 1, 0)]
        )
        saved = forward_layer(source.astype(jnp.float32), crop_rows, weights)
        sent_rows = saved[-1].astype(jnp.bfloat16)
        forward_rows.append(sent_rows)
        records.append((source, crop_rows))
        kept_saved.append(saved)
        if step_index < micro_count:
            incoming = passed_along(sent_rows, "section", 1)
    layer_outputs = jnp.where(
        is_first, jnp.stack(forward_rows[:micro_count]), jnp.stack(forward_rows[1:])
    )
    totals = jax.tree.map(lambda item: jnp.zeros(item.shape, jnp.float32), weights)
    back_in = jnp.zeros(block_input.shape[1:], jnp.bfloat16)
    backward_rows = []
    for step_index in range(micro_count + 1):
        late_tick = min(step_index + 1, micro_count)
        early_tick = max(step_index - 1, 0)
        source, crop_rows = pick(records[late_tick], records[early_tick])
        saved = pick(kept_saved[late_tick], kept_saved[early_tick])
        if step_index < micro_count:
            last_grad = out_grad[step_index]
        else:
            last_grad = jnp.zeros_like(out_grad[0])
        cotangent = jnp.where(is_first, back_in, last_grad)
        grad_hidden, feed_grads = backward_feed(cotangent.astype(jnp.float32), saved, weights)
        feed_totals = tuple((left + right for left, right in zip(totals[5:], feed_grads)))
        grad_in, attend_grads = backward_attend(grad_hidden, saved, crop_rows, weights)
        attend_totals = tuple((left + right for left, right in zip(totals[:5], attend_grads)))
        totals = attend_totals + feed_totals
        sent_grad = grad_in.astype(jnp.bfloat16)
        backward_rows.append(sent_grad)
        if step_index < micro_count:
            back_in = passed_along(sent_grad, "section", -1)
    input_grads = jnp.where(
        is_first, jnp.stack(backward_rows[1:]), jnp.stack(backward_rows[:micro_count])
    )
    summed = lax.psum_scatter(totals, "dp", scatter_dimension=0, tiled=True)
    outputs = tuple((item[None] for item in summed))
    return (layer_outputs[None], input_grads[None]) + outputs


MESH = pl.DeviceIdType.MESH
F = jnp.float32
B = jnp.bfloat16
VECTORS = ("g1", "s1", "bo", "g2", "s2", "bd", "bu")
PARTS = (
    (4, 0, 16, False, False),
    (0, 0, 32, False, False), (0, 32, 32, False, False),
    (1, 0, 64, True, False),
    (2, 0, 32, False, True), (2, 32, 32, True, False),
    (3, 0, 64, False, False), (3, 64, 64, True, False), (3, 128, 64, False, False), (3, 192, 64, True, False),
)
AHEAD = 4
SUMS = (
    (3, 0, 64, True, False),
    (3, 64, 64, False, False),
    (3, 128, 64, True, False),
    (3, 192, 64, False, False),
    (2, 0, 16, True, False),
    (2, 16, 16, False, False),
    (2, 32, 16, True, False),
    (2, 48, 16, False, False),
    (1, 0, 64, False, False),
    (0, 0, 32, True, False),
    (0, 32, 32, False, False),
    (4, 0, 16, False, False),
)
A, O, C, G, DM, DU, DB, DQKV = range(8)


def nt(left, right):
    return lax.dot_general(left, right, (((1,), (1,)), ((), ())), preferred_element_type=F)


def tn(left, right):
    return lax.dot_general(left, right, (((0,), (0,)), ((), ())), preferred_element_type=F)


def nn(left, right):
    return jnp.dot(left, right, preferred_element_type=F)


def tiles(total, step):
    def run(body):
        @pl.loop(0, total // step)
        def _(i):
            body(pl.ds(pl.multiple_of(i * step, step), step))

    return run


def normed(values):
    centred = values - jnp.mean(values, axis=-1, keepdims=True)
    scale = lax.rsqrt(jnp.mean(centred * centred, axis=-1, keepdims=True) + 1e-6)
    return centred * scale, scale


def norm_into(out, rows, gain, shift):
    @tiles(rows.shape[0], 64)
    def _(r):
        hat, _ = normed(rows[r, :].astype(F))
        out[r, :] = (hat * gain[...] + shift[...]).astype(B)


def norm_back(rows, grad, base, out, gain, gain_sum, shift_sum):
    @tiles(rows.shape[0], 64)
    def _(r):
        hat, scale = normed(rows[r, :].astype(F))
        d = grad[r, :]
        gain_sum[...] += jnp.sum(d * hat, axis=0, keepdims=True)
        shift_sum[...] += jnp.sum(d, axis=0, keepdims=True)
        d = d * gain[...]
        mean = jnp.mean(d, axis=-1, keepdims=True)
        along = jnp.mean(d * hat, axis=-1, keepdims=True)
        out[r, :] = (base[r, :].astype(F) + scale * (d - mean - hat * along)).astype(out.dtype)


def halves(pair):
    low = lax.broadcasted_iota(jnp.int32, pair.shape, 1) < HEAD
    zero = jnp.zeros_like(pair)
    return jnp.where(low, pair, zero), jnp.where(low, zero, pair)


def head_pairs(qkv, group, many):
    width = qkv.shape[1] // 3
    for i in range(many):
        for t in range(qkv.shape[0] // 128):
            cols = [pl.ds(pl.multiple_of(g * width + (group * many + i) * 128, 128), 128) for g in range(3)]
            yield pl.ds(t * 128, 128), cols


def softmaxes(items, bias):
    scores = [nt(qh, k) + bias[r, :] for r, q, k in items for qh in halves(q)]
    peaks = [jnp.max(s, axis=-1, keepdims=True) for s in scores]
    raised = [jnp.exp(s - m) for s, m in zip(scores, peaks)]
    totals = [1.0 / jnp.sum(e, axis=-1, keepdims=True) for e in raised]
    return [e * t for e, t in zip(raised, totals)]


def attend(qkv, mixed, bias):
    many = 1024 // qkv.shape[0]

    @pl.loop(0, qkv.shape[1] // 384 // many)
    def _(group):
        where = list(head_pairs(qkv, group, many))
        q, k, v = ([qkv[r, cols[g]] for r, cols in where] for g in range(3))
        q = [item * jnp.asarray(HEAD**-0.5, B) for item in q]
        probs = [p.astype(B) for p in softmaxes([(r, a, b) for (r, _), a, b in zip(where, q, k)], bias)]
        for n, (r, cols) in enumerate(where):
            low, high = halves(v[n])
            mixed[r, cols[0]] = (nn(probs[2 * n], low) + nn(probs[2 * n + 1], high)).astype(B)


def attend_back(qkv, grad, bias):
    many = 1024 // qkv.shape[0]

    def joined(items, axis):
        return jnp.concatenate(items, axis)

    @pl.loop(0, qkv.shape[1] // 384 // many)
    def _(group):
        where = list(head_pairs(qkv, group, many))
        q, k, v = ([qkv[r, cols[g]] for r, cols in where] for g in range(3))
        q = [item * jnp.asarray(HEAD**-0.5, B) for item in q]
        d = [grad[r, cols[0]] for r, cols in where]
        probs = softmaxes([(r, a, b) for (r, _), a, b in zip(where, q, k)], bias)
        slopes = [nt(dh, v[n]) for n in range(len(where)) for dh in halves(d[n])]
        centres = [jnp.sum(g * p, axis=-1, keepdims=True) for g, p in zip(slopes, probs)]
        slopes = [(p * (g - c)).astype(B) for p, g, c in zip(probs, slopes, centres)]
        probs = [p.astype(B) for p in probs]
        for n, (r, cols) in enumerate(where):
            pair = slice(2 * n, 2 * n + 2)
            grad_q = nn(joined(slopes[pair], 1), joined(halves(k[n]), 0))
            qkv[r, cols[0]] = (grad_q * HEAD**-0.5).astype(B)
            qkv[r, cols[1]] = tn(joined(slopes[pair], 0), joined(halves(q[n]), 0)).astype(B)
            qkv[r, cols[2]] = tn(joined(probs[pair], 0), joined(halves(d[n]), 0)).astype(B)


def relay(names, *refs):
    ref = dict(zip(names, refs))
    width = ref["x_own"].shape[1]
    rows = ref["x_own"].shape[0]
    ff = ref["w2"].shape[1]
    shard = [ref[f"own{j}"] for j in range(5)]
    full = [ref[f"w{j}"] for j in range(5)]
    both = [ref[n] for n in ("a", "o", "c", "g", "dm", "du", "db", "dqkv")]
    mine = [b.at[pl.ds(0, 2 * rows)] for b in both]
    theirs = [b.at[pl.ds(2 * rows, 2 * rows)] for b in both]
    vec = {n: ref["v_" + n] for n in VECTORS}
    vsum = {n: ref["d_" + n] for n in VECTORS}
    x, hidden, wide, dmixed, result = (ref[n] for n in ("x", "h", "wide", "do", "y"))
    for name in ("g1", "s1", "g2", "s2"):
        vsum[name][...] = jnp.zeros_like(vsum[name])
    p = lax.axis_index("dp")
    z, y, core = p // 4, (p // 2) % 2, p % 2
    inner = jnp.logical_or(z == 1, z == 2)
    section = lax.axis_index("section")
    zo, zn = jnp.where(z == 1, 0, 3), 3 - z
    zon = 3 - zo
    zi = jnp.where(z == 0, 1, 2)

    def idx(z, y, core):
        return (z * 2 + y) * 2 + core

    sibling, across, other = idx(z, y, 1 - core), idx(z, 1 - y, core), idx(zn, y, core)
    outer_one, inner_one = idx(zo, y, core), idx(zi, y, core)

    def remote(sec, src, dst, send_sem, recv_sem, to):
        return pltpu.make_async_remote_copy(
            src_ref=src, dst_ref=dst, send_sem=send_sem, recv_sem=recv_sem,
            device_id=(sec, to), device_id_type=MESH,
        )

    first = section == 0

    def only(condition):
        return lambda body: pl.when(condition)(body)

    class Flow:
        def __init__(self):
            self.sent = []

        def send(self, src, dst, made, recv_sem, to, sec=section):
            remote(sec, src, dst, made()[1], recv_sem, to).start()
            self.note(made)

        def note(self, made, condition=None):
            self.sent.append((made, condition))

        def arrived(self, dst, recv_sem):
            remote(section, dst, dst, ref["idle_sem"].at[0], recv_sem, sibling).wait_recv()

        def finish(self):
            for made, condition in self.sent:
                def wait():
                    like, send_sem = made()
                    remote(section, like, like, send_sem, ref["idle_sem"].at[0], sibling).wait_send()

                wait() if condition is None else pl.when(condition)(wait)
            self.sent = []

    def piece(k, b):
        j, first, count = PARTS[k][:3]
        size = shard[j].shape[0]
        return full[j].at[pl.ds(pl.multiple_of(b * size + first, count), count)]

    def own_piece(k):
        j, first, count = PARTS[k][:3]
        return shard[j].at[pl.ds(first, count)]

    def own_copy(k):
        return pltpu.make_async_copy(own_piece(k), piece(k, p), ref["ag_local"].at[k])

    def gather_steps(flow, is_inner):
        used = [0] * len(PARTS)

        def send(k, b, to, own=False):
            src = own_piece(k) if own else piece(k, b)
            n = used[k]

            def made():
                return full[PARTS[k][0]].at[pl.ds(0, PARTS[k][2])], ref["ag_send"].at[k, n]

            flow.send(src, piece(k, b), made, ref["ag_recv"].at[k, b], to)
            used[k] += 1

        def take(k, b, *to):
            flow.arrived(piece(k, b), ref["ag_recv"].at[k, b])
            for target in to:
                send(k, b, target)

        def begin(k):
            if is_inner:
                for to in (outer_one if PARTS[k][4] else across, other, sibling):
                    send(k, p, to, own=True)
                own_copy(k).start()
            else:
                send(k, p, inner_one, own=True)
                send(k, p, across, own=True)

        def early(k):
            take(k, idx(zo, y, core), other, sibling)
            take(k, idx(zn, y, core), across, sibling)
            if not PARTS[k][4]:
                take(k, idx(z, 1 - y, core), sibling)

        def late(k):
            by_z = PARTS[k][3]
            take(k, idx(zon, y, core), *((sibling,) if by_z else (across, sibling)))
            take(k, idx(zo, 1 - y, core), *((other, sibling) if by_z else (sibling,)))

        def end(k):
            if PARTS[k][4]:
                take(k, idx(z, 1 - y, core), sibling)
            take(k, idx(zn, 1 - y, core), sibling)
            take(k, idx(zon, 1 - y, core), sibling)

        def step(k):
            if k == 0:
                for first in range(AHEAD):
                    begin(first)
            if k + AHEAD < len(PARTS):
                begin(k + AHEAD)
            if is_inner:
                for stage, n in ((early, k), (late, k - 1), (end, k - 2)):
                    if 0 <= n < len(PARTS):
                        stage(n)
            else:
                take(k, across, inner_one)
                if PARTS[k][4]:
                    take(k, idx(zi, y, core), across)
                if k and PARTS[k - 1][4]:
                    take(k - 1, idx(zi, 1 - y, core), inner_one)

        return step

    def gathered(flow, j):
        for k, part in enumerate(PARTS):
            if part[0] == j:
                own_copy(k).wait()
                for b in range(8):
                    block = 2 * b + 1 - core
                    flow.arrived(piece(k, block), ref["ag_recv"].at[k, block])

    def write_small():
        stage = ref["stage"]
        stage[...] = jnp.zeros_like(stage)
        for c in range(2):
            @pl.when(core == c)
            def _():
                for n, name in enumerate(VECTORS[:6]):
                    stage[n : n + 1, 64 * c : 64 * c + 64] = ref["in_" + name][...].astype(F)
        for n in range(2):
            stage[6 + n : 7 + n, :] = ref["in_bu"][:, 128 * n : 128 * n + 128].astype(F)
        shard[4][...] = stage[...].astype(B)

    def write_crops():
        for m in range(2):
            ref["crops"][0:1, 64 * m : 64 * m + 64] = (ref["in_crop"][m : m + 1, :] + 1024 * m).astype(F)

    def write_bias(crops, first):
        along = jnp.broadcast_to(crops[0:1, :], (rows, rows))
        ref["bias"][pl.ds(first, rows), :] = jnp.where(along == along.T, 0.0, -1e30)

    def spread_vectors():
        for i in range(8):
            low = full[4][pl.ds(32 * i, 16), :].astype(F)
            high = full[4][pl.ds(32 * i + 16, 16), :].astype(F)
            joined = low + high
            for n, name in enumerate(VECTORS[:6]):
                vec[name][:, pl.ds(128 * i, 128)] = joined[n : n + 1]
            for n, part in enumerate((low[6:7], low[7:8], high[6:7], high[7:8])):
                vec["bu"][:, pl.ds(512 * i + 128 * n, 128)] = part

    def exchange(flow, which):
        pair = ref["act_send"].at[which], ref["act_recv"].at[which]
        remote(section, mine[which], theirs[which], *pair, sibling).start()

    def exchanged(flow, *which):
        for w in which:
            flow.arrived(theirs[w], ref["act_recv"].at[w])

    def forward_attend(r):
        norm_into(mine[A].at[r], x.at[r], vec["g1"], vec["s1"])

        @tiles(3 * width, 1536)
        def _(c):
            mine[DQKV][r, c] = nn(mine[A][r, :], full[0][:, c]).astype(B)

        attend(mine[DQKV].at[r], mine[O].at[r], ref["bias"].at[r])

    def forward_out(r):
        hidden[r, :] = x[r, :].astype(F) + nn(mine[O][r, :], full[1][...]) + vec["bo"][...]
        norm_into(mine[C].at[r], hidden.at[r], vec["g2"], vec["s2"])

    def forward_up(r):
        @tiles(ff, 1024)
        def _(c):
            u = nn(mine[C][r, :], full[2][:, c]) + vec["bu"][:, c]
            phi = 0.5 + 0.5 * lax.erf(u * 0.5**0.5)
            mine[G][r, c] = (u * phi).astype(B)
            mine[DU][r, c] = (phi + u * (jnp.exp(-0.5 * u * u) * (0.5 / jnp.pi) ** 0.5)).astype(B)

    def forward_down(r):
        result[r, :] = (hidden[r, :] + nn(mine[G][r, :], full[3][...]) + vec["bd"][...]).astype(B)

    def backward_du():
        vsum["bd"][...] = jnp.sum(mine[DM][...].astype(F), axis=0, keepdims=True)

        @tiles(ff, 1024)
        def _(c):
            du = (nt(mine[DM][...], full[3][c, :]) * mine[DU][:, c].astype(F)).astype(B)
            mine[DU][:, c] = du
            vsum["bu"][:, c] = jnp.sum(du.astype(F), axis=0, keepdims=True)

    def backward_dh():
        wide[...] = nt(mine[DU][...], full[2][...])
        norm_back(hidden, wide, mine[DM], hidden, vec["g2"], vsum["g2"], vsum["s2"])
        mine[DB][...] = hidden[...].astype(B)
        vsum["bo"][...] = jnp.sum(mine[DB][...].astype(F), axis=0, keepdims=True)

    def backward_attend():
        dmixed[...] = nt(mine[DB][...], full[1][...]).astype(B)
        attend_back(mine[DQKV], dmixed, ref["bias"])

    def backward_da():
        wide[...] = nt(mine[DQKV][...], full[0][...])

    def backward_dx(r):
        norm_back(x.at[r], wide.at[r], hidden.at[r], x.at[r], vec["g1"], vsum["g1"], vsum["s1"])

    def packed(which):
        src, out = both[which], ref["packed"]
        for i in range(width // 256):
            first = src[:, pl.ds(256 * i, 128)].astype(F)
            second = src[:, pl.ds(256 * i + 128, 128)].astype(F)
            low = lax.broadcasted_iota(jnp.int32, first.shape, 1) < HEAD
            even = jnp.where(low, first, pltpu.roll(second, HEAD, 1))
            odd = jnp.where(low, pltpu.roll(first, HEAD, 1), second)
            out[pl.ds(128 * i, 128), :] = jnp.where(core == 0, even, odd).T.astype(B)

    def grad_down():
        size = shard[3].shape[0]
        for o in range(8):
            c = pl.ds(pl.multiple_of(size * (2 * o + core), size), size)
            full[3][pl.ds(size * o, size), :] = tn(both[G][:, c], both[DM][...]).astype(B)

    def grad_of(j, left, right):
        packed(left)

        @tiles(both[right].shape[1], 512)
        def _(c):
            full[j][pl.ds(0, 8 * shard[j].shape[0]), c] = nn(ref["packed"][...], both[right][:, c]).astype(B)

    def grad_vectors():
        for o in range(8):
            for n, name in enumerate(VECTORS[:6]):
                ref["vp"][pl.ds(16 * o + n, 1), :] = vsum[name][:, pl.ds(128 * o, 128)]
            for n in range(4):
                ref["vp"][pl.ds(16 * o + 6 + n, 1), :] = vsum["bu"][:, pl.ds(512 * o + 128 * n, 128)]
            ref["vp"][pl.ds(16 * o + 10, 6), :] = jnp.zeros((6, 128), F)

    partial = [full[0], full[1], full[2], full[3], ref["vp"]]
    sums = [ref[f"out{j}"] for j in range(4)] + [ref["vs"]]
    NEAR, OWN, ALT, INNER, OUTER = range(5)
    slots = [[ref[f"r{s}_{j}"] for j in range(5)] for s in range(5)]

    def reducer(flow):
        def slot(s, k):
            j, first, count = SUMS[k][:3]
            return slots[s][j].at[pl.ds(first, count)]

        def part(k, zz, yy):
            j, first, count = SUMS[k][:3]
            size = partial[j].shape[0] // 8 if j == 4 else shard[j].shape[0]
            return partial[j].at[pl.ds(pl.multiple_of((zz * 2 + yy) * size + first, count), count)]

        def send(k, n, src, s, to):
            def made():
                return slot(s, k), ref["rs_send"].at[k, n]

            flow.send(src, slot(s, k), made, ref["rs_recv"].at[k, s], to)

        def arrived(k, s):
            flow.arrived(slot(s, k), ref["rs_recv"].at[k, s])

        def add(k, dst, *more):
            total = dst[...].astype(F)
            for s in more:
                total = total + slot(s, k)[...].astype(F)
            return total

        def issue(k):
            if SUMS[k][3]:
                send(k, 4, part(k, zon, y), OUTER, other)
                send(k, 1, part(k, zon, 1 - y), ALT, other)
            else:
                send(k, 1, part(k, zon, 1 - y), ALT, across)
                send(k, 6, part(k, zo, 1 - y), INNER, outer_one)

        def issue_near(k):
            send(k, 0, part(k, zn, 1 - y), NEAR, across)

        def issue_own(k):
            if SUMS[k][4]:
                send(k, 2, part(k, z, 1 - y), NEAR, outer_one)
            else:
                send(k, 2, part(k, z, 1 - y), OWN, across)

        def far_on(k):
            if not SUMS[k][3]:
                dst = part(k, zon, y)
                arrived(k, ALT)
                dst[...] = add(k, dst, ALT).astype(dst.dtype)
                send(k, 4, dst, OUTER, other)

        def near_on(k):
            dst = part(k, zn, y)
            arrived(k, NEAR)
            dst[...] = add(k, dst, NEAR).astype(dst.dtype)
            send(k, 3, dst, INNER, other)

        def outward(k):
            dst = part(k, zo, y)
            arrived(k, OUTER)
            dst[...] = add(k, dst, OUTER).astype(dst.dtype)
            send(k, 5, dst, OUTER, outer_one)
            if SUMS[k][3]:
                dst = part(k, zo, 1 - y)
                arrived(k, ALT)
                dst[...] = add(k, dst, ALT).astype(dst.dtype)
                send(k, 6, dst, INNER, outer_one)

        def last(k):
            arrived(k, INNER)
            arrived(k, OWN)
            j, first, count = SUMS[k][:3]
            sums[j][pl.ds(first, count), :] = add(k, part(k, z, y), OWN, INNER)

        def pass_on(k):
            arrived(k, INNER)
            send(k, 0, slot(INNER, k), OWN, across)

        def around(k, end):
            arrived(k, ALT if end else NEAR)
            if end:
                send(k, 2, slot(ALT, k), OWN, inner_one)
            else:
                send(k, 1, slot(NEAR, k), ALT, across)

        def collect(k):
            arrived(k, OUTER)
            arrived(k, OWN)
            j, first, count = SUMS[k][:3]
            sums[j][pl.ds(first, count), :] = slot(OUTER, k)[...].astype(F) + slot(OWN, k)[...].astype(F)

        def join_vectors():
            made = lambda: (ref["vs"], ref["vec_sem"].at[0])
            flow.send(ref["vs"], ref["vt"], made, ref["vec_sem"].at[1], sibling)
            flow.arrived(ref["vt"], ref["vec_sem"].at[1])
            ref["out4"][...] = ref["vs"][...] + ref["vt"][...]

        inner_steps = issue, issue_near, issue_own, far_on, near_on, outward, last
        return inner_steps, (pass_on, around, collect), join_vectors

    def hand_out(flow, src, out, n):
        made = lambda: (out, ref["res_send"].at[n])
        flow.send(src.at[pl.ds(rows, rows)], out, made, ref["res_recv"].at[n], outer_one)
        out[...] = src[pl.ds(0, rows), :]

    every = pl.ds(0, 2 * rows)
    near, far = pl.ds(0, rows), pl.ds(rows, rows)

    def half(h):
        return pl.ds(pl.multiple_of(h * rows, rows), rows)

    def inner_program():
        flow = Flow()
        step = gather_steps(flow, True)
        inner_steps, _, join_vectors = reducer(flow)
        issue, issue_near, issue_own, far_on, near_on, outward, last = inner_steps
        step(0)
        own = [
            pltpu.make_async_copy(src, dst.at[near], ref["tok_local"].at[0])
            for src, dst in ((ref["x_own"], x), (ref["dy_own"], mine[DM]))
        ]
        for n, copy in enumerate(own):
            pl.when(section == n)(copy.start)
        write_bias(ref["crops"], 0)

        def tokens():
            for n, (copy, dst) in enumerate(zip(own, (x, mine[DM]))):
                @pl.when(section == n)
                def _():
                    copy.wait()
                    flow.arrived(dst.at[far], ref["tok_recv"].at[1])
            flow.arrived(ref["far_crops"], ref["tok_recv"].at[0])
            write_bias(ref["far_crops"], rows)

        def steps(begin, end):
            for k in range(begin, end):
                step(k)

        @pl.loop(0, 2)
        def _(turn):
            gathering, active = only(turn == 0), only(section == turn)

            @gathering
            def _():
                steps(1, 6)
                gathered(flow, 4)
                spread_vectors()
                tokens()
                gathered(flow, 0)

            @active
            def _():
                @pl.loop(0, 2)
                def _(h):
                    @pl.when(jnp.logical_not(first))
                    def _():
                        flow.arrived(x.at[half(h)], ref["x_recv"].at[h])

                    forward_attend(half(h))

            @gathering
            def _():
                steps(6, 7)
                gathered(flow, 1)

            @active
            def _():
                forward_out(every)

            @gathering
            def _():
                steps(7, 9)
                gathered(flow, 2)

            @active
            def _():
                forward_up(every)

            @gathering
            def _():
                steps(9, len(PARTS) + 2)
                gathered(flow, 3)

            @active
            def _():
                forward_down(every)

        @pl.when(first)
        def _():
            for n, r in enumerate((near, far)):
                remote(1, result.at[r], x.at[r], ref["x_send"].at[n], ref["x_recv"].at[n], p).start()

        for n in range(2):
            flow.note(lambda n=n: (result.at[near], ref["x_send"].at[n]), first)
        flow.finish()
        for which in (G, C, O, A):
            exchange(flow, which)
        hand_out(flow, result, ref["y_out"], 0)

        def exchange_when(condition, *which):
            @pl.when(condition)
            def _():
                for w in which:
                    exchange(flow, w)

        @pl.loop(0, 2)
        def _(turn):
            main, grads = only(turn == 0), only(section == turn)
            leading = jnp.logical_and(turn == 0, first)
            trailing = jnp.logical_and(turn == 1, section == 1)

            @pl.when(leading)
            def _():
                for n, r in enumerate((near, far)):
                    flow.arrived(mine[DM].at[r], ref["x_recv"].at[2 + n])

            exchange_when(turn == 0, DM)
            main(backward_du)
            exchange_when(leading, DU)
            exchange_when(trailing, DU, DB, DQKV)

            @grads
            def _():
                exchanged(flow, G, DM)
                grad_down()
                issue(0)
                issue_near(0)
                issue(1)
                issue_near(1)

            main(backward_dh)
            exchange_when(leading, DB)

            @grads
            def _():
                issue(2)
                issue_near(2)
                issue(3)
                exchanged(flow, C, DU)
                grad_of(2, C, DU)

            main(backward_attend)
            exchange_when(leading, DQKV)

            @grads
            def _():
                for k in range(4, 8):
                    issue(k)
                issue_near(3)
                exchanged(flow, O, DB)
                grad_of(1, O, DB)
                issue(8)

            main(backward_da)

            @grads
            def _():
                far_on(1)
                near_on(0)
                exchanged(flow, A, DQKV)
                grad_of(0, A, DQKV)
                issue(9)
                issue(10)
                issue_near(4)

            @main
            def _():
                @pl.loop(0, 2)
                def _(h):
                    r = half(h)
                    backward_dx(r)

                    @pl.when(jnp.logical_not(first))
                    def _():
                        to = mine[DM].at[r]
                        remote(0, x.at[r], to, ref["x_send"].at[2 + h], ref["x_recv"].at[2 + h], p).start()

        for n in range(2):
            flow.note(lambda n=n: (x.at[near], ref["x_send"].at[2 + n]), jnp.logical_not(first))
        for which in range(8):
            flow.note(lambda w=which: (mine[w], ref["act_send"].at[w]))
        grad_vectors()
        issue(11)
        hand_out(flow, x, ref["dx_out"], 1)
        count = len(SUMS)
        for k in range(2, count + 4):
            plan = ((far_on, [2 * k - 2, 2 * k - 1]), (issue_near, [k + 3]), (near_on, [k - 1]), (outward, [k - 3] if k < 8 else [2 * k - 11, 2 * k - 10]), (issue_own, [k - 4]))
            for turn, which in plan:
                for n in which:
                    if 0 <= n < count:
                        turn(n)
        for k in range(count):
            last(k)
        join_vectors()
        flow.finish()

    def outer_program():
        flow = Flow()
        step = gather_steps(flow, False)
        _, (pass_on, around, collect), join_vectors = reducer(flow)
        for k in range(len(PARTS)):
            step(k)
            if k == 1:
                made = lambda: (ref["crops"], ref["tok_send"].at[0])
                flow.send(ref["crops"], ref["far_crops"], made, ref["tok_recv"].at[0], inner_one)
                for n, (src, dst) in enumerate(((ref["x_own"], x), (ref["dy_own"], mine[DM]))):
                    pl.when(section == n)(
                        remote(section, src, dst.at[far], ref["tok_send"].at[1], ref["tok_recv"].at[1], inner_one).start
                    )
                flow.note(lambda: (x.at[far], ref["tok_send"].at[1]))
        for k in range(len(SUMS)):
            for turn, n in ((pass_on, k), (collect, k - 1)):
                if 0 <= n:
                    turn(n)
            for end in range(2):
                n = k - 3 - end
                if 0 <= n < len(SUMS) and SUMS[n][4]:
                    around(n, end)
        collect(len(SUMS) - 1)
        join_vectors()
        flow.arrived(ref["y_out"], ref["res_recv"].at[0])
        flow.arrived(ref["dx_out"], ref["res_recv"].at[1])
        flow.finish()

    write_small()
    write_crops()
    pl.when(inner)(inner_program)
    pl.when(jnp.logical_not(inner))(outer_program)


def relay_call(x_own, dy_own, small, shards, dp):
    rows, width = x_own.shape
    ff = shards[2].shape[1]
    count = 2 * rows
    shapes = [item.shape for item in shards] + [(16, 128)]
    inputs = {"x_own": x_own, "dy_own": dy_own}
    inputs.update({f"own{j}": item for j, item in enumerate(shards)})
    outputs = {"y_out": ((rows, width), B), "dx_out": ((rows, width), B)}
    outputs.update({f"out{j}": (item.shape, F) for j, item in enumerate(shards)})
    outputs["out4"] = ((16, 128), F)
    scratch = {f"w{j}": ((dp * shape[0], shape[1]), B) for j, shape in enumerate(shapes)}
    for name, cols in zip(("a", "o", "c", "g", "dm", "du", "db", "dqkv"), (1, 1, 1, 0, 1, 0, 1, 3)):
        scratch[name] = ((2 * count, cols * width or ff), B)
    scratch.update(x=((count, width), B), h=((count, width), F), wide=((count, width), F), do=((count, width), B))
    scratch.update(y=((count, width), B), bias=((count, 128), F), packed=((width // 2, 2 * count), B))
    for name in VECTORS:
        scratch["v_" + name] = scratch["d_" + name] = ((1, ff if name == "bu" else width), F)
    scratch.update(vp=((128, 128), F), vs=((16, 128), F), vt=((16, 128), F), stage=((16, 128), F), crops=((8, 128), F), far_crops=((8, 128), F), own4=((16, 128), B))
    for s in range(5):
        for j, shape in enumerate(shapes):
            scratch[f"r{s}_{j}"] = (shape, F if j == 4 else B)
    sems = dict(
        ag_send=(len(PARTS), 16), ag_recv=(len(PARTS), dp), ag_local=(len(PARTS),), tok_local=(1,), tok_send=(2,),
        tok_recv=(2,), x_send=(4,), x_recv=(4,), act_send=(8,), act_recv=(8,), res_send=(2,), res_recv=(2,),
        rs_send=(len(SUMS), 7), rs_recv=(len(SUMS), 5), vec_sem=(2,), idle_sem=(1,),
    )
    names = [*inputs, *small, *outputs, *scratch, *sems]
    whole, anywhere = pl.BlockSpec(memory_space=pltpu.VMEM), pl.BlockSpec(memory_space=pl.ANY)
    return pl.pallas_call(
        functools.partial(relay, names),
        out_shape=[jax.ShapeDtypeStruct(*item) for item in outputs.values()],
        in_specs=[anywhere] * len(inputs) + [whole] * len(small),
        out_specs=[whole] * len(outputs),
        scratch_shapes=[pltpu.VMEM(*item) for item in scratch.values()]
        + [pltpu.SemaphoreType.DMA(item) for item in sems.values()],
        compiler_params=pltpu.CompilerParams(has_side_effects=True, vmem_limit_bytes=62 << 20),
        name="relay",
    )(*inputs.values(), *small.values())


def hand_over(*refs):
    rows, vectors, out, small = refs[:6], refs[6], refs[7:13], refs[13:20]
    for n in range(2):
        size = out[n].shape[2]
        for m in range(out[n].shape[1]):
            out[n][0, m] = rows[n][pl.ds(m * size, size), :]
    for n in range(2, 6):
        out[n][0] = rows[n][...]
    core = lax.axis_index("dp") % 2
    for c in range(2):
        @pl.when(core == c)
        def _():
            for n in range(6):
                small[n][...] = vectors[n : n + 1, 64 * c : 64 * c + 64]
            small[6][...] = vectors[6 + 2 * c : 8 + 2 * c, :]


def middle(
    block_input, crop_ids, out_grad, norm1_gain, norm1_shift, w_qkv, w_out, b_out,
    norm2_gain, norm2_shift, w_up, b_up, w_down, b_down,
):
    micro, rows, width = block_input.shape
    small = dict(zip(VECTORS, (norm1_gain, norm1_shift, b_out, norm2_gain, norm2_shift, b_down, b_up)))
    small = {"in_" + name: item for name, item in small.items()} | {"in_crop": crop_ids}
    got = relay_call(
        block_input.reshape(-1, width), out_grad.reshape(-1, width), small,
        (w_qkv[0], w_out[0], w_up[0], w_down[0]), lax.axis_size("dp"),
    )
    whole = pl.BlockSpec(memory_space=pltpu.VMEM)
    shapes = [((1, micro, rows, width), B)] * 2 + [((1,) + item.shape, F) for item in got[2:6]]
    shapes += [((1, 64), F)] * 6 + [((2, 128), F)]
    y, dx, g_qkv, g_out, g_up, g_down, g1, s1, bo, g2, s2, bd, bu = pl.pallas_call(
        hand_over,
        out_shape=[jax.ShapeDtypeStruct(*item) for item in shapes],
        in_specs=[whole] * 7,
        out_specs=[whole] * 13,
        compiler_params=pltpu.CompilerParams(vmem_limit_bytes=62 << 20),
        name="hand_over",
    )(*got)
    return y, dx, g1, s1, g_qkv, g_out, bo, g2, s2, g_up, bu.reshape(1, -1), g_down, bd


def solution(mesh):
    in_specs = (
        P(None, "dp", None),
        P(None, "dp"),
        P(None, "dp", None),
        P("section", "dp"),
        P("section", "dp"),
        P("section", "dp", None),
        P("section", "dp", None),
        P("section", "dp"),
        P("section", "dp"),
        P("section", "dp"),
        P("section", "dp", None),
        P("section", "dp"),
        P("section", "dp", None),
        P("section", "dp"),
    )
    out_specs = (
        P("section", None, "dp", None),
        P("section", None, "dp", None),
        P("section", "dp"),
        P("section", "dp"),
        P("section", "dp", None),
        P("section", "dp", None),
        P("section", "dp"),
        P("section", "dp"),
        P("section", "dp"),
        P("section", "dp", None),
        P("section", "dp"),
        P("section", "dp", None),
        P("section", "dp"),
    )
    fits = mesh.shape["dp"] == 16 and mesh.shape["section"] == 2
    return jax.shard_map(middle if fits else local, mesh=mesh, in_specs=in_specs, out_specs=out_specs, check_vma=False)
```

```python
import functools

import jax
import jax.numpy as jnp
from jax import lax
from jax.experimental import pallas as pl
from jax.experimental.pallas import tpu as pltpu
from jax.sharding import PartitionSpec as P

HEAD = 64


def passed_along(x, axis, by):
    devices = lax.axis_size(axis)
    pairs = [(i, i + by) for i in range(devices) if 0 <= i + by < devices]
    return lax.ppermute(x, axis, pairs)


def norm_rows(values, gain, shift):
    centred = values - jnp.mean(values, axis=-1, keepdims=True)
    spread = jnp.mean(centred * centred, axis=-1, keepdims=True)
    return centred * lax.rsqrt(spread + 1e-06) * gain + shift


def gelu_exact(values):
    return jax.nn.gelu(values, approximate=False)


def inner_rows(left, right):
    return lax.dot_general(
        left, right, (((0,), (0,)), ((), ())), preferred_element_type=jnp.float32
    )


def times_transpose(left, right):
    return lax.dot_general(
        left, right, (((1,), (1,)), ((), ())), preferred_element_type=jnp.float32
    )


def split_heads(qkv_rows):
    model_width = qkv_rows.shape[1] // 3
    head_count = model_width // HEAD
    queries = qkv_rows[:, :model_width].reshape(-1, head_count, HEAD)
    key_rows = qkv_rows[:, model_width : 2 * model_width].reshape(-1, head_count, HEAD)
    value_rows = qkv_rows[:, 2 * model_width :].reshape(-1, head_count, HEAD)
    return (queries, key_rows, value_rows)


def head_scores(qkv_rows, crop_rows):
    queries, key_rows, value_rows = split_heads(qkv_rows)
    scores = jnp.einsum("qhd,khd->hqk", queries, key_rows, preferred_element_type=jnp.float32)
    scores = scores * HEAD ** (-0.5)
    same_crop = crop_rows[:, None] == crop_rows[None, :]
    return jnp.where(same_crop[None], scores, -1e30)


def forward_layer(layer_in, crop_rows, weights):
    gain_one, shift_one, w_qkv, w_out, b_out, gain_two, shift_two, w_up, b_up, w_down, b_down = (
        weights
    )
    row_count = layer_in.shape[0]
    normed = norm_rows(
        layer_in, gain_one.astype(jnp.float32), shift_one.astype(jnp.float32)
    ).astype(jnp.bfloat16)
    qkv_rows = jnp.dot(normed, w_qkv, preferred_element_type=jnp.float32).astype(jnp.bfloat16)
    scores = head_scores(qkv_rows, crop_rows)
    row_peak = jnp.max(scores, axis=-1, keepdims=True)
    log_total = row_peak + jnp.log(jnp.sum(jnp.exp(scores - row_peak), axis=-1, keepdims=True))
    softmax_low = jnp.exp(scores - log_total).astype(jnp.bfloat16)
    queries, key_rows, value_rows = split_heads(qkv_rows)
    mixed_heads = jnp.einsum(
        "hqk,khd->qhd", softmax_low, value_rows, preferred_element_type=jnp.float32
    )
    mixed_heads = mixed_heads.reshape(row_count, -1).astype(jnp.bfloat16)
    hidden = (
        layer_in
        + jnp.dot(mixed_heads, w_out, preferred_element_type=jnp.float32)
        + b_out.astype(jnp.float32)
    )
    squeezed = norm_rows(
        hidden, gain_two.astype(jnp.float32), shift_two.astype(jnp.float32)
    ).astype(jnp.bfloat16)
    up_rows = jnp.dot(squeezed, w_up, preferred_element_type=jnp.float32) + b_up.astype(jnp.float32)
    active = gelu_exact(up_rows).astype(jnp.bfloat16)
    result = (
        hidden
        + jnp.dot(active, w_down, preferred_element_type=jnp.float32)
        + b_down.astype(jnp.float32)
    )
    return (
        layer_in,
        normed,
        qkv_rows,
        log_total,
        mixed_heads,
        hidden,
        squeezed,
        up_rows,
        active,
        result,
    )


def backward_feed(grad_result, saved, weights):
    gain_one, shift_one, w_qkv, w_out, b_out, gain_two, shift_two, w_up, b_up, w_down, b_down = (
        weights
    )
    (
        layer_in,
        normed,
        qkv_rows,
        log_total,
        mixed_heads,
        hidden,
        squeezed,
        up_rows,
        active,
        result,
    ) = saved
    grad_branch = grad_result.astype(jnp.bfloat16)
    grad_w_down = inner_rows(active, grad_branch)
    grad_b_down = jnp.sum(grad_branch.astype(jnp.float32), axis=0)
    grad_active = times_transpose(grad_branch, w_down)
    gelu_value, gelu_pull = jax.vjp(gelu_exact, up_rows)
    grad_up = gelu_pull(grad_active)[0].astype(jnp.bfloat16)
    grad_w_up = inner_rows(squeezed, grad_up)
    grad_b_up = jnp.sum(grad_up.astype(jnp.float32), axis=0)
    grad_squeezed = times_transpose(grad_up, w_up)
    norm_value, norm_pull = jax.vjp(
        norm_rows, hidden, gain_two.astype(jnp.float32), shift_two.astype(jnp.float32)
    )
    grad_hid, grad_gain_two, grad_shift_two = norm_pull(grad_squeezed)
    grad_hidden = grad_result + grad_hid
    return (
        grad_hidden,
        (grad_gain_two, grad_shift_two, grad_w_up, grad_b_up, grad_w_down, grad_b_down),
    )


def backward_attend(grad_hidden, saved, crop_rows, weights):
    gain_one, shift_one, w_qkv, w_out, b_out, gain_two, shift_two, w_up, b_up, w_down, b_down = (
        weights
    )
    (
        layer_in,
        normed,
        qkv_rows,
        log_total,
        mixed_heads,
        hidden,
        squeezed,
        up_rows,
        active,
        result,
    ) = saved
    row_count = layer_in.shape[0]
    grad_attn = grad_hidden.astype(jnp.bfloat16)
    grad_w_out = inner_rows(mixed_heads, grad_attn)
    grad_b_out = jnp.sum(grad_attn.astype(jnp.float32), axis=0)
    grad_mixed = times_transpose(grad_attn, w_out).astype(jnp.bfloat16)
    queries, key_rows, value_rows = split_heads(qkv_rows)
    grad_mixed = grad_mixed.reshape(queries.shape)
    softmax_out = jnp.exp(head_scores(qkv_rows, crop_rows) - log_total)
    grad_soft = jnp.einsum(
        "qhd,khd->hqk", grad_mixed, value_rows, preferred_element_type=jnp.float32
    )
    grad_values = jnp.einsum(
        "hqk,qhd->khd",
        softmax_out.astype(jnp.bfloat16),
        grad_mixed,
        preferred_element_type=jnp.float32,
    )
    row_centre = jnp.sum(grad_soft * softmax_out, axis=-1, keepdims=True)
    grad_scores = (softmax_out * (grad_soft - row_centre)).astype(jnp.bfloat16)
    grad_queries = jnp.einsum(
        "hqk,khd->qhd", grad_scores, key_rows, preferred_element_type=jnp.float32
    ) * HEAD ** (-0.5)
    grad_keys = jnp.einsum(
        "hqk,qhd->khd", grad_scores, queries, preferred_element_type=jnp.float32
    ) * HEAD ** (-0.5)
    grad_qkv = jnp.concatenate(
        [
            grad_queries.reshape(row_count, -1),
            grad_keys.reshape(row_count, -1),
            grad_values.reshape(row_count, -1),
        ],
        axis=1,
    ).astype(jnp.bfloat16)
    grad_w_qkv = inner_rows(normed, grad_qkv)
    grad_normed = times_transpose(grad_qkv, w_qkv)
    first_value, first_pull = jax.vjp(
        norm_rows, layer_in, gain_one.astype(jnp.float32), shift_one.astype(jnp.float32)
    )
    grad_in, grad_gain_one, grad_shift_one = first_pull(grad_normed)
    return (
        grad_hidden + grad_in,
        (grad_gain_one, grad_shift_one, grad_w_qkv, grad_w_out, grad_b_out),
    )


def local(
    block_input,
    crop_ids,
    out_grad,
    norm1_gain,
    norm1_shift,
    w_qkv,
    w_out,
    b_out,
    norm2_gain,
    norm2_shift,
    w_up,
    b_up,
    w_down,
    b_down,
):
    is_first = lax.axis_index("section") == 0
    shards = (
        norm1_gain,
        norm1_shift,
        w_qkv,
        w_out,
        b_out,
        norm2_gain,
        norm2_shift,
        w_up,
        b_up,
        w_down,
        b_down,
    )
    gathered = (
        lax.all_gather(shards[0], "dp", axis=1, tiled=True),
        lax.all_gather(shards[1], "dp", axis=1, tiled=True),
        lax.all_gather(shards[2], "dp", axis=1, tiled=True),
        lax.all_gather(shards[3], "dp", axis=1, tiled=True),
        lax.all_gather(shards[4], "dp", axis=1, tiled=True),
        lax.all_gather(shards[5], "dp", axis=1, tiled=True),
        lax.all_gather(shards[6], "dp", axis=1, tiled=True),
        lax.all_gather(shards[7], "dp", axis=1, tiled=True),
        lax.all_gather(shards[8], "dp", axis=1, tiled=True),
        lax.all_gather(shards[9], "dp", axis=1, tiled=True),
        lax.all_gather(shards[10], "dp", axis=1, tiled=True),
    )
    weights = tuple((item[0] for item in gathered))
    micro_count = block_input.shape[0]

    def pick(upper, lower):
        return jax.tree.map(
            lambda later, earlier: jnp.where(is_first, earlier, later), upper, lower
        )

    incoming = jnp.zeros(block_input.shape[1:], jnp.bfloat16)
    records = []
    kept_saved = []
    forward_rows = []
    for step_index in range(micro_count + 1):
        own_rows = block_input[min(step_index, micro_count - 1)]
        source = jnp.where(is_first, own_rows, incoming)
        crop_rows = jnp.where(
            is_first, crop_ids[min(step_index, micro_count - 1)], crop_ids[max(step_index - 1, 0)]
        )
        saved = forward_layer(source.astype(jnp.float32), crop_rows, weights)
        sent_rows = saved[-1].astype(jnp.bfloat16)
        forward_rows.append(sent_rows)
        records.append((source, crop_rows))
        kept_saved.append(saved)
        if step_index < micro_count:
            incoming = passed_along(sent_rows, "section", 1)
    layer_outputs = jnp.where(
        is_first, jnp.stack(forward_rows[:micro_count]), jnp.stack(forward_rows[1:])
    )
    totals = jax.tree.map(lambda item: jnp.zeros(item.shape, jnp.float32), weights)
    back_in = jnp.zeros(block_input.shape[1:], jnp.bfloat16)
    backward_rows = []
    for step_index in range(micro_count + 1):
        late_tick = min(step_index + 1, micro_count)
        early_tick = max(step_index - 1, 0)
        source, crop_rows = pick(records[late_tick], records[early_tick])
        saved = pick(kept_saved[late_tick], kept_saved[early_tick])
        if step_index < micro_count:
            last_grad = out_grad[step_index]
        else:
            last_grad = jnp.zeros_like(out_grad[0])
        cotangent = jnp.where(is_first, back_in, last_grad)
        grad_hidden, feed_grads = backward_feed(cotangent.astype(jnp.float32), saved, weights)
        feed_totals = tuple((left + right for left, right in zip(totals[5:], feed_grads)))
        grad_in, attend_grads = backward_attend(grad_hidden, saved, crop_rows, weights)
        attend_totals = tuple((left + right for left, right in zip(totals[:5], attend_grads)))
        totals = attend_totals + feed_totals
        sent_grad = grad_in.astype(jnp.bfloat16)
        backward_rows.append(sent_grad)
        if step_index < micro_count:
            back_in = passed_along(sent_grad, "section", -1)
    input_grads = jnp.where(
        is_first, jnp.stack(backward_rows[1:]), jnp.stack(backward_rows[:micro_count])
    )
    summed = lax.psum_scatter(totals, "dp", scatter_dimension=0, tiled=True)
    outputs = tuple((item[None] for item in summed))
    return (layer_outputs[None], input_grads[None]) + outputs


MESH = pl.DeviceIdType.MESH
F = jnp.float32
B = jnp.bfloat16
VECTORS = ("g1", "s1", "bo", "g2", "s2", "bd", "bu")
PARTS = (
    (4, 0, 16, False, False),
    (0, 0, 32, False, False), (0, 32, 32, False, False),
    (1, 0, 64, True, False),
    (2, 0, 32, False, True), (2, 32, 32, True, False),
    (3, 0, 64, False, False), (3, 64, 64, True, False), (3, 128, 64, False, False), (3, 192, 64, True, False),
)
AHEAD = 4
SUMS = (
    (3, 0, 64, True, False),
    (3, 64, 64, False, False),
    (3, 128, 64, True, False),
    (3, 192, 64, False, False),
    (2, 0, 16, True, False),
    (2, 16, 16, False, False),
    (2, 32, 16, True, False),
    (2, 48, 16, False, False),
    (1, 0, 64, False, False),
    (0, 0, 32, True, False),
    (0, 32, 32, False, False),
    (4, 0, 16, False, False),
)
A, O, C, G, DM, DU, DB, DQKV = range(8)


def nt(left, right):
    return lax.dot_general(left, right, (((1,), (1,)), ((), ())), preferred_element_type=F)


def tn(left, right):
    return lax.dot_general(left, right, (((0,), (0,)), ((), ())), preferred_element_type=F)


def nn(left, right):
    return jnp.dot(left, right, preferred_element_type=F)


def tiles(total, step):
    def run(body):
        @pl.loop(0, total // step)
        def _(i):
            body(pl.ds(pl.multiple_of(i * step, step), step))

    return run


def normed(values):
    centred = values - jnp.mean(values, axis=-1, keepdims=True)
    scale = lax.rsqrt(jnp.mean(centred * centred, axis=-1, keepdims=True) + 1e-6)
    return centred * scale, scale


def norm_into(out, rows, gain, shift):
    @tiles(rows.shape[0], 64)
    def _(r):
        hat, _ = normed(rows[r, :].astype(F))
        out[r, :] = (hat * gain[...] + shift[...]).astype(B)


def norm_back(rows, grad, base, out, gain, gain_sum, shift_sum):
    @tiles(rows.shape[0], 64)
    def _(r):
        hat, scale = normed(rows[r, :].astype(F))
        d = grad[r, :]
        gain_sum[...] += jnp.sum(d * hat, axis=0, keepdims=True)
        shift_sum[...] += jnp.sum(d, axis=0, keepdims=True)
        d = d * gain[...]
        mean = jnp.mean(d, axis=-1, keepdims=True)
        along = jnp.mean(d * hat, axis=-1, keepdims=True)
        out[r, :] = (base[r, :].astype(F) + scale * (d - mean - hat * along)).astype(out.dtype)


def halves(pair):
    low = lax.broadcasted_iota(jnp.int32, pair.shape, 1) < HEAD
    zero = jnp.zeros_like(pair)
    return jnp.where(low, pair, zero), jnp.where(low, zero, pair)


def head_pairs(qkv, group, many):
    width = qkv.shape[1] // 3
    for i in range(many):
        for t in range(qkv.shape[0] // 128):
            cols = [pl.ds(pl.multiple_of(g * width + (group * many + i) * 128, 128), 128) for g in range(3)]
            yield pl.ds(t * 128, 128), cols


def softmaxes(items, bias):
    scores = [nt(qh, k) + bias[r, :] for r, q, k in items for qh in halves(q)]
    peaks = [jnp.max(s, axis=-1, keepdims=True) for s in scores]
    raised = [jnp.exp(s - m) for s, m in zip(scores, peaks)]
    totals = [1.0 / jnp.sum(e, axis=-1, keepdims=True) for e in raised]
    return [e * t for e, t in zip(raised, totals)]


def attend(qkv, mixed, bias):
    many = 1024 // qkv.shape[0]

    @pl.loop(0, qkv.shape[1] // 384 // many)
    def _(group):
        where = list(head_pairs(qkv, group, many))
        q, k, v = ([qkv[r, cols[g]] for r, cols in where] for g in range(3))
        q = [item * jnp.asarray(HEAD**-0.5, B) for item in q]
        probs = [p.astype(B) for p in softmaxes([(r, a, b) for (r, _), a, b in zip(where, q, k)], bias)]
        for n, (r, cols) in enumerate(where):
            low, high = halves(v[n])
            mixed[r, cols[0]] = (nn(probs[2 * n], low) + nn(probs[2 * n + 1], high)).astype(B)


def attend_back(qkv, grad, bias):
    many = 1024 // qkv.shape[0]

    def joined(items, axis):
        return jnp.concatenate(items, axis)

    @pl.loop(0, qkv.shape[1] // 384 // many)
    def _(group):
        where = list(head_pairs(qkv, group, many))
        q, k, v = ([qkv[r, cols[g]] for r, cols in where] for g in range(3))
        q = [item * jnp.asarray(HEAD**-0.5, B) for item in q]
        d = [grad[r, cols[0]] for r, cols in where]
        probs = softmaxes([(r, a, b) for (r, _), a, b in zip(where, q, k)], bias)
        slopes = [nt(dh, v[n]) for n in range(len(where)) for dh in halves(d[n])]
        centres = [jnp.sum(g * p, axis=-1, keepdims=True) for g, p in zip(slopes, probs)]
        slopes = [(p * (g - c)).astype(B) for p, g, c in zip(probs, slopes, centres)]
        probs = [p.astype(B) for p in probs]
        for n, (r, cols) in enumerate(where):
            pair = slice(2 * n, 2 * n + 2)
            grad_q = nn(joined(slopes[pair], 1), joined(halves(k[n]), 0))
            qkv[r, cols[0]] = (grad_q * HEAD**-0.5).astype(B)
            qkv[r, cols[1]] = tn(joined(slopes[pair], 0), joined(halves(q[n]), 0)).astype(B)
            qkv[r, cols[2]] = tn(joined(probs[pair], 0), joined(halves(d[n]), 0)).astype(B)


def relay(names, *refs):
    ref = dict(zip(names, refs))
    width = ref["x_own"].shape[1]
    rows = ref["x_own"].shape[0]
    ff = ref["w2"].shape[1]
    shard = [ref[f"own{j}"] for j in range(5)]
    full = [ref[f"w{j}"] for j in range(5)]
    both = [ref[n] for n in ("a", "o", "c", "g", "dm", "du", "db", "dqkv")]
    mine = [b.at[pl.ds(0, 2 * rows)] for b in both]
    theirs = [b.at[pl.ds(2 * rows, 2 * rows)] for b in both]
    vec = {n: ref["v_" + n] for n in VECTORS}
    vsum = {n: ref["d_" + n] for n in VECTORS}
    x, hidden, wide, dmixed, result = (ref[n] for n in ("x", "h", "wide", "do", "y"))
    for name in ("g1", "s1", "g2", "s2"):
        vsum[name][...] = jnp.zeros_like(vsum[name])
    p = lax.axis_index("dp")
    z, y, core = p // 4, (p // 2) % 2, p % 2
    inner = jnp.logical_or(z == 1, z == 2)
    section = lax.axis_index("section")
    zo, zn = jnp.where(z == 1, 0, 3), 3 - z
    zon = 3 - zo
    zi = jnp.where(z == 0, 1, 2)

    def idx(z, y, core):
        return (z * 2 + y) * 2 + core

    sibling, across, other = idx(z, y, 1 - core), idx(z, 1 - y, core), idx(zn, y, core)
    outer_one, inner_one = idx(zo, y, core), idx(zi, y, core)

    def remote(sec, src, dst, send_sem, recv_sem, to):
        return pltpu.make_async_remote_copy(
            src_ref=src, dst_ref=dst, send_sem=send_sem, recv_sem=recv_sem,
            device_id=(sec, to), device_id_type=MESH,
        )

    first = section == 0

    def only(condition):
        return lambda body: pl.when(condition)(body)

    class Flow:
        def __init__(self):
            self.sent = []

        def send(self, src, dst, made, recv_sem, to, sec=section):
            remote(sec, src, dst, made()[1], recv_sem, to).start()
            self.note(made)

        def note(self, made, condition=None):
            self.sent.append((made, condition))

        def arrived(self, dst, recv_sem):
            remote(section, dst, dst, ref["idle_sem"].at[0], recv_sem, sibling).wait_recv()

        def finish(self):
            for made, condition in self.sent:
                def wait():
                    like, send_sem = made()
                    remote(section, like, like, send_sem, ref["idle_sem"].at[0], sibling).wait_send()

                wait() if condition is None else pl.when(condition)(wait)
            self.sent = []

    def piece(k, b):
        j, first, count = PARTS[k][:3]
        size = shard[j].shape[0]
        return full[j].at[pl.ds(pl.multiple_of(b * size + first, count), count)]

    def own_piece(k):
        j, first, count = PARTS[k][:3]
        return shard[j].at[pl.ds(first, count)]

    def own_copy(k):
        return pltpu.make_async_copy(own_piece(k), piece(k, p), ref["ag_local"].at[k])

    def gather_steps(flow, is_inner):
        used = [0] * len(PARTS)

        def send(k, b, to, own=False):
            src = own_piece(k) if own else piece(k, b)
            n = used[k]

            def made():
                return full[PARTS[k][0]].at[pl.ds(0, PARTS[k][2])], ref["ag_send"].at[k, n]

            flow.send(src, piece(k, b), made, ref["ag_recv"].at[k, b], to)
            used[k] += 1

        def take(k, b, *to):
            flow.arrived(piece(k, b), ref["ag_recv"].at[k, b])
            for target in to:
                send(k, b, target)

        def begin(k):
            if is_inner:
                for to in (outer_one if PARTS[k][4] else across, other, sibling):
                    send(k, p, to, own=True)
                own_copy(k).start()
            else:
                send(k, p, inner_one, own=True)
                send(k, p, across, own=True)

        def early(k):
            take(k, idx(zo, y, core), other, sibling)
            take(k, idx(zn, y, core), across, sibling)
            if not PARTS[k][4]:
                take(k, idx(z, 1 - y, core), sibling)

        def late(k):
            by_z = PARTS[k][3]
            take(k, idx(zon, y, core), *((sibling,) if by_z else (across, sibling)))
            take(k, idx(zo, 1 - y, core), *((other, sibling) if by_z else (sibling,)))

        def end(k):
            if PARTS[k][4]:
                take(k, idx(z, 1 - y, core), sibling)
            take(k, idx(zn, 1 - y, core), sibling)
            take(k, idx(zon, 1 - y, core), sibling)

        def step(k):
            if k == 0:
                for first in range(AHEAD):
                    begin(first)
            if k + AHEAD < len(PARTS):
                begin(k + AHEAD)
            if is_inner:
                for stage, n in ((early, k), (late, k - 1), (end, k - 2)):
                    if 0 <= n < len(PARTS):
                        stage(n)
            else:
                take(k, across, inner_one)
                if PARTS[k][4]:
                    take(k, idx(zi, y, core), across)
                if k and PARTS[k - 1][4]:
                    take(k - 1, idx(zi, 1 - y, core), inner_one)

        return step

    def gathered(flow, j):
        for k, part in enumerate(PARTS):
            if part[0] == j:
                own_copy(k).wait()
                for b in range(8):
                    block = 2 * b + 1 - core
                    flow.arrived(piece(k, block), ref["ag_recv"].at[k, block])

    def write_small():
        stage = ref["stage"]
        stage[...] = jnp.zeros_like(stage)
        for c in range(2):
            @pl.when(core == c)
            def _():
                for n, name in enumerate(VECTORS[:6]):
                    stage[n : n + 1, 64 * c : 64 * c + 64] = ref["in_" + name][...].astype(F)
        for n in range(2):
            stage[6 + n : 7 + n, :] = ref["in_bu"][:, 128 * n : 128 * n + 128].astype(F)
        shard[4][...] = stage[...].astype(B)

    def write_crops():
        for m in range(2):
            ref["crops"][0:1, 64 * m : 64 * m + 64] = (ref["in_crop"][m : m + 1, :] + 1024 * m).astype(F)

    def write_bias(crops, first):
        along = jnp.broadcast_to(crops[0:1, :], (rows, rows))
        ref["bias"][pl.ds(first, rows), :] = jnp.where(along == along.T, 0.0, -1e30)

    def spread_vectors():
        for i in range(8):
            low = full[4][pl.ds(32 * i, 16), :].astype(F)
            high = full[4][pl.ds(32 * i + 16, 16), :].astype(F)
            joined = low + high
            for n, name in enumerate(VECTORS[:6]):
                vec[name][:, pl.ds(128 * i, 128)] = joined[n : n + 1]
            for n, part in enumerate((low[6:7], low[7:8], high[6:7], high[7:8])):
                vec["bu"][:, pl.ds(512 * i + 128 * n, 128)] = part

    def exchange(flow, which):
        pair = ref["act_send"].at[which], ref["act_recv"].at[which]
        remote(section, mine[which], theirs[which], *pair, sibling).start()

    def exchanged(flow, *which):
        for w in which:
            flow.arrived(theirs[w], ref["act_recv"].at[w])

    def forward_attend(r):
        norm_into(mine[A].at[r], x.at[r], vec["g1"], vec["s1"])

        @tiles(3 * width, 1536)
        def _(c):
            mine[DQKV][r, c] = nn(mine[A][r, :], full[0][:, c]).astype(B)

        attend(mine[DQKV].at[r], mine[O].at[r], ref["bias"].at[r])

    def forward_out(r):
        hidden[r, :] = x[r, :].astype(F) + nn(mine[O][r, :], full[1][...]) + vec["bo"][...]
        norm_into(mine[C].at[r], hidden.at[r], vec["g2"], vec["s2"])

    def forward_up(r):
        @tiles(ff, 1024)
        def _(c):
            u = nn(mine[C][r, :], full[2][:, c]) + vec["bu"][:, c]
            phi = 0.5 + 0.5 * lax.erf(u * 0.5**0.5)
            mine[G][r, c] = (u * phi).astype(B)
            mine[DU][r, c] = (phi + u * (jnp.exp(-0.5 * u * u) * (0.5 / jnp.pi) ** 0.5)).astype(B)

    def forward_down(r):
        result[r, :] = (hidden[r, :] + nn(mine[G][r, :], full[3][...]) + vec["bd"][...]).astype(B)

    def backward_du():
        vsum["bd"][...] = jnp.sum(mine[DM][...].astype(F), axis=0, keepdims=True)

        @tiles(ff, 1024)
        def _(c):
            du = (nt(mine[DM][...], full[3][c, :]) * mine[DU][:, c].astype(F)).astype(B)
            mine[DU][:, c] = du
            vsum["bu"][:, c] = jnp.sum(du.astype(F), axis=0, keepdims=True)

    def backward_dh():
        wide[...] = nt(mine[DU][...], full[2][...])
        norm_back(hidden, wide, mine[DM], hidden, vec["g2"], vsum["g2"], vsum["s2"])
        mine[DB][...] = hidden[...].astype(B)
        vsum["bo"][...] = jnp.sum(mine[DB][...].astype(F), axis=0, keepdims=True)

    def backward_attend():
        dmixed[...] = nt(mine[DB][...], full[1][...]).astype(B)
        attend_back(mine[DQKV], dmixed, ref["bias"])

    def backward_da():
        wide[...] = nt(mine[DQKV][...], full[0][...])

    def backward_dx(r):
        norm_back(x.at[r], wide.at[r], hidden.at[r], x.at[r], vec["g1"], vsum["g1"], vsum["s1"])

    def packed(which):
        src, out = both[which], ref["packed"]
        for i in range(width // 256):
            first = src[:, pl.ds(256 * i, 128)].astype(F)
            second = src[:, pl.ds(256 * i + 128, 128)].astype(F)
            low = lax.broadcasted_iota(jnp.int32, first.shape, 1) < HEAD
            even = jnp.where(low, first, pltpu.roll(second, HEAD, 1))
            odd = jnp.where(low, pltpu.roll(first, HEAD, 1), second)
            out[pl.ds(128 * i, 128), :] = jnp.where(core == 0, even, odd).T.astype(B)

    def grad_down():
        size = shard[3].shape[0]
        for o in range(8):
            c = pl.ds(pl.multiple_of(size * (2 * o + core), size), size)
            full[3][pl.ds(size * o, size), :] = tn(both[G][:, c], both[DM][...]).astype(B)

    def grad_of(j, left, right):
        packed(left)

        @tiles(both[right].shape[1], 512)
        def _(c):
            full[j][pl.ds(0, 8 * shard[j].shape[0]), c] = nn(ref["packed"][...], both[right][:, c]).astype(B)

    def grad_vectors():
        for o in range(8):
            for n, name in enumerate(VECTORS[:6]):
                ref["vp"][pl.ds(16 * o + n, 1), :] = vsum[name][:, pl.ds(128 * o, 128)]
            for n in range(4):
                ref["vp"][pl.ds(16 * o + 6 + n, 1), :] = vsum["bu"][:, pl.ds(512 * o + 128 * n, 128)]
            ref["vp"][pl.ds(16 * o + 10, 6), :] = jnp.zeros((6, 128), F)

    partial = [full[0], full[1], full[2], full[3], ref["vp"]]
    sums = [ref[f"out{j}"] for j in range(4)] + [ref["vs"]]
    NEAR, OWN, ALT, INNER, OUTER = range(5)
    slots = [[ref[f"r{s}_{j}"] for j in range(5)] for s in range(5)]

    def reducer(flow):
        def slot(s, k):
            j, first, count = SUMS[k][:3]
            return slots[s][j].at[pl.ds(first, count)]

        def part(k, zz, yy):
            j, first, count = SUMS[k][:3]
            size = partial[j].shape[0] // 8 if j == 4 else shard[j].shape[0]
            return partial[j].at[pl.ds(pl.multiple_of((zz * 2 + yy) * size + first, count), count)]

        def send(k, n, src, s, to):
            def made():
                return slot(s, k), ref["rs_send"].at[k, n]

            flow.send(src, slot(s, k), made, ref["rs_recv"].at[k, s], to)

        def arrived(k, s):
            flow.arrived(slot(s, k), ref["rs_recv"].at[k, s])

        def add(k, dst, *more):
            total = dst[...].astype(F)
            for s in more:
                total = total + slot(s, k)[...].astype(F)
            return total

        def issue(k):
            if SUMS[k][3]:
                send(k, 4, part(k, zon, y), OUTER, other)
                send(k, 1, part(k, zon, 1 - y), ALT, other)
            else:
                send(k, 1, part(k, zon, 1 - y), ALT, across)
                send(k, 6, part(k, zo, 1 - y), INNER, outer_one)

        def issue_near(k):
            send(k, 0, part(k, zn, 1 - y), NEAR, across)

        def issue_own(k):
            if SUMS[k][4]:
                send(k, 2, part(k, z, 1 - y), NEAR, outer_one)
            else:
                send(k, 2, part(k, z, 1 - y), OWN, across)

        def far_on(k):
            if not SUMS[k][3]:
                dst = part(k, zon, y)
                arrived(k, ALT)
                dst[...] = add(k, dst, ALT).astype(dst.dtype)
                send(k, 4, dst, OUTER, other)

        def near_on(k):
            dst = part(k, zn, y)
            arrived(k, NEAR)
            dst[...] = add(k, dst, NEAR).astype(dst.dtype)
            send(k, 3, dst, INNER, other)

        def outward(k):
            dst = part(k, zo, y)
            arrived(k, OUTER)
            dst[...] = add(k, dst, OUTER).astype(dst.dtype)
            send(k, 5, dst, OUTER, outer_one)
            if SUMS[k][3]:
                dst = part(k, zo, 1 - y)
                arrived(k, ALT)
                dst[...] = add(k, dst, ALT).astype(dst.dtype)
                send(k, 6, dst, INNER, outer_one)

        def last(k):
            arrived(k, INNER)
            arrived(k, OWN)
            j, first, count = SUMS[k][:3]
            sums[j][pl.ds(first, count), :] = add(k, part(k, z, y), OWN, INNER)

        def pass_on(k):
            arrived(k, INNER)
            send(k, 0, slot(INNER, k), OWN, across)

        def around(k, end):
            arrived(k, ALT if end else NEAR)
            if end:
                send(k, 2, slot(ALT, k), OWN, inner_one)
            else:
                send(k, 1, slot(NEAR, k), ALT, across)

        def collect(k):
            arrived(k, OUTER)
            arrived(k, OWN)
            j, first, count = SUMS[k][:3]
            sums[j][pl.ds(first, count), :] = slot(OUTER, k)[...].astype(F) + slot(OWN, k)[...].astype(F)

        def join_vectors():
            made = lambda: (ref["vs"], ref["vec_sem"].at[0])
            flow.send(ref["vs"], ref["vt"], made, ref["vec_sem"].at[1], sibling)
            flow.arrived(ref["vt"], ref["vec_sem"].at[1])
            ref["out4"][...] = ref["vs"][...] + ref["vt"][...]

        inner_steps = issue, issue_near, issue_own, far_on, near_on, outward, last
        return inner_steps, (pass_on, around, collect), join_vectors

    def hand_out(flow, src, out, n):
        made = lambda: (out, ref["res_send"].at[n])
        flow.send(src.at[pl.ds(rows, rows)], out, made, ref["res_recv"].at[n], outer_one)
        out[...] = src[pl.ds(0, rows), :]

    every = pl.ds(0, 2 * rows)
    near, far = pl.ds(0, rows), pl.ds(rows, rows)

    def half(h):
        return pl.ds(pl.multiple_of(h * rows, rows), rows)

    direct = pl.ds(rows, rows // 2)
    detours = [pl.ds(rows + rows // 4 * n, rows // 4) for n in (2, 3)]

    def cross_far(src, dst, sec, kind, between=lambda: None):
        for n, r in enumerate(detours):
            pair = ref["way_send"].at[kind + n], ref["way_recv"].at[kind + n]
            remote(section, src.at[r], dst.at[r], *pair, outer_one).start()
        between()
        pair = ref["x_send"].at[kind + 1], ref["x_recv"].at[kind + 1]
        remote(sec, src.at[direct], dst.at[direct], *pair, p).start()

    def crossed_far(flow, dst, kind):
        flow.arrived(dst.at[direct], ref["x_recv"].at[kind + 1])
        for n, r in enumerate(detours):
            flow.arrived(dst.at[r], ref["way_recv"].at[kind + n])

    def note_crossing(flow, kind, condition):
        flow.note(lambda: (x.at[near], ref["x_send"].at[kind]), condition)
        flow.note(lambda: (x.at[direct], ref["x_send"].at[kind + 1]), condition)
        for n in range(2):
            flow.note(lambda n=n: (x.at[detours[0]], ref["way_send"].at[kind + n]), condition)

    def detour(flow, dst, sec, kind):
        for n, r in enumerate(detours):
            pair = ref["way_send"].at[kind + n], ref["way_recv"].at[kind + n]
            flow.arrived(dst.at[r], pair[1])
            pl.when(section != sec)(remote(sec, dst.at[r], dst.at[r], *pair, p).start)
            pl.when(section == sec)(remote(sec, dst.at[r], dst.at[r], *pair, inner_one).start)
            flow.note(lambda n=n: (x.at[detours[0]], ref["way_send"].at[kind + n]))

    def inner_program():
        flow = Flow()
        step = gather_steps(flow, True)
        inner_steps, _, join_vectors = reducer(flow)
        issue, issue_near, issue_own, far_on, near_on, outward, last = inner_steps
        step(0)
        own = [
            pltpu.make_async_copy(src, dst.at[near], ref["tok_local"].at[0])
            for src, dst in ((ref["x_own"], x), (ref["dy_own"], mine[DM]))
        ]
        for n, copy in enumerate(own):
            pl.when(section == n)(copy.start)
        write_bias(ref["crops"], 0)

        def tokens():
            for n, (copy, dst) in enumerate(zip(own, (x, mine[DM]))):
                @pl.when(section == n)
                def _():
                    copy.wait()
                    flow.arrived(dst.at[far], ref["tok_recv"].at[1])
            flow.arrived(ref["far_crops"], ref["tok_recv"].at[0])
            write_bias(ref["far_crops"], rows)

        def steps(begin, end):
            for k in range(begin, end):
                step(k)

        @pl.loop(0, 2)
        def _(turn):
            gathering, active = only(turn == 0), only(section == turn)

            @gathering
            def _():
                steps(1, 6)
                gathered(flow, 4)
                spread_vectors()
                tokens()
                gathered(flow, 0)

            @active
            def _():
                @pl.loop(0, 2)
                def _(h):
                    @pl.when(jnp.logical_and(h == 0, section == 1))
                    def _():
                        flow.arrived(x.at[near], ref["x_recv"].at[0])

                    @pl.when(jnp.logical_and(h == 1, section == 1))
                    def _():
                        crossed_far(flow, x, 0)

                    forward_attend(half(h))

            @gathering
            def _():
                steps(6, 7)
                gathered(flow, 1)

            @active
            def _():
                forward_out(every)

            @gathering
            def _():
                steps(7, 9)
                gathered(flow, 2)

            @active
            def _():
                forward_up(every)

            @gathering
            def _():
                steps(9, len(PARTS) + 2)
                gathered(flow, 3)

            @active
            def _():
                forward_down(every)

        @pl.when(first)
        def _():
            cross_far(
                result, x, 1, 0,
                remote(1, result.at[near], x.at[near], ref["x_send"].at[0], ref["x_recv"].at[0], p).start,
            )

        note_crossing(flow, 0, first)
        flow.finish()
        for which in (G, C, O, A):
            exchange(flow, which)
        hand_out(flow, result, ref["y_out"], 0)

        def exchange_when(condition, *which):
            @pl.when(condition)
            def _():
                for w in which:
                    exchange(flow, w)

        @pl.loop(0, 2)
        def _(turn):
            main, grads = only(turn == 0), only(section == turn)
            leading = jnp.logical_and(turn == 0, first)
            trailing = jnp.logical_and(turn == 1, section == 1)

            @pl.when(leading)
            def _():
                flow.arrived(mine[DM].at[near], ref["x_recv"].at[2])
                crossed_far(flow, mine[DM], 2)

            exchange_when(turn == 0, DM)
            main(backward_du)
            exchange_when(leading, DU)
            exchange_when(trailing, DU, DB, DQKV)

            @grads
            def _():
                exchanged(flow, G, DM)
                grad_down()
                issue(0)
                issue_near(0)
                issue(1)
                issue_near(1)

            main(backward_dh)
            exchange_when(leading, DB)

            @grads
            def _():
                issue(2)
                issue_near(2)
                issue(3)
                exchanged(flow, C, DU)
                grad_of(2, C, DU)

            main(backward_attend)
            exchange_when(leading, DQKV)

            @grads
            def _():
                for k in range(4, 8):
                    issue(k)
                issue_near(3)
                exchanged(flow, O, DB)
                grad_of(1, O, DB)
                issue(8)

            main(backward_da)

            @grads
            def _():
                far_on(1)
                near_on(0)
                exchanged(flow, A, DQKV)
                grad_of(0, A, DQKV)
                issue(9)
                issue(10)
                issue_near(4)

            @main
            def _():
                @pl.loop(0, 2)
                def _(h):
                    backward_dx(half(1 - h))

                    @pl.when(jnp.logical_and(h == 0, section == 1))
                    def _():
                        cross_far(x, mine[DM], 0, 2)

                    @pl.when(jnp.logical_and(h == 1, section == 1))
                    def _():
                        to = mine[DM].at[near]
                        remote(0, x.at[near], to, ref["x_send"].at[2], ref["x_recv"].at[2], p).start()

        note_crossing(flow, 2, section == 1)
        for which in range(8):
            flow.note(lambda w=which: (mine[w], ref["act_send"].at[w]))
        grad_vectors()
        issue(11)
        hand_out(flow, x, ref["dx_out"], 1)
        count = len(SUMS)
        for k in range(2, count + 4):
            plan = ((far_on, [2 * k - 2, 2 * k - 1]), (issue_near, [k + 3]), (near_on, [k - 1]), (outward, [k - 3] if k < 8 else [2 * k - 11, 2 * k - 10]), (issue_own, [k - 4]))
            for turn, which in plan:
                for n in which:
                    if 0 <= n < count:
                        turn(n)
        for k in range(count):
            last(k)
        join_vectors()
        flow.finish()

    def outer_program():
        flow = Flow()
        step = gather_steps(flow, False)
        _, (pass_on, around, collect), join_vectors = reducer(flow)
        for k in range(len(PARTS)):
            step(k)
            if k == 1:
                made = lambda: (ref["crops"], ref["tok_send"].at[0])
                flow.send(ref["crops"], ref["far_crops"], made, ref["tok_recv"].at[0], inner_one)
                for n, (src, dst) in enumerate(((ref["x_own"], x), (ref["dy_own"], mine[DM]))):
                    pl.when(section == n)(
                        remote(section, src, dst.at[far], ref["tok_send"].at[1], ref["tok_recv"].at[1], inner_one).start
                    )
                flow.note(lambda: (x.at[far], ref["tok_send"].at[1]))
        detour(flow, x, 1, 0)
        detour(flow, mine[DM], 0, 2)
        for k in range(len(SUMS)):
            for turn, n in ((pass_on, k), (collect, k - 1)):
                if 0 <= n:
                    turn(n)
            for end in range(2):
                n = k - 3 - end
                if 0 <= n < len(SUMS) and SUMS[n][4]:
                    around(n, end)
        collect(len(SUMS) - 1)
        join_vectors()
        flow.arrived(ref["y_out"], ref["res_recv"].at[0])
        flow.arrived(ref["dx_out"], ref["res_recv"].at[1])
        flow.finish()

    write_small()
    write_crops()
    pl.when(inner)(inner_program)
    pl.when(jnp.logical_not(inner))(outer_program)


def relay_call(x_own, dy_own, small, shards, dp):
    rows, width = x_own.shape
    ff = shards[2].shape[1]
    count = 2 * rows
    shapes = [item.shape for item in shards] + [(16, 128)]
    inputs = {"x_own": x_own, "dy_own": dy_own}
    inputs.update({f"own{j}": item for j, item in enumerate(shards)})
    outputs = {"y_out": ((rows, width), B), "dx_out": ((rows, width), B)}
    outputs.update({f"out{j}": (item.shape, F) for j, item in enumerate(shards)})
    outputs["out4"] = ((16, 128), F)
    scratch = {f"w{j}": ((dp * shape[0], shape[1]), B) for j, shape in enumerate(shapes)}
    for name, cols in zip(("a", "o", "c", "g", "dm", "du", "db", "dqkv"), (1, 1, 1, 0, 1, 0, 1, 3)):
        scratch[name] = ((2 * count, cols * width or ff), B)
    scratch.update(x=((count, width), B), h=((count, width), F), wide=((count, width), F), do=((count, width), B))
    scratch.update(y=((count, width), B), bias=((count, 128), F), packed=((width // 2, 2 * count), B))
    for name in VECTORS:
        scratch["v_" + name] = scratch["d_" + name] = ((1, ff if name == "bu" else width), F)
    scratch.update(vp=((128, 128), F), vs=((16, 128), F), vt=((16, 128), F), stage=((16, 128), F), crops=((8, 128), F), far_crops=((8, 128), F), own4=((16, 128), B))
    for s in range(5):
        for j, shape in enumerate(shapes):
            scratch[f"r{s}_{j}"] = (shape, F if j == 4 else B)
    sems = dict(
        ag_send=(len(PARTS), 16), ag_recv=(len(PARTS), dp), ag_local=(len(PARTS),), tok_local=(1,), tok_send=(2,),
        tok_recv=(2,), x_send=(4,), x_recv=(4,), way_send=(4,), way_recv=(4,), act_send=(8,), act_recv=(8,), res_send=(2,), res_recv=(2,),
        rs_send=(len(SUMS), 7), rs_recv=(len(SUMS), 5), vec_sem=(2,), idle_sem=(1,),
    )
    names = [*inputs, *small, *outputs, *scratch, *sems]
    whole, anywhere = pl.BlockSpec(memory_space=pltpu.VMEM), pl.BlockSpec(memory_space=pl.ANY)
    return pl.pallas_call(
        functools.partial(relay, names),
        out_shape=[jax.ShapeDtypeStruct(*item) for item in outputs.values()],
        in_specs=[anywhere] * len(inputs) + [whole] * len(small),
        out_specs=[whole] * len(outputs),
        scratch_shapes=[pltpu.VMEM(*item) for item in scratch.values()]
        + [pltpu.SemaphoreType.DMA(item) for item in sems.values()],
        compiler_params=pltpu.CompilerParams(has_side_effects=True, vmem_limit_bytes=62 << 20),
        name="relay",
    )(*inputs.values(), *small.values())


def hand_over(*refs):
    rows, vectors, out, small = refs[:6], refs[6], refs[7:13], refs[13:20]
    for n in range(2):
        size = out[n].shape[2]
        for m in range(out[n].shape[1]):
            out[n][0, m] = rows[n][pl.ds(m * size, size), :]
    for n in range(2, 6):
        out[n][0] = rows[n][...]
    core = lax.axis_index("dp") % 2
    for c in range(2):
        @pl.when(core == c)
        def _():
            for n in range(6):
                small[n][...] = vectors[n : n + 1, 64 * c : 64 * c + 64]
            small[6][...] = vectors[6 + 2 * c : 8 + 2 * c, :]


def middle(
    block_input, crop_ids, out_grad, norm1_gain, norm1_shift, w_qkv, w_out, b_out,
    norm2_gain, norm2_shift, w_up, b_up, w_down, b_down,
):
    micro, rows, width = block_input.shape
    small = dict(zip(VECTORS, (norm1_gain, norm1_shift, b_out, norm2_gain, norm2_shift, b_down, b_up)))
    small = {"in_" + name: item for name, item in small.items()} | {"in_crop": crop_ids}
    got = relay_call(
        block_input.reshape(-1, width), out_grad.reshape(-1, width), small,
        (w_qkv[0], w_out[0], w_up[0], w_down[0]), lax.axis_size("dp"),
    )
    whole = pl.BlockSpec(memory_space=pltpu.VMEM)
    shapes = [((1, micro, rows, width), B)] * 2 + [((1,) + item.shape, F) for item in got[2:6]]
    shapes += [((1, 64), F)] * 6 + [((2, 128), F)]
    y, dx, g_qkv, g_out, g_up, g_down, g1, s1, bo, g2, s2, bd, bu = pl.pallas_call(
        hand_over,
        out_shape=[jax.ShapeDtypeStruct(*item) for item in shapes],
        in_specs=[whole] * 7,
        out_specs=[whole] * 13,
        compiler_params=pltpu.CompilerParams(vmem_limit_bytes=62 << 20),
        name="hand_over",
    )(*got)
    return y, dx, g1, s1, g_qkv, g_out, bo, g2, s2, g_up, bu.reshape(1, -1), g_down, bd


def solution(mesh):
    in_specs = (
        P(None, "dp", None),
        P(None, "dp"),
        P(None, "dp", None),
        P("section", "dp"),
        P("section", "dp"),
        P("section", "dp", None),
        P("section", "dp", None),
        P("section", "dp"),
        P("section", "dp"),
        P("section", "dp"),
        P("section", "dp", None),
        P("section", "dp"),
        P("section", "dp", None),
        P("section", "dp"),
    )
    out_specs = (
        P("section", None, "dp", None),
        P("section", None, "dp", None),
        P("section", "dp"),
        P("section", "dp"),
        P("section", "dp", None),
        P("section", "dp", None),
        P("section", "dp"),
        P("section", "dp"),
        P("section", "dp"),
        P("section", "dp", None),
        P("section", "dp"),
        P("section", "dp", None),
        P("section", "dp"),
    )
    fits = mesh.shape["dp"] == 16 and mesh.shape["section"] == 2
    return jax.shard_map(middle if fits else local, mesh=mesh, in_specs=in_specs, out_specs=out_specs, check_vma=False)
```

```python
import functools

import jax
import jax.numpy as jnp
from jax import lax
from jax.experimental import pallas as pl
from jax.experimental.pallas import tpu as pltpu
from jax.sharding import PartitionSpec as P

HEAD = 64


def passed_along(x, axis, by):
    devices = lax.axis_size(axis)
    pairs = [(i, i + by) for i in range(devices) if 0 <= i + by < devices]
    return lax.ppermute(x, axis, pairs)


def norm_rows(values, gain, shift):
    centred = values - jnp.mean(values, axis=-1, keepdims=True)
    spread = jnp.mean(centred * centred, axis=-1, keepdims=True)
    return centred * lax.rsqrt(spread + 1e-06) * gain + shift


def gelu_exact(values):
    return jax.nn.gelu(values, approximate=False)


def inner_rows(left, right):
    return lax.dot_general(
        left, right, (((0,), (0,)), ((), ())), preferred_element_type=jnp.float32
    )


def times_transpose(left, right):
    return lax.dot_general(
        left, right, (((1,), (1,)), ((), ())), preferred_element_type=jnp.float32
    )


def split_heads(qkv_rows):
    model_width = qkv_rows.shape[1] // 3
    head_count = model_width // HEAD
    queries = qkv_rows[:, :model_width].reshape(-1, head_count, HEAD)
    key_rows = qkv_rows[:, model_width : 2 * model_width].reshape(-1, head_count, HEAD)
    value_rows = qkv_rows[:, 2 * model_width :].reshape(-1, head_count, HEAD)
    return (queries, key_rows, value_rows)


def head_scores(qkv_rows, crop_rows):
    queries, key_rows, value_rows = split_heads(qkv_rows)
    scores = jnp.einsum("qhd,khd->hqk", queries, key_rows, preferred_element_type=jnp.float32)
    scores = scores * HEAD ** (-0.5)
    same_crop = crop_rows[:, None] == crop_rows[None, :]
    return jnp.where(same_crop[None], scores, -1e30)


def forward_layer(layer_in, crop_rows, weights):
    gain_one, shift_one, w_qkv, w_out, b_out, gain_two, shift_two, w_up, b_up, w_down, b_down = (
        weights
    )
    row_count = layer_in.shape[0]
    normed = norm_rows(
        layer_in, gain_one.astype(jnp.float32), shift_one.astype(jnp.float32)
    ).astype(jnp.bfloat16)
    qkv_rows = jnp.dot(normed, w_qkv, preferred_element_type=jnp.float32).astype(jnp.bfloat16)
    scores = head_scores(qkv_rows, crop_rows)
    row_peak = jnp.max(scores, axis=-1, keepdims=True)
    log_total = row_peak + jnp.log(jnp.sum(jnp.exp(scores - row_peak), axis=-1, keepdims=True))
    softmax_low = jnp.exp(scores - log_total).astype(jnp.bfloat16)
    queries, key_rows, value_rows = split_heads(qkv_rows)
    mixed_heads = jnp.einsum(
        "hqk,khd->qhd", softmax_low, value_rows, preferred_element_type=jnp.float32
    )
    mixed_heads = mixed_heads.reshape(row_count, -1).astype(jnp.bfloat16)
    hidden = (
        layer_in
        + jnp.dot(mixed_heads, w_out, preferred_element_type=jnp.float32)
        + b_out.astype(jnp.float32)
    )
    squeezed = norm_rows(
        hidden, gain_two.astype(jnp.float32), shift_two.astype(jnp.float32)
    ).astype(jnp.bfloat16)
    up_rows = jnp.dot(squeezed, w_up, preferred_element_type=jnp.float32) + b_up.astype(jnp.float32)
    active = gelu_exact(up_rows).astype(jnp.bfloat16)
    result = (
        hidden
        + jnp.dot(active, w_down, preferred_element_type=jnp.float32)
        + b_down.astype(jnp.float32)
    )
    return (
        layer_in,
        normed,
        qkv_rows,
        log_total,
        mixed_heads,
        hidden,
        squeezed,
        up_rows,
        active,
        result,
    )


def backward_feed(grad_result, saved, weights):
    gain_one, shift_one, w_qkv, w_out, b_out, gain_two, shift_two, w_up, b_up, w_down, b_down = (
        weights
    )
    (
        layer_in,
        normed,
        qkv_rows,
        log_total,
        mixed_heads,
        hidden,
        squeezed,
        up_rows,
        active,
        result,
    ) = saved
    grad_branch = grad_result.astype(jnp.bfloat16)
    grad_w_down = inner_rows(active, grad_branch)
    grad_b_down = jnp.sum(grad_branch.astype(jnp.float32), axis=0)
    grad_active = times_transpose(grad_branch, w_down)
    gelu_value, gelu_pull = jax.vjp(gelu_exact, up_rows)
    grad_up = gelu_pull(grad_active)[0].astype(jnp.bfloat16)
    grad_w_up = inner_rows(squeezed, grad_up)
    grad_b_up = jnp.sum(grad_up.astype(jnp.float32), axis=0)
    grad_squeezed = times_transpose(grad_up, w_up)
    norm_value, norm_pull = jax.vjp(
        norm_rows, hidden, gain_two.astype(jnp.float32), shift_two.astype(jnp.float32)
    )
    grad_hid, grad_gain_two, grad_shift_two = norm_pull(grad_squeezed)
    grad_hidden = grad_result + grad_hid
    return (
        grad_hidden,
        (grad_gain_two, grad_shift_two, grad_w_up, grad_b_up, grad_w_down, grad_b_down),
    )


def backward_attend(grad_hidden, saved, crop_rows, weights):
    gain_one, shift_one, w_qkv, w_out, b_out, gain_two, shift_two, w_up, b_up, w_down, b_down = (
        weights
    )
    (
        layer_in,
        normed,
        qkv_rows,
        log_total,
        mixed_heads,
        hidden,
        squeezed,
        up_rows,
        active,
        result,
    ) = saved
    row_count = layer_in.shape[0]
    grad_attn = grad_hidden.astype(jnp.bfloat16)
    grad_w_out = inner_rows(mixed_heads, grad_attn)
    grad_b_out = jnp.sum(grad_attn.astype(jnp.float32), axis=0)
    grad_mixed = times_transpose(grad_attn, w_out).astype(jnp.bfloat16)
    queries, key_rows, value_rows = split_heads(qkv_rows)
    grad_mixed = grad_mixed.reshape(queries.shape)
    softmax_out = jnp.exp(head_scores(qkv_rows, crop_rows) - log_total)
    grad_soft = jnp.einsum(
        "qhd,khd->hqk", grad_mixed, value_rows, preferred_element_type=jnp.float32
    )
    grad_values = jnp.einsum(
        "hqk,qhd->khd",
        softmax_out.astype(jnp.bfloat16),
        grad_mixed,
        preferred_element_type=jnp.float32,
    )
    row_centre = jnp.sum(grad_soft * softmax_out, axis=-1, keepdims=True)
    grad_scores = (softmax_out * (grad_soft - row_centre)).astype(jnp.bfloat16)
    grad_queries = jnp.einsum(
        "hqk,khd->qhd", grad_scores, key_rows, preferred_element_type=jnp.float32
    ) * HEAD ** (-0.5)
    grad_keys = jnp.einsum(
        "hqk,qhd->khd", grad_scores, queries, preferred_element_type=jnp.float32
    ) * HEAD ** (-0.5)
    grad_qkv = jnp.concatenate(
        [
            grad_queries.reshape(row_count, -1),
            grad_keys.reshape(row_count, -1),
            grad_values.reshape(row_count, -1),
        ],
        axis=1,
    ).astype(jnp.bfloat16)
    grad_w_qkv = inner_rows(normed, grad_qkv)
    grad_normed = times_transpose(grad_qkv, w_qkv)
    first_value, first_pull = jax.vjp(
        norm_rows, layer_in, gain_one.astype(jnp.float32), shift_one.astype(jnp.float32)
    )
    grad_in, grad_gain_one, grad_shift_one = first_pull(grad_normed)
    return (
        grad_hidden + grad_in,
        (grad_gain_one, grad_shift_one, grad_w_qkv, grad_w_out, grad_b_out),
    )


def local(
    block_input,
    crop_ids,
    out_grad,
    norm1_gain,
    norm1_shift,
    w_qkv,
    w_out,
    b_out,
    norm2_gain,
    norm2_shift,
    w_up,
    b_up,
    w_down,
    b_down,
):
    is_first = lax.axis_index("section") == 0
    shards = (
        norm1_gain,
        norm1_shift,
        w_qkv,
        w_out,
        b_out,
        norm2_gain,
        norm2_shift,
        w_up,
        b_up,
        w_down,
        b_down,
    )
    gathered = (
        lax.all_gather(shards[0], "dp", axis=1, tiled=True),
        lax.all_gather(shards[1], "dp", axis=1, tiled=True),
        lax.all_gather(shards[2], "dp", axis=1, tiled=True),
        lax.all_gather(shards[3], "dp", axis=1, tiled=True),
        lax.all_gather(shards[4], "dp", axis=1, tiled=True),
        lax.all_gather(shards[5], "dp", axis=1, tiled=True),
        lax.all_gather(shards[6], "dp", axis=1, tiled=True),
        lax.all_gather(shards[7], "dp", axis=1, tiled=True),
        lax.all_gather(shards[8], "dp", axis=1, tiled=True),
        lax.all_gather(shards[9], "dp", axis=1, tiled=True),
        lax.all_gather(shards[10], "dp", axis=1, tiled=True),
    )
    weights = tuple((item[0] for item in gathered))
    micro_count = block_input.shape[0]

    def pick(upper, lower):
        return jax.tree.map(
            lambda later, earlier: jnp.where(is_first, earlier, later), upper, lower
        )

    incoming = jnp.zeros(block_input.shape[1:], jnp.bfloat16)
    records = []
    kept_saved = []
    forward_rows = []
    for step_index in range(micro_count + 1):
        own_rows = block_input[min(step_index, micro_count - 1)]
        source = jnp.where(is_first, own_rows, incoming)
        crop_rows = jnp.where(
            is_first, crop_ids[min(step_index, micro_count - 1)], crop_ids[max(step_index - 1, 0)]
        )
        saved = forward_layer(source.astype(jnp.float32), crop_rows, weights)
        sent_rows = saved[-1].astype(jnp.bfloat16)
        forward_rows.append(sent_rows)
        records.append((source, crop_rows))
        kept_saved.append(saved)
        if step_index < micro_count:
            incoming = passed_along(sent_rows, "section", 1)
    layer_outputs = jnp.where(
        is_first, jnp.stack(forward_rows[:micro_count]), jnp.stack(forward_rows[1:])
    )
    totals = jax.tree.map(lambda item: jnp.zeros(item.shape, jnp.float32), weights)
    back_in = jnp.zeros(block_input.shape[1:], jnp.bfloat16)
    backward_rows = []
    for step_index in range(micro_count + 1):
        late_tick = min(step_index + 1, micro_count)
        early_tick = max(step_index - 1, 0)
        source, crop_rows = pick(records[late_tick], records[early_tick])
        saved = pick(kept_saved[late_tick], kept_saved[early_tick])
        if step_index < micro_count:
            last_grad = out_grad[step_index]
        else:
            last_grad = jnp.zeros_like(out_grad[0])
        cotangent = jnp.where(is_first, back_in, last_grad)
        grad_hidden, feed_grads = backward_feed(cotangent.astype(jnp.float32), saved, weights)
        feed_totals = tuple((left + right for left, right in zip(totals[5:], feed_grads)))
        grad_in, attend_grads = backward_attend(grad_hidden, saved, crop_rows, weights)
        attend_totals = tuple((left + right for left, right in zip(totals[:5], attend_grads)))
        totals = attend_totals + feed_totals
        sent_grad = grad_in.astype(jnp.bfloat16)
        backward_rows.append(sent_grad)
        if step_index < micro_count:
            back_in = passed_along(sent_grad, "section", -1)
    input_grads = jnp.where(
        is_first, jnp.stack(backward_rows[1:]), jnp.stack(backward_rows[:micro_count])
    )
    summed = lax.psum_scatter(totals, "dp", scatter_dimension=0, tiled=True)
    outputs = tuple((item[None] for item in summed))
    return (layer_outputs[None], input_grads[None]) + outputs


MESH = pl.DeviceIdType.MESH
F = jnp.float32
B = jnp.bfloat16
VECTORS = ("g1", "s1", "bo", "g2", "s2", "bd", "bu")
PARTS = (
    (4, 0, 16, False, False),
    (0, 0, 32, False, False), (0, 32, 32, False, False),
    (1, 0, 64, True, False),
    (2, 0, 32, False, True), (2, 32, 32, True, False),
    (3, 0, 64, False, False), (3, 64, 64, True, False), (3, 128, 64, False, False), (3, 192, 64, True, False),
)
AHEAD = 4
SUMS = (
    (3, 0, 64, True, False),
    (3, 64, 64, False, False),
    (3, 128, 64, True, False),
    (3, 192, 64, False, False),
    (2, 0, 16, True, False),
    (2, 16, 16, False, False),
    (2, 32, 16, True, False),
    (2, 48, 16, False, False),
    (1, 0, 64, False, False),
    (0, 0, 32, True, False),
    (0, 32, 32, False, False),
    (4, 0, 16, False, False),
)
A, O, C, G, DM, DU, DB, DQKV = range(8)


def nt(left, right):
    return lax.dot_general(left, right, (((1,), (1,)), ((), ())), preferred_element_type=F)


def tn(left, right):
    return lax.dot_general(left, right, (((0,), (0,)), ((), ())), preferred_element_type=F)


def nn(left, right):
    return jnp.dot(left, right, preferred_element_type=F)


def tiles(total, step):
    def run(body):
        @pl.loop(0, total // step)
        def _(i):
            body(pl.ds(pl.multiple_of(i * step, step), step))

    return run


def normed(values):
    centred = values - jnp.mean(values, axis=-1, keepdims=True)
    scale = lax.rsqrt(jnp.mean(centred * centred, axis=-1, keepdims=True) + 1e-6)
    return centred * scale, scale


def norm_into(out, rows, gain, shift):
    @tiles(rows.shape[0], 64)
    def _(r):
        hat, _ = normed(rows[r, :].astype(F))
        out[r, :] = (hat * gain[...] + shift[...]).astype(B)


def norm_back(rows, grad, base, out, gain, gain_sum, shift_sum):
    @tiles(rows.shape[0], 64)
    def _(r):
        hat, scale = normed(rows[r, :].astype(F))
        d = grad[r, :]
        gain_sum[...] += jnp.sum(d * hat, axis=0, keepdims=True)
        shift_sum[...] += jnp.sum(d, axis=0, keepdims=True)
        d = d * gain[...]
        mean = jnp.mean(d, axis=-1, keepdims=True)
        along = jnp.mean(d * hat, axis=-1, keepdims=True)
        out[r, :] = (base[r, :].astype(F) + scale * (d - mean - hat * along)).astype(out.dtype)


def halves(pair):
    low = lax.broadcasted_iota(jnp.int32, pair.shape, 1) < HEAD
    zero = jnp.zeros_like(pair)
    return jnp.where(low, pair, zero), jnp.where(low, zero, pair)


def head_pairs(qkv, group, many):
    width = qkv.shape[1] // 3
    for i in range(many):
        for t in range(qkv.shape[0] // 128):
            cols = [pl.ds(pl.multiple_of(g * width + (group * many + i) * 128, 128), 128) for g in range(3)]
            yield pl.ds(t * 128, 128), cols


def softmaxes(items, bias):
    scores = [nt(qh, k) + bias[r, :] for r, q, k in items for qh in halves(q)]
    peaks = [jnp.max(s, axis=-1, keepdims=True) for s in scores]
    raised = [jnp.exp(s - m) for s, m in zip(scores, peaks)]
    totals = [1.0 / jnp.sum(e, axis=-1, keepdims=True) for e in raised]
    return [e * t for e, t in zip(raised, totals)]


def attend(qkv, mixed, bias):
    many = 1024 // qkv.shape[0]

    @pl.loop(0, qkv.shape[1] // 384 // many)
    def _(group):
        where = list(head_pairs(qkv, group, many))
        q, k, v = ([qkv[r, cols[g]] for r, cols in where] for g in range(3))
        q = [item * jnp.asarray(HEAD**-0.5, B) for item in q]
        probs = [p.astype(B) for p in softmaxes([(r, a, b) for (r, _), a, b in zip(where, q, k)], bias)]
        for n, (r, cols) in enumerate(where):
            low, high = halves(v[n])
            mixed[r, cols[0]] = (nn(probs[2 * n], low) + nn(probs[2 * n + 1], high)).astype(B)


def attend_back(qkv, grad, bias):
    many = 1024 // qkv.shape[0]

    def joined(items, axis):
        return jnp.concatenate(items, axis)

    @pl.loop(0, qkv.shape[1] // 384 // many)
    def _(group):
        where = list(head_pairs(qkv, group, many))
        q, k, v = ([qkv[r, cols[g]] for r, cols in where] for g in range(3))
        q = [item * jnp.asarray(HEAD**-0.5, B) for item in q]
        d = [grad[r, cols[0]] for r, cols in where]
        probs = softmaxes([(r, a, b) for (r, _), a, b in zip(where, q, k)], bias)
        slopes = [nt(dh, v[n]) for n in range(len(where)) for dh in halves(d[n])]
        centres = [jnp.sum(g * p, axis=-1, keepdims=True) for g, p in zip(slopes, probs)]
        slopes = [(p * (g - c)).astype(B) for p, g, c in zip(probs, slopes, centres)]
        probs = [p.astype(B) for p in probs]
        for n, (r, cols) in enumerate(where):
            pair = slice(2 * n, 2 * n + 2)
            grad_q = nn(joined(slopes[pair], 1), joined(halves(k[n]), 0))
            qkv[r, cols[0]] = (grad_q * HEAD**-0.5).astype(B)
            qkv[r, cols[1]] = tn(joined(slopes[pair], 0), joined(halves(q[n]), 0)).astype(B)
            qkv[r, cols[2]] = tn(joined(probs[pair], 0), joined(halves(d[n]), 0)).astype(B)


def relay(names, *refs):
    ref = dict(zip(names, refs))
    width = ref["x_own"].shape[1]
    rows = ref["x_own"].shape[0]
    ff = ref["w2"].shape[1]
    shard = [ref[f"own{j}"] for j in range(5)]
    full = [ref[f"w{j}"] for j in range(5)]
    both = [ref[n] for n in ("a", "o", "c", "g", "dm", "du", "db", "dqkv")]
    mine = [b.at[pl.ds(0, 2 * rows)] for b in both]
    theirs = [b.at[pl.ds(2 * rows, 2 * rows)] for b in both]
    vec = {n: ref["v_" + n] for n in VECTORS}
    vsum = {n: ref["d_" + n] for n in VECTORS}
    x, hidden, wide, dmixed, result = (ref[n] for n in ("x", "h", "wide", "do", "y"))
    for name in ("g1", "s1", "g2", "s2"):
        vsum[name][...] = jnp.zeros_like(vsum[name])
    p = lax.axis_index("dp")
    z, y, core = p // 4, (p // 2) % 2, p % 2
    inner = jnp.logical_or(z == 1, z == 2)
    section = lax.axis_index("section")
    zo, zn = jnp.where(z == 1, 0, 3), 3 - z
    zon = 3 - zo
    zi = jnp.where(z == 0, 1, 2)

    def idx(z, y, core):
        return (z * 2 + y) * 2 + core

    sibling, across, other = idx(z, y, 1 - core), idx(z, 1 - y, core), idx(zn, y, core)
    outer_one, inner_one = idx(zo, y, core), idx(zi, y, core)

    def remote(sec, src, dst, send_sem, recv_sem, to):
        return pltpu.make_async_remote_copy(
            src_ref=src, dst_ref=dst, send_sem=send_sem, recv_sem=recv_sem,
            device_id=(sec, to), device_id_type=MESH,
        )

    first = section == 0

    def only(condition):
        return lambda body: pl.when(condition)(body)

    class Flow:
        def __init__(self):
            self.sent = []

        def send(self, src, dst, made, recv_sem, to, sec=section):
            remote(sec, src, dst, made()[1], recv_sem, to).start()
            self.note(made)

        def note(self, made, condition=None):
            self.sent.append((made, condition))

        def arrived(self, dst, recv_sem):
            remote(section, dst, dst, ref["idle_sem"].at[0], recv_sem, sibling).wait_recv()

        def finish(self):
            for made, condition in self.sent:
                def wait():
                    like, send_sem = made()
                    remote(section, like, like, send_sem, ref["idle_sem"].at[0], sibling).wait_send()

                wait() if condition is None else pl.when(condition)(wait)
            self.sent = []

    def piece(k, b):
        j, first, count = PARTS[k][:3]
        size = shard[j].shape[0]
        return full[j].at[pl.ds(pl.multiple_of(b * size + first, count), count)]

    def own_piece(k):
        j, first, count = PARTS[k][:3]
        return shard[j].at[pl.ds(first, count)]

    def own_copy(k):
        return pltpu.make_async_copy(own_piece(k), piece(k, p), ref["ag_local"].at[k])

    def gather_steps(flow, is_inner):
        used = [0] * len(PARTS)

        def send(k, b, to, own=False):
            src = own_piece(k) if own else piece(k, b)
            n = used[k]

            def made():
                return full[PARTS[k][0]].at[pl.ds(0, PARTS[k][2])], ref["ag_send"].at[k, n]

            flow.send(src, piece(k, b), made, ref["ag_recv"].at[k, b], to)
            used[k] += 1

        def take(k, b, *to):
            flow.arrived(piece(k, b), ref["ag_recv"].at[k, b])
            for target in to:
                send(k, b, target)

        def begin(k):
            if is_inner:
                for to in (outer_one if PARTS[k][4] else across, other, sibling):
                    send(k, p, to, own=True)
                own_copy(k).start()
            else:
                send(k, p, inner_one, own=True)
                send(k, p, across, own=True)

        def early(k):
            take(k, idx(zo, y, core), other, sibling)
            take(k, idx(zn, y, core), across, sibling)
            if not PARTS[k][4]:
                take(k, idx(z, 1 - y, core), sibling)

        def late(k):
            by_z = PARTS[k][3]
            take(k, idx(zon, y, core), *((sibling,) if by_z else (across, sibling)))
            take(k, idx(zo, 1 - y, core), *((other, sibling) if by_z else (sibling,)))

        def end(k):
            if PARTS[k][4]:
                take(k, idx(z, 1 - y, core), sibling)
            take(k, idx(zn, 1 - y, core), sibling)
            take(k, idx(zon, 1 - y, core), sibling)

        def step(k):
            if k == 0:
                for first in range(AHEAD):
                    begin(first)
            if k + AHEAD < len(PARTS):
                begin(k + AHEAD)
            if is_inner:
                for stage, n in ((early, k), (late, k - 1), (end, k - 2)):
                    if 0 <= n < len(PARTS):
                        stage(n)
            else:
                take(k, across, inner_one)
                if PARTS[k][4]:
                    take(k, idx(zi, y, core), across)
                if k and PARTS[k - 1][4]:
                    take(k - 1, idx(zi, 1 - y, core), inner_one)

        return step

    def gathered(flow, j):
        for k, part in enumerate(PARTS):
            if part[0] == j:
                own_copy(k).wait()
                for b in range(8):
                    block = 2 * b + 1 - core
                    flow.arrived(piece(k, block), ref["ag_recv"].at[k, block])

    def write_small():
        stage = ref["stage"]
        stage[...] = jnp.zeros_like(stage)
        for c in range(2):
            @pl.when(core == c)
            def _():
                for n, name in enumerate(VECTORS[:6]):
                    stage[n : n + 1, 64 * c : 64 * c + 64] = ref["in_" + name][...].astype(F)
        for n in range(2):
            stage[6 + n : 7 + n, :] = ref["in_bu"][:, 128 * n : 128 * n + 128].astype(F)
        shard[4][...] = stage[...].astype(B)

    def write_crops():
        for m in range(2):
            ref["crops"][0:1, 64 * m : 64 * m + 64] = (ref["in_crop"][m : m + 1, :] + 1024 * m).astype(F)

    def write_bias(crops, first):
        along = jnp.broadcast_to(crops[0:1, :], (rows, rows))
        ref["bias"][pl.ds(first, rows), :] = jnp.where(along == along.T, 0.0, -1e30)

    def spread_vectors():
        for i in range(8):
            low = full[4][pl.ds(32 * i, 16), :].astype(F)
            high = full[4][pl.ds(32 * i + 16, 16), :].astype(F)
            joined = low + high
            for n, name in enumerate(VECTORS[:6]):
                vec[name][:, pl.ds(128 * i, 128)] = joined[n : n + 1]
            for n, part in enumerate((low[6:7], low[7:8], high[6:7], high[7:8])):
                vec["bu"][:, pl.ds(512 * i + 128 * n, 128)] = part

    def exchange(flow, which):
        pair = ref["act_send"].at[which], ref["act_recv"].at[which]
        remote(section, mine[which], theirs[which], *pair, sibling).start()

    def exchanged(flow, *which):
        for w in which:
            flow.arrived(theirs[w], ref["act_recv"].at[w])

    def forward_attend(r):
        norm_into(mine[A].at[r], x.at[r], vec["g1"], vec["s1"])

        @tiles(3 * width, 1536)
        def _(c):
            mine[DQKV][r, c] = nn(mine[A][r, :], full[0][:, c]).astype(B)

        attend(mine[DQKV].at[r], mine[O].at[r], ref["bias"].at[r])

    def forward_out(r):
        hidden[r, :] = x[r, :].astype(F) + nn(mine[O][r, :], full[1][...]) + vec["bo"][...]
        norm_into(mine[C].at[r], hidden.at[r], vec["g2"], vec["s2"])

    def forward_up(r):
        @tiles(ff, 1024)
        def _(c):
            u = nn(mine[C][r, :], full[2][:, c]) + vec["bu"][:, c]
            phi = 0.5 + 0.5 * lax.erf(u * 0.5**0.5)
            mine[G][r, c] = (u * phi).astype(B)
            mine[DU][r, c] = (phi + u * (jnp.exp(-0.5 * u * u) * (0.5 / jnp.pi) ** 0.5)).astype(B)

    def forward_down(r):
        result[r, :] = (hidden[r, :] + nn(mine[G][r, :], full[3][...]) + vec["bd"][...]).astype(B)

    def backward_du():
        vsum["bd"][...] = jnp.sum(mine[DM][...].astype(F), axis=0, keepdims=True)

        @tiles(ff, 1024)
        def _(c):
            du = (nt(mine[DM][...], full[3][c, :]) * mine[DU][:, c].astype(F)).astype(B)
            mine[DU][:, c] = du
            vsum["bu"][:, c] = jnp.sum(du.astype(F), axis=0, keepdims=True)

    def backward_dh():
        wide[...] = nt(mine[DU][...], full[2][...])
        norm_back(hidden, wide, mine[DM], hidden, vec["g2"], vsum["g2"], vsum["s2"])
        mine[DB][...] = hidden[...].astype(B)
        vsum["bo"][...] = jnp.sum(mine[DB][...].astype(F), axis=0, keepdims=True)

    def backward_attend():
        dmixed[...] = nt(mine[DB][...], full[1][...]).astype(B)
        attend_back(mine[DQKV], dmixed, ref["bias"])

    def backward_da():
        wide[...] = nt(mine[DQKV][...], full[0][...])

    def backward_dx(r):
        norm_back(x.at[r], wide.at[r], hidden.at[r], x.at[r], vec["g1"], vsum["g1"], vsum["s1"])

    def packed(which):
        src, out = both[which], ref["packed"]
        for i in range(width // 256):
            first = src[:, pl.ds(256 * i, 128)].astype(F)
            second = src[:, pl.ds(256 * i + 128, 128)].astype(F)
            low = lax.broadcasted_iota(jnp.int32, first.shape, 1) < HEAD
            even = jnp.where(low, first, pltpu.roll(second, HEAD, 1))
            odd = jnp.where(low, pltpu.roll(first, HEAD, 1), second)
            out[pl.ds(128 * i, 128), :] = jnp.where(core == 0, even, odd).T.astype(B)

    def grad_down():
        size = shard[3].shape[0]
        for o in range(8):
            c = pl.ds(pl.multiple_of(size * (2 * o + core), size), size)
            full[3][pl.ds(size * o, size), :] = tn(both[G][:, c], both[DM][...]).astype(B)

    def grad_of(j, left, right):
        packed(left)

        @tiles(both[right].shape[1], 512)
        def _(c):
            full[j][pl.ds(0, 8 * shard[j].shape[0]), c] = nn(ref["packed"][...], both[right][:, c]).astype(B)

    def grad_vectors():
        for o in range(8):
            for n, name in enumerate(VECTORS[:6]):
                ref["vp"][pl.ds(16 * o + n, 1), :] = vsum[name][:, pl.ds(128 * o, 128)]
            for n in range(4):
                ref["vp"][pl.ds(16 * o + 6 + n, 1), :] = vsum["bu"][:, pl.ds(512 * o + 128 * n, 128)]
            ref["vp"][pl.ds(16 * o + 10, 6), :] = jnp.zeros((6, 128), F)

    partial = [full[0], full[1], full[2], full[3], ref["vp"]]
    sums = [ref[f"out{j}"] for j in range(4)] + [ref["vs"]]
    NEAR, OWN, ALT, INNER, OUTER = range(5)
    slots = [[ref[f"r{s}_{j}"] for j in range(5)] for s in range(5)]

    def reducer(flow):
        def slot(s, k):
            j, first, count = SUMS[k][:3]
            return slots[s][j].at[pl.ds(first, count)]

        def part(k, zz, yy):
            j, first, count = SUMS[k][:3]
            size = partial[j].shape[0] // 8 if j == 4 else shard[j].shape[0]
            return partial[j].at[pl.ds(pl.multiple_of((zz * 2 + yy) * size + first, count), count)]

        def send(k, n, src, s, to):
            def made():
                return slot(s, k), ref["rs_send"].at[k, n]

            flow.send(src, slot(s, k), made, ref["rs_recv"].at[k, s], to)

        def arrived(k, s):
            flow.arrived(slot(s, k), ref["rs_recv"].at[k, s])

        def add(k, dst, *more):
            total = dst[...].astype(F)
            for s in more:
                total = total + slot(s, k)[...].astype(F)
            return total

        def issue(k):
            if SUMS[k][3]:
                send(k, 4, part(k, zon, y), OUTER, other)
                send(k, 1, part(k, zon, 1 - y), ALT, other)
            else:
                send(k, 1, part(k, zon, 1 - y), ALT, across)
                send(k, 6, part(k, zo, 1 - y), INNER, outer_one)

        def issue_near(k):
            send(k, 0, part(k, zn, 1 - y), NEAR, across)

        def issue_own(k):
            if SUMS[k][4]:
                send(k, 2, part(k, z, 1 - y), NEAR, outer_one)
            else:
                send(k, 2, part(k, z, 1 - y), OWN, across)

        def far_on(k):
            if not SUMS[k][3]:
                dst = part(k, zon, y)
                arrived(k, ALT)
                dst[...] = add(k, dst, ALT).astype(dst.dtype)
                send(k, 4, dst, OUTER, other)

        def near_on(k):
            dst = part(k, zn, y)
            arrived(k, NEAR)
            dst[...] = add(k, dst, NEAR).astype(dst.dtype)
            send(k, 3, dst, INNER, other)

        def outward(k):
            dst = part(k, zo, y)
            arrived(k, OUTER)
            dst[...] = add(k, dst, OUTER).astype(dst.dtype)
            send(k, 5, dst, OUTER, outer_one)
            if SUMS[k][3]:
                dst = part(k, zo, 1 - y)
                arrived(k, ALT)
                dst[...] = add(k, dst, ALT).astype(dst.dtype)
                send(k, 6, dst, INNER, outer_one)

        def last(k):
            arrived(k, INNER)
            arrived(k, OWN)
            j, first, count = SUMS[k][:3]
            sums[j][pl.ds(first, count), :] = add(k, part(k, z, y), OWN, INNER)

        def pass_on(k):
            arrived(k, INNER)
            send(k, 0, slot(INNER, k), OWN, across)

        def around(k, end):
            arrived(k, ALT if end else NEAR)
            if end:
                send(k, 2, slot(ALT, k), OWN, inner_one)
            else:
                send(k, 1, slot(NEAR, k), ALT, across)

        def collect(k):
            arrived(k, OUTER)
            arrived(k, OWN)
            j, first, count = SUMS[k][:3]
            sums[j][pl.ds(first, count), :] = slot(OUTER, k)[...].astype(F) + slot(OWN, k)[...].astype(F)

        def join_vectors():
            made = lambda: (ref["vs"], ref["vec_sem"].at[0])
            flow.send(ref["vs"], ref["vt"], made, ref["vec_sem"].at[1], sibling)
            flow.arrived(ref["vt"], ref["vec_sem"].at[1])
            ref["out4"][...] = ref["vs"][...] + ref["vt"][...]

        inner_steps = issue, issue_near, issue_own, far_on, near_on, outward, last
        return inner_steps, (pass_on, around, collect), join_vectors

    def hand_out(flow, src, out, n):
        made = lambda: (out, ref["res_send"].at[n])
        flow.send(src.at[pl.ds(rows, rows)], out, made, ref["res_recv"].at[n], outer_one)
        out[...] = src[pl.ds(0, rows), :]

    every = pl.ds(0, 2 * rows)
    near, far = pl.ds(0, rows), pl.ds(rows, rows)

    def half(h):
        return pl.ds(pl.multiple_of(h * rows, rows), rows)

    direct = pl.ds(rows, rows // 2)
    detours = [pl.ds(rows + rows // 4 * n, rows // 4) for n in (2, 3)]

    def cross_far(src, dst, sec, kind, between=lambda: None):
        for n, r in enumerate(detours):
            pair = ref["way_send"].at[kind + n], ref["way_recv"].at[kind + n]
            remote(section, src.at[r], dst.at[r], *pair, outer_one).start()
        between()
        pair = ref["x_send"].at[kind + 1], ref["x_recv"].at[kind + 1]
        remote(sec, src.at[direct], dst.at[direct], *pair, p).start()

    def crossed_far(flow, dst, kind):
        flow.arrived(dst.at[direct], ref["x_recv"].at[kind + 1])
        for n, r in enumerate(detours):
            flow.arrived(dst.at[r], ref["way_recv"].at[kind + n])

    def note_crossing(flow, kind, condition):
        flow.note(lambda: (x.at[near], ref["x_send"].at[kind]), condition)
        flow.note(lambda: (x.at[direct], ref["x_send"].at[kind + 1]), condition)
        for n in range(2):
            flow.note(lambda n=n: (x.at[detours[0]], ref["way_send"].at[kind + n]), condition)

    def detour(flow, dst, sec, kind):
        for n, r in enumerate(detours):
            pair = ref["way_send"].at[kind + n], ref["way_recv"].at[kind + n]
            flow.arrived(dst.at[r], pair[1])
            pl.when(section != sec)(remote(sec, dst.at[r], dst.at[r], *pair, p).start)
            pl.when(section == sec)(remote(sec, dst.at[r], dst.at[r], *pair, inner_one).start)
            flow.note(lambda n=n: (x.at[detours[0]], ref["way_send"].at[kind + n]))

    def inner_program():
        flow = Flow()
        step = gather_steps(flow, True)
        inner_steps, _, join_vectors = reducer(flow)
        issue, issue_near, issue_own, far_on, near_on, outward, last = inner_steps
        step(0)
        own = [
            pltpu.make_async_copy(src, dst.at[near], ref["tok_local"].at[0])
            for src, dst in ((ref["x_own"], x), (ref["dy_own"], mine[DM]))
        ]
        for n, copy in enumerate(own):
            pl.when(section == n)(copy.start)
        write_bias(ref["crops"], 0)

        def tokens():
            for n, (copy, dst) in enumerate(zip(own, (x, mine[DM]))):
                @pl.when(section == n)
                def _():
                    copy.wait()
                    flow.arrived(dst.at[far], ref["tok_recv"].at[1])
            flow.arrived(ref["far_crops"], ref["tok_recv"].at[0])
            write_bias(ref["far_crops"], rows)

        def steps(begin, end):
            for k in range(begin, end):
                step(k)

        @pl.loop(0, 2)
        def _(turn):
            gathering, active = only(turn == 0), only(section == turn)

            @gathering
            def _():
                steps(1, 6)
                gathered(flow, 4)
                spread_vectors()
                tokens()
                gathered(flow, 0)

            @active
            def _():
                @pl.loop(0, 2)
                def _(h):
                    @pl.when(jnp.logical_and(h == 0, section == 1))
                    def _():
                        flow.arrived(x.at[near], ref["x_recv"].at[0])

                    @pl.when(jnp.logical_and(h == 1, section == 1))
                    def _():
                        crossed_far(flow, x, 0)

                    forward_attend(half(h))

            @gathering
            def _():
                steps(6, 7)
                gathered(flow, 1)

            @active
            def _():
                forward_out(every)

            @gathering
            def _():
                steps(7, 9)
                gathered(flow, 2)

            @active
            def _():
                forward_up(every)

            @gathering
            def _():
                steps(9, len(PARTS) + 2)
                gathered(flow, 3)

            @active
            def _():
                forward_down(every)

        @pl.when(first)
        def _():
            cross_far(
                result, x, 1, 0,
                remote(1, result.at[near], x.at[near], ref["x_send"].at[0], ref["x_recv"].at[0], p).start,
            )

        note_crossing(flow, 0, first)
        flow.finish()
        for which in (G, C, O, A):
            exchange(flow, which)
        hand_out(flow, result, ref["y_out"], 0)

        def exchange_when(condition, *which):
            @pl.when(condition)
            def _():
                for w in which:
                    exchange(flow, w)

        @pl.loop(0, 2)
        def _(turn):
            main, grads = only(turn == 0), only(section == turn)
            leading = jnp.logical_and(turn == 0, first)
            trailing = jnp.logical_and(turn == 1, section == 1)

            @pl.when(leading)
            def _():
                flow.arrived(mine[DM].at[near], ref["x_recv"].at[2])
                crossed_far(flow, mine[DM], 2)

            exchange_when(turn == 0, DM)
            main(backward_du)
            exchange_when(leading, DU)
            exchange_when(trailing, DU, DB, DQKV)

            @grads
            def _():
                exchanged(flow, G, DM)
                grad_down()
                issue(0)
                issue_near(0)
                issue(1)
                issue_near(1)
                issue(2)
                issue(3)

            main(backward_dh)
            exchange_when(leading, DB)

            @grads
            def _():
                issue_near(2)
                exchanged(flow, C, DU)
                grad_of(2, C, DU)

            main(backward_attend)
            exchange_when(leading, DQKV)

            @grads
            def _():
                for k in range(4, 8):
                    issue(k)
                issue_near(3)
                exchanged(flow, O, DB)
                grad_of(1, O, DB)
                issue(8)

            main(backward_da)

            @grads
            def _():
                far_on(1)
                near_on(0)
                exchanged(flow, A, DQKV)
                grad_of(0, A, DQKV)
                issue(9)
                issue(10)
                issue_near(4)

            @main
            def _():
                @pl.loop(0, 2)
                def _(h):
                    backward_dx(half(1 - h))

                    @pl.when(jnp.logical_and(h == 0, section == 1))
                    def _():
                        cross_far(x, mine[DM], 0, 2)

                    @pl.when(jnp.logical_and(h == 1, section == 1))
                    def _():
                        to = mine[DM].at[near]
                        remote(0, x.at[near], to, ref["x_send"].at[2], ref["x_recv"].at[2], p).start()

        note_crossing(flow, 2, section == 1)
        for which in range(8):
            flow.note(lambda w=which: (mine[w], ref["act_send"].at[w]))
        grad_vectors()
        issue(11)
        hand_out(flow, x, ref["dx_out"], 1)
        count = len(SUMS)
        for k in range(2, count + 4):
            plan = ((far_on, [2 * k - 2, 2 * k - 1]), (issue_near, [k + 3]), (near_on, [k - 1]), (outward, [k - 3] if k < 8 else [2 * k - 11, 2 * k - 10]), (issue_own, [k - 4]))
            for turn, which in plan:
                for n in which:
                    if 0 <= n < count:
                        turn(n)
        for k in range(count):
            last(k)
        join_vectors()
        flow.finish()

    def outer_program():
        flow = Flow()
        step = gather_steps(flow, False)
        _, (pass_on, around, collect), join_vectors = reducer(flow)
        for k in range(len(PARTS)):
            step(k)
            if k == 1:
                made = lambda: (ref["crops"], ref["tok_send"].at[0])
                flow.send(ref["crops"], ref["far_crops"], made, ref["tok_recv"].at[0], inner_one)
                for n, (src, dst) in enumerate(((ref["x_own"], x), (ref["dy_own"], mine[DM]))):
                    pl.when(section == n)(
                        remote(section, src, dst.at[far], ref["tok_send"].at[1], ref["tok_recv"].at[1], inner_one).start
                    )
                flow.note(lambda: (x.at[far], ref["tok_send"].at[1]))
        detour(flow, x, 1, 0)
        detour(flow, mine[DM], 0, 2)
        for k in range(len(SUMS)):
            for turn, n in ((pass_on, k), (collect, k - 1)):
                if 0 <= n:
                    turn(n)
            for end in range(2):
                n = k - 3 - end
                if 0 <= n < len(SUMS) and SUMS[n][4]:
                    around(n, end)
        collect(len(SUMS) - 1)
        join_vectors()
        flow.arrived(ref["y_out"], ref["res_recv"].at[0])
        flow.arrived(ref["dx_out"], ref["res_recv"].at[1])
        flow.finish()

    write_small()
    write_crops()
    pl.when(inner)(inner_program)
    pl.when(jnp.logical_not(inner))(outer_program)


def relay_call(x_own, dy_own, small, shards, dp):
    rows, width = x_own.shape
    ff = shards[2].shape[1]
    count = 2 * rows
    shapes = [item.shape for item in shards] + [(16, 128)]
    inputs = {"x_own": x_own, "dy_own": dy_own}
    inputs.update({f"own{j}": item for j, item in enumerate(shards)})
    outputs = {"y_out": ((rows, width), B), "dx_out": ((rows, width), B)}
    outputs.update({f"out{j}": (item.shape, F) for j, item in enumerate(shards)})
    outputs["out4"] = ((16, 128), F)
    scratch = {f"w{j}": ((dp * shape[0], shape[1]), B) for j, shape in enumerate(shapes)}
    for name, cols in zip(("a", "o", "c", "g", "dm", "du", "db", "dqkv"), (1, 1, 1, 0, 1, 0, 1, 3)):
        scratch[name] = ((2 * count, cols * width or ff), B)
    scratch.update(x=((count, width), B), h=((count, width), F), wide=((count, width), F), do=((count, width), B))
    scratch.update(y=((count, width), B), bias=((count, 128), F), packed=((width // 2, 2 * count), B))
    for name in VECTORS:
        scratch["v_" + name] = scratch["d_" + name] = ((1, ff if name == "bu" else width), F)
    scratch.update(vp=((128, 128), F), vs=((16, 128), F), vt=((16, 128), F), stage=((16, 128), F), crops=((8, 128), F), far_crops=((8, 128), F), own4=((16, 128), B))
    for s in range(5):
        for j, shape in enumerate(shapes):
            scratch[f"r{s}_{j}"] = (shape, F if j == 4 else B)
    sems = dict(
        ag_send=(len(PARTS), 16), ag_recv=(len(PARTS), dp), ag_local=(len(PARTS),), tok_local=(1,), tok_send=(2,),
        tok_recv=(2,), x_send=(4,), x_recv=(4,), way_send=(4,), way_recv=(4,), act_send=(8,), act_recv=(8,), res_send=(2,), res_recv=(2,),
        rs_send=(len(SUMS), 7), rs_recv=(len(SUMS), 5), vec_sem=(2,), idle_sem=(1,),
    )
    names = [*inputs, *small, *outputs, *scratch, *sems]
    whole, anywhere = pl.BlockSpec(memory_space=pltpu.VMEM), pl.BlockSpec(memory_space=pl.ANY)
    return pl.pallas_call(
        functools.partial(relay, names),
        out_shape=[jax.ShapeDtypeStruct(*item) for item in outputs.values()],
        in_specs=[anywhere] * len(inputs) + [whole] * len(small),
        out_specs=[whole] * len(outputs),
        scratch_shapes=[pltpu.VMEM(*item) for item in scratch.values()]
        + [pltpu.SemaphoreType.DMA(item) for item in sems.values()],
        compiler_params=pltpu.CompilerParams(has_side_effects=True, vmem_limit_bytes=62 << 20),
        name="relay",
    )(*inputs.values(), *small.values())


def hand_over(*refs):
    rows, vectors, out, small = refs[:6], refs[6], refs[7:13], refs[13:20]
    for n in range(2):
        size = out[n].shape[2]
        for m in range(out[n].shape[1]):
            out[n][0, m] = rows[n][pl.ds(m * size, size), :]
    for n in range(2, 6):
        out[n][0] = rows[n][...]
    core = lax.axis_index("dp") % 2
    for c in range(2):
        @pl.when(core == c)
        def _():
            for n in range(6):
                small[n][...] = vectors[n : n + 1, 64 * c : 64 * c + 64]
            small[6][...] = vectors[6 + 2 * c : 8 + 2 * c, :]


def middle(
    block_input, crop_ids, out_grad, norm1_gain, norm1_shift, w_qkv, w_out, b_out,
    norm2_gain, norm2_shift, w_up, b_up, w_down, b_down,
):
    micro, rows, width = block_input.shape
    small = dict(zip(VECTORS, (norm1_gain, norm1_shift, b_out, norm2_gain, norm2_shift, b_down, b_up)))
    small = {"in_" + name: item for name, item in small.items()} | {"in_crop": crop_ids}
    got = relay_call(
        block_input.reshape(-1, width), out_grad.reshape(-1, width), small,
        (w_qkv[0], w_out[0], w_up[0], w_down[0]), lax.axis_size("dp"),
    )
    whole = pl.BlockSpec(memory_space=pltpu.VMEM)
    shapes = [((1, micro, rows, width), B)] * 2 + [((1,) + item.shape, F) for item in got[2:6]]
    shapes += [((1, 64), F)] * 6 + [((2, 128), F)]
    y, dx, g_qkv, g_out, g_up, g_down, g1, s1, bo, g2, s2, bd, bu = pl.pallas_call(
        hand_over,
        out_shape=[jax.ShapeDtypeStruct(*item) for item in shapes],
        in_specs=[whole] * 7,
        out_specs=[whole] * 13,
        compiler_params=pltpu.CompilerParams(vmem_limit_bytes=62 << 20),
        name="hand_over",
    )(*got)
    return y, dx, g1, s1, g_qkv, g_out, bo, g2, s2, g_up, bu.reshape(1, -1), g_down, bd


def solution(mesh):
    in_specs = (
        P(None, "dp", None),
        P(None, "dp"),
        P(None, "dp", None),
        P("section", "dp"),
        P("section", "dp"),
        P("section", "dp", None),
        P("section", "dp", None),
        P("section", "dp"),
        P("section", "dp"),
        P("section", "dp"),
        P("section", "dp", None),
        P("section", "dp"),
        P("section", "dp", None),
        P("section", "dp"),
    )
    out_specs = (
        P("section", None, "dp", None),
        P("section", None, "dp", None),
        P("section", "dp"),
        P("section", "dp"),
        P("section", "dp", None),
        P("section", "dp", None),
        P("section", "dp"),
        P("section", "dp"),
        P("section", "dp"),
        P("section", "dp", None),
        P("section", "dp"),
        P("section", "dp", None),
        P("section", "dp"),
    )
    fits = mesh.shape["dp"] == 16 and mesh.shape["section"] == 2
    return jax.shard_map(middle if fits else local, mesh=mesh, in_specs=in_specs, out_specs=out_specs, check_vma=False)
```
